32 devices in a mesh: dp: 8 (over z, x), vocab: 4 (over y, core).
Axes of the slice: x: 2, y: 2, z: 4, core: 2. Of those that a mesh axis runs over, the one named last changes fastest.
Arguments:
- input_token_ids: int32 [2, 32, 512], P(None, ('dp', 'vocab')), may hold values from 0 to 50303
- lengths: int32 [2, 32], P(None, ('dp', 'vocab')), may hold values from 2 to 512, as said below
- masked_positions: int32 [2, 32, 76], P(None, ('dp', 'vocab')), may hold values from 1 to 511, as said below
- masked_token_targets: int32 [2, 32, 76], P(None, ('dp', 'vocab')), may hold values from 0 to 50303
- labels: int32 [2, 32], P(None, ('dp', 'vocab')), may hold values from 0 to 2
- token_embedding_table: bfloat16 [50304, 768], P('vocab'), may hold values from -0.649519 to 0.649519
- position_table: bfloat16 [512, 768], replicated, may hold values from -0.25 to 0.25
- norm_gain_table: float32 [6, 768], replicated, may hold values from 0.5 to 1.5
- query_key_value_weight: bfloat16 [2, 768, 2304], replicated, may hold values from -0.21875 to 0.21875
- output_weight: bfloat16 [2, 768, 768], replicated, may hold values from -0.875 to 0.875
- up_weight: bfloat16 [2, 768, 3072], replicated, may hold values from -0.21875 to 0.21875
- down_weight: bfloat16 [2, 3072, 768], replicated, may hold values from -0.109375 to 0.109375
- adapter_inputs: bfloat16 [2, 768, 40], replicated, may hold values from -0.21875 to 0.21875
- adapter_down_input: bfloat16 [2, 3072, 8], replicated, may hold values from -0.109375 to 0.109375
- head_dense_maps: bfloat16 [2, 768, 768], replicated, may hold values from -0.21875 to 0.21875
- adapter_outputs: float32 [2, 8, 6912], replicated, may hold values from -0.3125 to 0.3125
- class_projection: float32 [769, 3], replicated, may hold values from -0.21875 to 0.21875
- adapter_moment_first: float32 [2, 8, 6912], replicated, may hold values from -4.7683716e-06 to 4.7683716e-06
- adapter_moment_second: float32 [2, 8, 6912], replicated, may hold values from 8.857474e-15 to 3.5429897e-14
- class_moment_first: float32 [769, 3], replicated, may hold values from -4.7683716e-06 to 4.7683716e-06
- class_moment_second: float32 [769, 3], replicated, may hold values from 8.857474e-15 to 3.5429897e-14
Outputs:
- loss_and_terms: float32 [2], replicated
- grad_norm: float32 [1], replicated
- adapter_outputs_next: float32 [2, 8, 6912], replicated
- adapter_moment_first_next: float32 [2, 8, 6912], replicated
- adapter_moment_second_next: float32 [2, 8, 6912], replicated
- class_projection_next: float32 [769, 3], replicated
- class_moment_first_next: float32 [769, 3], replicated
- class_moment_second_next: float32 [769, 3], replicated
The draws below stay inside these ranges and needn't reach their ends.
Inputs may be any that keep to these rules, and one draw needn't show every extreme that they name: `lengths`: some item of each micro-batch has length exactly 512. `masked_positions`: each position lies from 1 to its item's length minus 1; positions may repeat.
All inputs are finite; a program needn't handle non-finite values.
Results may differ from the reference program's by a relative error of at most 0.006.
Values may be sent and summed in bfloat16 or wider, within the bound.
No kernel may reach another device: no remote copies, remote signals or barrier semaphores. Data moves between devices by JAX's collectives and lax.ppermute only.
A program may use at most 320 MiB of HBM per device.

```python
import math
import jax
import jax.numpy as jnp
import numpy as np
from jax import lax

MODEL_DIM = 768
HDIM = 64
FEEDFWD_UNITS = 3072
VOCAB = 50304
ADAPTER_RANK = 8
LABELS = 3
ENCODER_LAYERS = 2
MICRO = 2
ITEM_LEN = 512
STEP = 10
ITEMS = 1
SLOTS = 76
ITEMS_ALL = 32
GROUP = 4
TRAINED_COUNT = 112899


def length_table(key):
    key = jax.random.fold_in(key, 101)
    index = jnp.arange(ITEMS_ALL, dtype=jnp.int32)
    data_span = max(ITEMS_ALL // GROUP - 1, 1)
    vocab_span = max(GROUP // ITEMS - 1, 1)
    data_place = index // GROUP
    vocab_place = index % GROUP // ITEMS
    base = ITEM_LEN * (5 * data_span + 4 * data_place) * (5 * vocab_span + 4 * vocab_place) // (81 * data_span * vocab_span)
    jitter = jax.random.randint(key, (MICRO, ITEMS_ALL), 0, ITEM_LEN // 8 + 1)
    drawn = jnp.clip(base[None, :] - jitter, 2, ITEM_LEN)
    return jnp.where(index[None, :] == ITEMS_ALL - 1, ITEM_LEN, drawn).astype(jnp.int32)


def draw_lengths(key, part):
    return length_table(key)


def draw_masked_positions(key, part):
    length_matrix = length_table(key)
    key = jax.random.fold_in(key, 7)
    raw = jax.random.randint(key, (MICRO, ITEMS_ALL, SLOTS), 0, 1 << 30)
    return (1 + raw % (length_matrix[..., None] - 1)).astype(jnp.int32)


def draw_token_embedding_table(key, part):
    key = jax.random.fold_in(key, 5)
    row_place = jnp.arange(VOCAB, dtype=jnp.float32)[:, None] / (VOCAB - 1)
    noise = jnp.clip(jax.random.normal(key, (VOCAB, MODEL_DIM), jnp.float32), -6.0, 6.0)
    scale = 1.0 + 2.0 * row_place
    return (noise * scale * MODEL_DIM ** (-0.5)).astype(jnp.bfloat16)


def touch_ends(entries, stream_key, low, high):
    place = [jax.random.randint(jax.random.fold_in(stream_key, axis), (), 0, length) for axis, length in enumerate(entries.shape)]
    widest = entries.shape.index(max(entries.shape))
    next_to = place[:widest] + [(place[widest] + 1) % entries.shape[widest]] + place[widest + 1:]
    return entries.at[tuple(place)].set(low).at[tuple(next_to)].set(high)


def rank_table(count, slope):
    weights = [(1 << 20) // math.isqrt(rank ** slope) + 1 for rank in range(1, count + 1)]
    deviation = 1 + sum(weights) // (1 << 30)
    return np.cumsum(np.array([max(1, weight // deviation) for weight in weights]))


def ranked_ids(key, shape, number_of, slope):
    table = rank_table(number_of, slope)
    pick = jax.random.randint(jax.random.fold_in(key, 1), shape, 0, int(table[number_of - 1]))
    grade = jnp.searchsorted(jnp.asarray(table, jnp.int32), pick, side="right")
    return jax.random.permutation(jax.random.fold_in(key, 2), number_of)[grade].astype(jnp.int32)


def normal_values(stream_key, shape, scale, most, kind=jnp.bfloat16):
    return jnp.clip(scale * jax.random.normal(stream_key, shape, jnp.float32), -most, most).astype(kind)


def setup_inputs(seed: int = 0) -> dict:
    key_of = jax.random.split(jax.random.key(seed), 22)
    return {
        "input_token_ids": touch_ends(ranked_ids(key_of[0], (MICRO, ITEMS_ALL, ITEM_LEN), VOCAB, 2), jax.random.fold_in(key_of[0], 3), 0, VOCAB - 1).astype(jnp.int32),
        "lengths": draw_lengths(jax.random.fold_in(key_of[21], 71), 0),
        "masked_positions": draw_masked_positions(jax.random.fold_in(key_of[21], 71), 0),
        "masked_token_targets": touch_ends(ranked_ids(key_of[3], (MICRO, ITEMS_ALL, SLOTS), VOCAB, 2), jax.random.fold_in(key_of[3], 3), 0, VOCAB - 1).astype(jnp.int32),
        "labels": touch_ends(jax.random.randint(key_of[4], (MICRO, ITEMS_ALL), 0, LABELS), jax.random.fold_in(key_of[4], 1), 0, LABELS - 1).astype(jnp.int32),
        "token_embedding_table": draw_token_embedding_table(jax.random.fold_in(key_of[21], 71), 0),
        "position_table": normal_values(key_of[6], (ITEM_LEN, MODEL_DIM), (0.5 * MODEL_DIM ** -0.5), 0.25),
        "norm_gain_table": jnp.clip(1.0 + 0.1 * jax.random.normal(key_of[7], (2 * ENCODER_LAYERS + 2, MODEL_DIM), jnp.float32), 0.5, 1.5),
        "query_key_value_weight": normal_values(key_of[8], (ENCODER_LAYERS, MODEL_DIM, 3 * MODEL_DIM), MODEL_DIM ** -0.5, 0.21875),
        "output_weight": normal_values(key_of[9], (ENCODER_LAYERS, MODEL_DIM, MODEL_DIM), (MODEL_DIM // 16) ** -0.5, 0.875),
        "up_weight": normal_values(key_of[10], (ENCODER_LAYERS, MODEL_DIM, FEEDFWD_UNITS), MODEL_DIM ** -0.5, 0.21875),
        "down_weight": normal_values(key_of[11], (ENCODER_LAYERS, FEEDFWD_UNITS, MODEL_DIM), FEEDFWD_UNITS ** -0.5, 0.109375),
        "adapter_inputs": normal_values(key_of[12], (ENCODER_LAYERS, MODEL_DIM, 5 * ADAPTER_RANK), MODEL_DIM ** -0.5, 0.21875),
        "adapter_down_input": normal_values(key_of[13], (ENCODER_LAYERS, FEEDFWD_UNITS, ADAPTER_RANK), FEEDFWD_UNITS ** -0.5, 0.109375),
        "head_dense_maps": normal_values(key_of[14], (2, MODEL_DIM, MODEL_DIM), MODEL_DIM ** -0.5, 0.21875),
        "adapter_outputs": normal_values(key_of[15], (ENCODER_LAYERS, ADAPTER_RANK, 5 * MODEL_DIM + FEEDFWD_UNITS), 0.02, 0.3125, jnp.float32),
        "class_projection": normal_values(key_of[16], (MODEL_DIM + 1, LABELS), MODEL_DIM ** -0.5, 0.21875, jnp.float32),
        "adapter_moment_first": normal_values(key_of[17], (ENCODER_LAYERS, ADAPTER_RANK, 5 * MODEL_DIM + FEEDFWD_UNITS), (1.1e-4 * TRAINED_COUNT ** -0.5), 4.76837158203125e-06, jnp.float32),
        "adapter_moment_second": jnp.clip(jnp.exp(jax.random.uniform(key_of[18], (ENCODER_LAYERS, ADAPTER_RANK, 5 * MODEL_DIM + FEEDFWD_UNITS), jnp.float32, math.log(8.857474351415054e-15), math.log(3.5429897405660216e-14))), 8.857474351415054e-15, 3.5429897405660216e-14),
        "class_moment_first": normal_values(key_of[19], (MODEL_DIM + 1, LABELS), (1.1e-4 * TRAINED_COUNT ** -0.5), 4.76837158203125e-06, jnp.float32),
        "class_moment_second": jnp.clip(jnp.exp(jax.random.uniform(key_of[20], (MODEL_DIM + 1, LABELS), jnp.float32, math.log(8.857474351415054e-15), math.log(3.5429897405660216e-14))), 8.857474351415054e-15, 3.5429897405660216e-14),
    }


@jax.custom_vjp
def reduced_rows(v):
    return lax.optimization_barrier(v.astype(jnp.bfloat16)).astype(jnp.float32)

@jax.custom_vjp
def reduced_backward(v):
    return v

def low_keep(v):
    return (reduced_rows(v), None)

def low_pass(kept, grad):
    return (grad,)

def back_keep(v):
    return (v, None)

def back_low(kept, grad):
    return (reduced_rows(grad),)
reduced_rows.defvjp(low_keep, low_pass)
reduced_backward.defvjp(back_keep, back_low)
FULL_PRECISION = lax.Precision.HIGHEST
NORM_EPS = 1e-05
ADAPTER_SCALE = 2.0
NEG_FILL = -1e+30
CLIP_AT = 0.001
RATE = 0.03
BETA_ONE = 0.9
BETA_TWO = 0.999
ADAM_EPS = 1e-08
DECAY = 0.01

def layer_norm(values, gain):
    center = values - lax.optimization_barrier(jnp.mean(values, -1, keepdims=True))
    spread = lax.optimization_barrier(jnp.mean(center * center, -1, keepdims=True))
    return center * lax.rsqrt(spread + NORM_EPS) * gain

def precise_product(left, right):
    return jnp.matmul(left, right, precision=FULL_PRECISION)

def inner_low(rows, a_columns):
    return reduced_backward(reduced_rows(precise_product(rows, a_columns)))

def adapter_change(inner_rows, adapter_out_columns, term_tally):
    row_tally = inner_rows.shape[0]
    rank_size = adapter_out_columns.shape[0]
    output_width = adapter_out_columns.shape[1] // term_tally
    block_list = inner_rows.reshape(row_tally, term_tally, rank_size)
    adapter_out_blocks = adapter_out_columns.reshape(rank_size, term_tally, output_width)
    return ADAPTER_SCALE * jnp.einsum('bhx,xhs->bhs', block_list, adapter_out_blocks, precision=FULL_PRECISION).reshape(row_tally, term_tally * output_width)

def apply_layer(hidden_rows, adapter_out_columns, query_key_value_weight, output_weight, up_weight, down_weight, a_in, a_down, gain_pair, key_valid_mask):
    seq_len, hidden_width = hidden_rows.shape
    head_count = hidden_width // HDIM
    rank_size = a_down.shape[1]
    flattened_input = reduced_rows(hidden_rows)
    inner_attention_rows = inner_low(flattened_input, a_in[:, :3 * rank_size])
    query_key_value = reduced_backward(reduced_rows(precise_product(flattened_input, query_key_value_weight) + adapter_change(inner_attention_rows, adapter_out_columns[:, :3 * hidden_width], 3)))
    triple = query_key_value.reshape(seq_len, 3, head_count, HDIM)
    scores = reduced_backward(jnp.einsum('qhd,khd->hqk', triple[:, 0], triple[:, 1], precision=FULL_PRECISION) * HDIM ** (-0.5))
    scores = jnp.where(key_valid_mask[None, None, :], scores, NEG_FILL)
    row_top = lax.optimization_barrier(jnp.max(scores, -1, keepdims=True))
    exponent = jnp.exp(scores - row_top)
    probs = exponent / lax.optimization_barrier(jnp.sum(exponent, -1, keepdims=True))
    attended_rows = jnp.einsum('hqk,khd->qhd', reduced_rows(probs), triple[:, 2], precision=FULL_PRECISION).reshape(seq_len, hidden_width)
    attended_rows = reduced_backward(reduced_rows(attended_rows))
    inner_output_rows = inner_low(attended_rows, a_in[:, 3 * rank_size:4 * rank_size])
    side_branch = reduced_backward(precise_product(attended_rows, output_weight) + adapter_change(inner_output_rows, adapter_out_columns[:, 3 * hidden_width:4 * hidden_width], 1))
    middle = layer_norm(hidden_rows + side_branch, gain_pair[0])
    middle_reduced = reduced_rows(middle)
    inner_up_rows = inner_low(middle_reduced, a_in[:, 4 * rank_size:5 * rank_size])
    upper_half = reduced_backward(precise_product(middle_reduced, up_weight) + adapter_change(inner_up_rows, adapter_out_columns[:, 5 * hidden_width:], 1))
    activated = reduced_rows(jax.nn.gelu(upper_half))
    inner_down_rows = inner_low(activated, a_down)
    lower_half = reduced_backward(precise_product(activated, down_weight) + adapter_change(inner_down_rows, adapter_out_columns[:, 4 * hidden_width:5 * hidden_width], 1))
    return layer_norm(middle + lower_half, gain_pair[1])

def item_loss(trained_part, frozen_part, item):
    adapter_outputs, class_projection = trained_part
    token_embedding_table, position_table, norm_gain_table, query_key_value_weight, output_weight, up_weight, down_weight, adapter_inputs, adapter_down_input, head_dense_maps = frozen_part
    token_row, length_one, masked_selector, target_row, label_one = item
    hidden_rows = layer_norm(token_embedding_table[token_row] + position_table, norm_gain_table[0])
    key_valid_mask = jnp.arange(ITEM_LEN) < length_one
    for layer_number in range(ENCODER_LAYERS):
        hidden_rows = apply_layer(hidden_rows, adapter_outputs[layer_number], query_key_value_weight[layer_number], output_weight[layer_number], up_weight[layer_number], down_weight[layer_number], adapter_inputs[layer_number], adapter_down_input[layer_number], norm_gain_table[1 + 2 * layer_number:3 + 2 * layer_number], key_valid_mask)
    final_low = reduced_rows(hidden_rows)
    picked_rows = final_low[masked_selector]
    pre_mask = reduced_backward(precise_product(picked_rows, head_dense_maps[0]))
    feature = reduced_rows(layer_norm(jax.nn.gelu(pre_mask), norm_gain_table[2 * ENCODER_LAYERS + 1]))
    logits = reduced_backward(precise_product(feature, token_embedding_table.T))
    logit_top = lax.optimization_barrier(jnp.max(logits, -1, keepdims=True))
    log_total = logit_top[:, 0] + jnp.log(lax.optimization_barrier(jnp.sum(jnp.exp(logits - logit_top), -1)))
    target_logit = jnp.take_along_axis(logits, target_row[:, None], 1)[:, 0]
    slot_live = jnp.arange(SLOTS) < length_one * 15 // 100
    masked_sum = jnp.sum(jnp.where(slot_live, log_total - target_logit, 0.0))
    pooled = jnp.tanh(reduced_backward(precise_product(final_low[0:1], head_dense_maps[1])))
    class_logits = precise_product(pooled, class_projection[:-1]) + class_projection[-1:]
    class_top = jnp.max(class_logits)
    class_total = class_top + jnp.log(jnp.sum(jnp.exp(class_logits - class_top)))
    class_pick = jnp.sum(jnp.where(jnp.arange(LABELS) == label_one, class_logits[0], 0.0))
    return masked_sum + class_total - class_pick

def moment_update(weight, grad, first, second):
    first_new = BETA_ONE * first + (1.0 - BETA_ONE) * grad
    second_new = BETA_TWO * second + (1.0 - BETA_TWO) * grad * grad
    fix_one = 1.0 - BETA_ONE ** STEP
    fix_two = 1.0 - BETA_TWO ** STEP
    step_size = first_new / fix_one / (jnp.sqrt(second_new / fix_two) + ADAM_EPS)
    return (weight - RATE * (step_size + DECAY * weight), first_new, second_new)

def reference(input_token_ids, lengths, masked_positions, masked_token_targets, labels, token_embedding_table, position_table, norm_gain_table, query_key_value_weight, output_weight, up_weight, down_weight, adapter_inputs, adapter_down_input, head_dense_maps, adapter_outputs, class_projection, adapter_moment_first, adapter_moment_second, class_moment_first, class_moment_second):
    frozen_part = tuple((make_array.astype(jnp.float32) for make_array in (token_embedding_table, position_table, norm_gain_table, query_key_value_weight, output_weight, up_weight, down_weight, adapter_inputs, adapter_down_input, head_dense_maps)))
    items = (input_token_ids.reshape(-1, ITEM_LEN), lengths.reshape(-1), masked_positions.reshape(-1, SLOTS), masked_token_targets.reshape(-1, SLOTS), labels.reshape(-1))

    def overall_loss(trained_part):

        def one_item(item):
            return item_loss(trained_part, frozen_part, item)
        return jnp.sum(lax.map(jax.checkpoint(one_item), items))
    loss_accumulated, backward_pull = jax.vjp(overall_loss, (adapter_outputs, class_projection))
    (adapter_out_gradient, grad_head), = backward_pull(jnp.ones((), jnp.float32))
    term_count = (jnp.sum(lengths * 15 // 100) + MICRO * ITEMS_ALL).astype(jnp.float32)
    adapter_out_gradient = adapter_out_gradient / term_count
    grad_head = grad_head / term_count
    overall_norm = jnp.sqrt(jnp.sum(adapter_out_gradient * adapter_out_gradient) + jnp.sum(grad_head * grad_head))
    multiplier = CLIP_AT / jnp.maximum(overall_norm, CLIP_AT)
    adapter_outputs_next, adapter_moment_first_next, adapter_moment_second_next = moment_update(adapter_outputs, adapter_out_gradient * multiplier, adapter_moment_first, adapter_moment_second)
    class_projection_next, class_moment_first_next, class_moment_second_next = moment_update(class_projection, grad_head * multiplier, class_moment_first, class_moment_second)
    loss_and_terms = jnp.stack([loss_accumulated, term_count])
    return (loss_and_terms, overall_norm.reshape(1), adapter_outputs_next, adapter_moment_first_next, adapter_moment_second_next, class_projection_next, class_moment_first_next, class_moment_second_next)
```

```python
import jax
import jax.numpy as jnp
from jax import lax
from jax.sharding import PartitionSpec as P

HDIM = 64
STEP = 10
NORM_EPS = 1e-05
ADAPTER_SCALE = 2.0
NEG_FILL = -1e30
CLIP_AT = 0.001
RATE = 0.03
BETA_ONE = 0.9
BETA_TWO = 0.999
ADAM_EPS = 1e-08
DECAY = 0.01
BF = jnp.bfloat16
F32 = jnp.float32


def dot(left, right):
    return jnp.dot(left, right, preferred_element_type=F32)


def dot_nt(left, right):
    return lax.dot_general(left, right, (((1,), (1,)), ((), ())), preferred_element_type=F32)


def dot_tn(left, right):
    return lax.dot_general(left, right, (((0,), (0,)), ((), ())), preferred_element_type=F32)


def norm_parts(values):
    center = values - jnp.mean(values, -1, keepdims=True)
    spread = jnp.mean(center * center, -1, keepdims=True)
    rstd = lax.rsqrt(spread + NORM_EPS)
    return center * rstd, rstd


def norm_back(grad_hat, hat, rstd):
    first = jnp.mean(grad_hat, -1, keepdims=True)
    second = jnp.mean(grad_hat * hat, -1, keepdims=True)
    return rstd * (grad_hat - first - hat * second)


def gelu_both(values):
    root = 0.7978845608028654
    square = values * values
    bend = jnp.tanh(root * values * (1.0 + 0.044715 * square))
    half = 0.5 * (1.0 + bend)
    slope = half + 0.5 * values * (1.0 - bend * bend) * root * (1.0 + 0.134145 * square)
    return values * half, slope


def high_low(values):
    high = lax.reduce_precision(values, 8, 7)
    return high.astype(BF), (values - high).astype(BF)


def swap(value, axis, mask):
    size = lax.axis_size(axis)
    return lax.ppermute(value, axis, [(i, i ^ mask) for i in range(size)])


def deliver(parts):
    size = parts.shape[0]
    if size & (size - 1):
        return lax.psum_scatter(parts, "vocab", scatter_dimension=0, tiled=True)[0]
    index = lax.axis_index("vocab")
    core = index % 2
    pairs = parts.reshape((size // 2, 2) + parts.shape[1:])
    mine = lax.dynamic_index_in_dim(pairs, core, 1, keepdims=False)
    other = lax.dynamic_index_in_dim(pairs, 1 - core, 1, keepdims=False)
    mine = mine + swap(other, "vocab", 1)
    row = index // 2
    total = lax.dynamic_index_in_dim(mine, row, 0, keepdims=False)
    for mask in range(1, size // 2):
        sent = lax.dynamic_index_in_dim(mine, row ^ mask, 0, keepdims=False)
        total = total + swap(sent, "vocab", 2 * mask)
    return total


def reduce_all(flat):
    rows = flat.shape[0]
    steps = []
    for axis in ("vocab", "dp"):
        size = lax.axis_size(axis)
        mask = 1
        while mask < size:
            steps.append((axis, mask))
            mask *= 2
    pad = -rows % (8 << len(steps))
    now = jnp.pad(flat, ((0, pad), (0, 0)))
    for axis, mask in steps:
        bit = (lax.axis_index(axis) // mask) % 2
        half = now.shape[0] // 2
        keep = lax.dynamic_slice_in_dim(now, bit * half, half)
        send = lax.dynamic_slice_in_dim(now, (1 - bit) * half, half)
        now = keep + swap(send, axis, mask)
    for axis, mask in reversed(steps):
        bit = (lax.axis_index(axis) // mask) % 2
        got = swap(now, axis, mask)
        now = jnp.where(bit == 0, jnp.concatenate([now, got]), jnp.concatenate([got, now]))
    return now[:rows]


def adapter_tables(adapter_inputs, adapter_down_input, adapter_outputs):
    layers, width, columns = adapter_inputs.shape
    rank = adapter_down_input.shape[2]
    total = adapter_outputs.shape[2]
    one = jnp.pad(adapter_inputs, ((0, 0), (0, 0), (0, 64 - columns)))
    a_all = jnp.concatenate([one, one], 2)
    one = jnp.pad(adapter_down_input, ((0, 0), (0, 0), (columns, 64 - columns - rank)))
    a_down = jnp.concatenate([one, one], 2)
    high = lax.reduce_precision(ADAPTER_SCALE * adapter_outputs, 8, 7)
    both = jnp.stack([high, ADAPTER_SCALE * adapter_outputs - high], 1)
    column = jnp.arange(total) // width
    group = jnp.where(column < 4, column, jnp.where(column == 4, 5, 4))
    keep = jnp.arange(8)[:, None] == group[None, :]
    b_all = jnp.where(keep[None, None, :, None, :], both[:, :, None, :, :], 0.0)
    return a_all, a_down, b_all.reshape(layers, 128, total).astype(BF)


def heads(rows):
    return rows.reshape(rows.shape[0], -1, HDIM)


def attend(q, k, v, length):
    scores = jnp.einsum("qhd,khd->hqk", heads(q), heads(k), preferred_element_type=F32)
    valid = jnp.arange(k.shape[0]) < length
    scores = jnp.where(valid, scores * HDIM**-0.5, NEG_FILL)
    top = jnp.max(scores, -1, keepdims=True)
    exponent = jnp.exp(scores - top)
    total = jnp.sum(exponent, -1, keepdims=True)
    out = jnp.einsum("hqk,khd->qhd", (exponent / total).astype(BF), heads(v), preferred_element_type=F32)
    return out.reshape(q.shape).astype(BF), top + jnp.log(total)


def attend_back(q, k, v, length, log_total, grad):
    scores = jnp.einsum("qhd,khd->hqk", heads(q), heads(k), preferred_element_type=F32)
    valid = jnp.arange(k.shape[0]) < length
    scores = jnp.where(valid, scores * HDIM**-0.5, NEG_FILL)
    probs = jnp.exp(scores - log_total)
    grad_probs = jnp.einsum("qhd,khd->hqk", heads(grad), heads(v), preferred_element_type=F32)
    grad_v = jnp.einsum("hqk,qhd->khd", probs.astype(BF), heads(grad), preferred_element_type=F32)
    row = jnp.sum(grad_probs * probs, -1, keepdims=True)
    grad_scores = (probs * (grad_probs - row)).astype(BF)
    grad_q = jnp.einsum("hqk,khd->qhd", grad_scores, heads(k), preferred_element_type=F32) * HDIM**-0.5
    grad_k = jnp.einsum("hqk,qhd->khd", grad_scores, heads(q), preferred_element_type=F32) * HDIM**-0.5
    return (
        grad_q.reshape(q.shape).astype(BF),
        grad_k.reshape(k.shape).astype(BF),
        grad_v.reshape(k.shape).astype(BF),
    )


def upper_part(hidden, attn, weights, gains):
    (_, wo, wu, wd, a_all, a_down, b_all) = weights
    width = wo.shape[0]
    inner_o = dot(attn, a_all).astype(BF)
    first = hidden + dot(attn, wo) + dot(inner_o, b_all[:, 3 * width : 4 * width])
    hat1, rstd1 = norm_parts(first)
    mid = hat1 * gains[0]
    low = mid.astype(BF)
    inner_u = dot(low, a_all).astype(BF)
    upper = dot(low, wu) + dot(inner_u, b_all[:, 5 * width :])
    active, slope = gelu_both(upper)
    active = active.astype(BF)
    inner_d = dot(active, a_down).astype(BF)
    second = mid + dot(active, wd) + dot(inner_d, b_all[:, 4 * width : 5 * width])
    hat2, rstd2 = norm_parts(second)
    lane = jnp.arange(128) % 64 // 8
    inner = jnp.where(lane == 3, inner_o, jnp.where(lane == 4, inner_u, inner_d))
    return hat2 * gains[1], (hat1.astype(BF), rstd1, slope.astype(BF), hat2.astype(BF), rstd2, inner)


def upper_back(grad, saved, weights, gains):
    (_, wo, wu, wd, a_all, a_down, b_all) = weights
    width = wo.shape[0]
    hat1, rstd1, slope, hat2, rstd2, inner = saved
    grad2 = norm_back(grad * gains[1], hat2.astype(F32), rstd2)
    low = grad2.astype(BF)
    d_inner = dot_nt(low, b_all[:, 4 * width : 5 * width]).astype(BF)
    grad_active = dot_nt(low, wd) + dot_nt(d_inner, a_down)
    b_down = dot_tn(inner, low)[40:48]
    grad_upper = (grad_active * slope.astype(F32)).astype(BF)
    d_inner = dot_nt(grad_upper, b_all[:, 5 * width :]).astype(BF)
    grad_mid = grad2 + dot_nt(grad_upper, wu) + dot_nt(d_inner, a_all)
    b_up = dot_tn(inner, grad_upper)[32:40]
    grad1 = norm_back(grad_mid * gains[0], hat1.astype(F32), rstd1)
    low = grad1.astype(BF)
    d_inner = dot_nt(low, b_all[:, 3 * width : 4 * width]).astype(BF)
    grad_attn = (dot_nt(low, wo) + dot_nt(d_inner, a_all)).astype(BF)
    b_out = dot_tn(inner, low)[24:32]
    return grad1, grad_attn, ADAPTER_SCALE * jnp.concatenate([b_out, b_down, b_up], 1)


def first_layer(length, rows, positions, gain, gains, weights):
    wqkv, a_all, b_all = weights[0], weights[4], weights[6]
    width = rows.shape[1]
    hat0, _ = norm_parts(rows.astype(F32) + positions.astype(F32))
    hidden = hat0 * gain
    low = hidden.astype(BF)
    inner = dot(low, a_all).astype(BF)
    qkv = (dot(low, wqkv) + dot(inner, b_all[:, : 3 * width])).astype(BF)
    q, k, v = (qkv[:, i * width : (i + 1) * width] for i in range(3))
    attn, log_total = attend(q, k, v, length)
    out, saved = upper_part(hidden, attn, weights, gains)
    return high_low(out), (q, k, v, log_total, inner) + saved


def first_back(length, grad, saved, weights, gains):
    q, k, v, log_total, inner = saved[:5]
    _, grad_attn, b_rest = upper_back(grad, saved[5:], weights, gains)
    grads = attend_back(q, k, v, length, log_total, grad_attn)
    b_qkv = [dot_tn(inner, g)[8 * i : 8 * i + 8] for i, g in enumerate(grads)]
    return jnp.concatenate([ADAPTER_SCALE * jnp.concatenate(b_qkv, 1), b_rest], 1)


def last_layer(length, high, low, picks, gains, weights):
    wqkv, a_all, b_all = weights[0], weights[4], weights[6]
    width = high.shape[1]
    hot = (picks[:, None] == jnp.arange(high.shape[0])[None, :]).astype(BF)
    x = dot(hot, high).astype(BF)
    hidden = x.astype(F32) + dot(hot, low)
    inner_q = dot(x, a_all).astype(BF)
    q = (dot(x, wqkv[:, :width]) + dot(inner_q, b_all[:, :width])).astype(BF)
    inner = dot(high, a_all).astype(BF)
    kv = (dot(high, wqkv[:, width:]) + dot(inner, b_all[:, width : 3 * width])).astype(BF)
    k, v = kv[:, :width], kv[:, width:]
    attn, log_total = attend(q, k, v, length)
    out, saved = upper_part(hidden, attn, weights, gains)
    return out.astype(BF), (hot, q, k, v, log_total, inner_q, inner) + saved


def last_back(length, grad, saved, weights, gains):
    wqkv, a_all, b_all = weights[0], weights[4], weights[6]
    hot, q, k, v, log_total, inner_q, inner = saved[:7]
    width = q.shape[1]
    grad1, grad_attn, b_rest = upper_back(grad, saved[7:], weights, gains)
    d_q, d_k, d_v = attend_back(q, k, v, length, log_total, grad_attn)
    d_inner = dot_nt(d_q, b_all[:, :width]).astype(BF)
    picked = grad1 + dot_nt(d_q, wqkv[:, :width]) + dot_nt(d_inner, a_all)
    high, low = high_low(picked)
    d_kv = jnp.concatenate([d_k, d_v], 1)
    d_inner = dot_nt(d_kv, b_all[:, width : 3 * width]).astype(BF)
    out = dot_nt(d_kv, wqkv[:, width:]) + dot_nt(d_inner, a_all) + dot_tn(hot, high) + dot_tn(hot, low)
    b_qkv = [dot_tn(inner_q, d_q)[0:8], dot_tn(inner, d_k)[8:16], dot_tn(inner, d_v)[16:24]]
    return out, jnp.concatenate([ADAPTER_SCALE * jnp.concatenate(b_qkv, 1), b_rest], 1)


def table_pass(features, table):
    logits = dot_nt(features, table)
    top = jnp.max(logits, -1, keepdims=True)
    exponent = jnp.exp(logits - top)
    total = jnp.sum(exponent, -1, keepdims=True)
    return dot(exponent.astype(BF), table) / total, top, total


def moment_update(weight, grad, first, second):
    first_new = BETA_ONE * first + (1.0 - BETA_ONE) * grad
    second_new = BETA_TWO * second + (1.0 - BETA_TWO) * grad * grad
    fix_one = 1.0 - BETA_ONE**STEP
    fix_two = 1.0 - BETA_TWO**STEP
    step_size = first_new / fix_one / (jnp.sqrt(second_new / fix_two) + ADAM_EPS)
    return (weight - RATE * (step_size + DECAY * weight), first_new, second_new)


def body(
    input_token_ids,
    lengths,
    masked_positions,
    masked_token_targets,
    labels,
    token_embedding_table,
    position_table,
    norm_gain_table,
    query_key_value_weight,
    output_weight,
    up_weight,
    down_weight,
    adapter_inputs,
    adapter_down_input,
    head_dense_maps,
    adapter_outputs,
    class_projection,
    adapter_moment_first,
    adapter_moment_second,
    class_moment_first,
    class_moment_second,
):
    table_rows, width = token_embedding_table.shape
    seq_len = input_token_ids.shape[2]
    slots = masked_positions.shape[2]
    vocab_size = lax.axis_size("vocab")
    vocab_index = lax.axis_index("vocab")
    vocab_start = vocab_index * table_rows
    count = input_token_ids.shape[0] * input_token_ids.shape[1]
    picks = -(-(slots + 1) // 16) * 16

    packed = jnp.concatenate(
        [
            input_token_ids.reshape(count, seq_len),
            masked_positions.reshape(count, slots),
            masked_token_targets.reshape(count, slots),
            lengths.reshape(count, 1),
            labels.reshape(count, 1),
        ],
        1,
    )
    items = lax.all_gather(packed, "vocab", axis=0, tiled=True)
    item_count = items.shape[0]
    item_lengths = items[:, -2]
    number = jnp.arange(item_count)
    before = (item_lengths[None, :] > item_lengths[:, None]) | (
        (item_lengths[None, :] == item_lengths[:, None]) & (number[None, :] < number[:, None])
    )
    rank = jnp.sum(before.astype(jnp.int32), 1)
    place = rank.reshape(item_count, 1) == number[None, :]
    items = jnp.sum(jnp.where(place[:, :, None], items[:, None, :], 0), 0)
    items = items.reshape(count, vocab_size, -1)
    items = jnp.stack([items[i] if i % 2 == 0 else items[i, ::-1] for i in range(count)])
    own = lax.dynamic_index_in_dim(items, vocab_index, 1, keepdims=False)
    own_lengths, own_labels = own[:, -2], own[:, -1]
    own_positions = own[:, seq_len : seq_len + slots]

    def lookup(ids):
        local = ids - vocab_start
        inside = (local >= 0) & (local < table_rows)
        rows = jnp.take(token_embedding_table, jnp.clip(local, 0, table_rows - 1), axis=0)
        return deliver(jnp.where(inside[..., None], rows, jnp.zeros((), BF)))

    a_all, a_down, b_all = adapter_tables(adapter_inputs, adapter_down_input, adapter_outputs)
    weights = [
        (query_key_value_weight[i], output_weight[i], up_weight[i], down_weight[i], a_all[i], a_down[i], b_all[i])
        for i in range(2)
    ]
    hidden, saved0, final, saved1 = [], [], [], []
    for i in range(count):
        rows = lookup(items[i, :, :seq_len])
        out, saved = first_layer(
            own_lengths[i], rows, position_table, norm_gain_table[0], norm_gain_table[1:3], weights[0]
        )
        hidden.append(out)
        saved0.append(saved)
    target_rows = jnp.stack(
        [lookup(items[i, :, seq_len + slots : seq_len + 2 * slots]) for i in range(count)]
    )
    pick_index = jnp.concatenate(
        [own_positions, jnp.zeros((count, 1), jnp.int32), jnp.full((count, picks - slots - 1), -1, jnp.int32)], 1
    )
    for i in range(count):
        out, saved = last_layer(
            own_lengths[i], hidden[i][0], hidden[i][1], pick_index[i], norm_gain_table[3:5], weights[1]
        )
        final.append(out)
        saved1.append(saved)

    features = jnp.concatenate([f[:slots] for f in final])
    pre = dot(features, head_dense_maps[0])
    act, act_slope = gelu_both(pre)
    hat, rstd = norm_parts(act)
    gain = norm_gain_table[5]
    z = (hat * gain).astype(BF)
    z_all = lax.all_gather(z, "vocab", axis=0, tiled=True)
    summed, top, total = table_pass(z_all, token_embedding_table)
    own_slots = count * slots
    stats = lax.all_gather(jnp.concatenate([top, total], 1), "vocab", axis=0)
    top_all = jnp.max(stats[:, :, 0], 0)
    total_all = jnp.sum(stats[:, :, 1] * jnp.exp(stats[:, :, 0] - top_all), 0)
    share = total[:, 0] * jnp.exp(top[:, 0] - top_all) / total_all
    grad_z = deliver((summed * share[:, None]).astype(BF).reshape(vocab_size, own_slots, width))
    log_total = lax.dynamic_slice_in_dim(top_all + jnp.log(total_all), vocab_index * own_slots, own_slots)
    target_rows = target_rows.reshape(own_slots, width).astype(F32)
    target_logit = jnp.sum(z.astype(F32) * target_rows, -1)
    live = (jnp.arange(slots)[None, :] < own_lengths[:, None] * 15 // 100).reshape(-1)
    masked_loss = jnp.sum(jnp.where(live, log_total - target_logit, 0.0))
    grad_z = jnp.where(live[:, None], grad_z.astype(F32) - target_rows, 0.0)
    grad_pre = (norm_back(grad_z * gain, hat, rstd) * act_slope).astype(BF)
    grad_rows = dot_nt(grad_pre, head_dense_maps[0]).reshape(count, slots, width)

    first_rows = jnp.concatenate([f[slots : slots + 1] for f in final])
    pooled = jnp.tanh(dot(first_rows, head_dense_maps[1]))
    classes = class_projection.shape[1]
    class_logits = (
        jnp.sum(pooled[:, :, None] * class_projection[None, :-1, :], 1) + class_projection[-1:]
    )
    class_top = jnp.max(class_logits, -1, keepdims=True)
    class_exp = jnp.exp(class_logits - class_top)
    class_sum = jnp.sum(class_exp, -1, keepdims=True)
    label_hot = (jnp.arange(classes)[None, :] == own_labels[:, None]).astype(F32)
    class_loss = jnp.sum(class_top[:, 0] + jnp.log(class_sum[:, 0]) - jnp.sum(class_logits * label_hot, -1))
    grad_class = class_exp / class_sum - label_hot
    grad_head = jnp.concatenate(
        [
            jnp.sum(pooled[:, :, None] * grad_class[:, None, :], 0),
            jnp.sum(grad_class, 0, keepdims=True),
        ],
        0,
    )
    grad_pooled = jnp.sum(grad_class[:, None, :] * class_projection[None, :-1, :], -1)
    grad_pre_class = (grad_pooled * (1.0 - pooled * pooled)).astype(BF)
    grad_first = dot_nt(grad_pre_class, head_dense_maps[1])

    grads = [0.0, 0.0]
    for i in range(count):
        grad = jnp.concatenate(
            [grad_rows[i], grad_first[i : i + 1], jnp.zeros((picks - slots - 1, width), F32)]
        )
        grad, b_grad = last_back(own_lengths[i], grad, saved1[i], weights[1], norm_gain_table[3:5])
        grads[1] = grads[1] + b_grad
        grads[0] = grads[0] + first_back(own_lengths[i], grad, saved0[i], weights[0], norm_gain_table[1:3])

    terms = (jnp.sum(live.astype(jnp.int32)) + count).astype(F32)
    flat = jnp.concatenate(
        [
            jnp.stack(grads).reshape(-1),
            grad_head.reshape(-1),
            jnp.stack([masked_loss + class_loss, terms]),
        ]
    )
    size = flat.shape[0]
    flat = jnp.pad(flat, (0, -size % 128)).reshape(-1, 128)
    flat = reduce_all(flat).reshape(-1)
    sum_stats = flat[size - 2 : size]
    split = adapter_outputs.size
    adapter_grad = flat[:split].reshape(adapter_outputs.shape) / sum_stats[1]
    grad_head = flat[split : size - 2].reshape(class_projection.shape) / sum_stats[1]
    overall_norm = jnp.sqrt(jnp.sum(adapter_grad * adapter_grad) + jnp.sum(grad_head * grad_head))
    multiplier = CLIP_AT / jnp.maximum(overall_norm, CLIP_AT)
    adapter_new = moment_update(
        adapter_outputs, adapter_grad * multiplier, adapter_moment_first, adapter_moment_second
    )
    class_new = moment_update(
        class_projection, grad_head * multiplier, class_moment_first, class_moment_second
    )
    return (sum_stats, overall_norm.reshape(1)) + adapter_new + class_new


def solution(mesh):
    split = P(None, ("dp", "vocab"), None)
    placed = (split, P(None, ("dp", "vocab")), split, split, P(None, ("dp", "vocab")), P("vocab", None)) + (P(),) * 15
    return jax.shard_map(body, mesh=mesh, in_specs=placed, out_specs=(P(),) * 8, check_vma=False)
```

```python
import functools

import jax
import jax.numpy as jnp
from jax import lax
from jax.experimental import pallas as pl
from jax.experimental.pallas import tpu as pltpu
from jax.sharding import PartitionSpec as P

HDIM = 64
STEP = 10
NORM_EPS = 1e-05
ADAPTER_SCALE = 2.0
NEG_FILL = -1e30
CLIP_AT = 0.001
RATE = 0.03
BETA_ONE = 0.9
BETA_TWO = 0.999
ADAM_EPS = 1e-08
DECAY = 0.01
BF = jnp.bfloat16
F32 = jnp.float32


def dot(left, right):
    return jnp.dot(left, right, preferred_element_type=F32)


def dot_nt(left, right):
    return lax.dot_general(left, right, (((1,), (1,)), ((), ())), preferred_element_type=F32)


def dot_tn(left, right):
    return lax.dot_general(left, right, (((0,), (0,)), ((), ())), preferred_element_type=F32)


def norm_parts(values):
    center = values - jnp.mean(values, -1, keepdims=True)
    spread = jnp.mean(center * center, -1, keepdims=True)
    rstd = lax.rsqrt(spread + NORM_EPS)
    return center * rstd, rstd


def norm_back(grad_hat, hat, rstd):
    first = jnp.mean(grad_hat, -1, keepdims=True)
    second = jnp.mean(grad_hat * hat, -1, keepdims=True)
    return rstd * (grad_hat - first - hat * second)


def gelu_both(values):
    root = 0.7978845608028654
    square = values * values
    bend = jnp.tanh(root * values * (1.0 + 0.044715 * square))
    half = 0.5 * (1.0 + bend)
    slope = half + 0.5 * values * (1.0 - bend * bend) * root * (1.0 + 0.134145 * square)
    return values * half, slope


def high_low(values):
    high = lax.reduce_precision(values, 8, 7)
    return high.astype(BF), (values - high).astype(BF)


def swap(value, axis, mask):
    size = lax.axis_size(axis)
    return lax.ppermute(value, axis, [(i, i ^ mask) for i in range(size)])


def deliver(parts):
    size = parts.shape[0]
    if size & (size - 1):
        return lax.psum_scatter(parts, "vocab", scatter_dimension=0, tiled=True)[0]
    index = lax.axis_index("vocab")
    core = index % 2
    pairs = parts.reshape((size // 2, 2) + parts.shape[1:])
    mine = lax.dynamic_index_in_dim(pairs, core, 1, keepdims=False)
    other = lax.dynamic_index_in_dim(pairs, 1 - core, 1, keepdims=False)
    mine = mine + swap(other, "vocab", 1)
    row = index // 2
    total = lax.dynamic_index_in_dim(mine, row, 0, keepdims=False)
    for mask in range(1, size // 2):
        sent = lax.dynamic_index_in_dim(mine, row ^ mask, 0, keepdims=False)
        total = total + swap(sent, "vocab", 2 * mask)
    return total


def reduce_all(flat):
    rows = flat.shape[0]
    steps = []
    for axis in ("vocab", "dp"):
        size = lax.axis_size(axis)
        mask = 1
        while mask < size:
            steps.append((axis, mask))
            mask *= 2
    pad = -rows % (8 << len(steps))
    now = jnp.pad(flat, ((0, pad), (0, 0)))
    for axis, mask in steps:
        bit = (lax.axis_index(axis) // mask) % 2
        half = now.shape[0] // 2
        keep = lax.dynamic_slice_in_dim(now, bit * half, half)
        send = lax.dynamic_slice_in_dim(now, (1 - bit) * half, half)
        now = keep + swap(send, axis, mask)
    for axis, mask in reversed(steps):
        bit = (lax.axis_index(axis) // mask) % 2
        got = swap(now, axis, mask)
        now = jnp.where(bit == 0, jnp.concatenate([now, got]), jnp.concatenate([got, now]))
    return now[:rows]


def adapter_tables(adapter_inputs, adapter_down_input, adapter_outputs):
    layers, width, columns = adapter_inputs.shape
    rank = adapter_down_input.shape[2]
    total = adapter_outputs.shape[2]
    one = jnp.pad(adapter_inputs, ((0, 0), (0, 0), (0, 64 - columns)))
    a_all = jnp.concatenate([one, one], 2)
    one = jnp.pad(adapter_down_input, ((0, 0), (0, 0), (columns, 64 - columns - rank)))
    a_down = jnp.concatenate([one, one], 2)
    high = lax.reduce_precision(ADAPTER_SCALE * adapter_outputs, 8, 7)
    both = jnp.stack([high, ADAPTER_SCALE * adapter_outputs - high], 1)
    column = jnp.arange(total) // width
    group = jnp.where(column < 4, column, jnp.where(column == 4, 5, 4))
    keep = jnp.arange(8)[:, None] == group[None, :]
    b_all = jnp.where(keep[None, None, :, None, :], both[:, :, None, :, :], 0.0)
    return a_all, a_down, b_all.reshape(layers, 128, total).astype(BF)


VMEM_SPEC = pl.BlockSpec(memory_space=pltpu.VMEM)
SMEM_SPEC = pl.BlockSpec(memory_space=pltpu.SMEM)
ANY_SPEC = pl.BlockSpec(memory_space=pl.ANY)
PARAMS = pltpu.CompilerParams(vmem_limit_bytes=60 * 2**20)
CHUNK = 16
EXTRA = 128


def chunked(rows, body, step=CHUNK):
    for start in range(0, rows, step):
        body(slice(start, start + step))


def lane_half():
    return lax.broadcasted_iota(jnp.int32, (1, 128), 1) < HDIM


def split_three(values):
    high = values.astype(BF)
    rest = values - high.astype(F32)
    middle = rest.astype(BF)
    return high, middle, (rest - middle.astype(F32)).astype(BF)


def lanes_of(parts):
    lane = lax.broadcasted_iota(jnp.int32, (1, 128), 1) % HDIM
    out = jnp.zeros((), BF)
    for i, part in reversed(list(enumerate(parts))):
        out = jnp.where(lane == i, part, out)
    return out


def key_extra(size, length):
    one = jnp.ones((), BF)
    mask = jnp.where(lax.broadcasted_iota(jnp.int32, (size, 1), 0) < length, 0.0, NEG_FILL)
    return lanes_of([one, one, one, jnp.broadcast_to(mask, (size, 128)).astype(BF)])


def attend_kernel(size, length, queries, q_at, k_at, v_at, out_ref, log_ref, score_ref, prob_ref):
    bias = jnp.where(lax.broadcasted_iota(jnp.int32, (1, size), 1) < length, 0.0, NEG_FILL)
    left = lane_half()

    def pair(p, carry):
        cols = pl.ds(pl.multiple_of(p * 128, 128), 128)
        q = q_at(cols) * 0.125
        k_t = k_at(cols).T
        v = v_at(cols)
        zero, one = jnp.zeros((), BF), jnp.ones((), BF)
        outs, tops = [], []
        for half in range(2):
            own = left if half == 0 else ~left
            score_ref[half] = dot(jnp.where(own, q, zero), k_t)
        for half in range(2):
            own = left if half == 0 else ~left
            top = []
            for start in range(0, queries, CHUNK):
                rows = slice(start, start + CHUNK)
                score = score_ref[half, rows, :] + bias
                highest = jnp.max(score, -1, keepdims=True)
                prob_ref[half, rows, :] = jnp.exp(score - highest).astype(BF)
                top.append(highest)
            outs.append(dot(prob_ref[half], jnp.where(own, v, one)))
            tops.append(jnp.concatenate(top, 0))
        total = pltpu.roll(jnp.where(left, outs[1], outs[0]), HDIM, 1)
        out_ref[:, cols] = (jnp.where(left, outs[0], outs[1]) / total).astype(BF)
        log_ref[:, cols] = jnp.where(left, tops[0], tops[1]) + jnp.log(total)
        return carry

    lax.fori_loop(0, log_ref.shape[1] // 128, pair, 0)


def attend_back_kernel(size, length, queries, q_at, k_at, v_at, o_at, g_at, log_ref, dq_ref, dk_ref, dv_ref,
                       score_ref, grad_ref, prob_ref, ds_ref):
    left = lane_half()
    k_extra = key_extra(size, length)
    one = jnp.ones((), BF)
    v_extra = lanes_of([one, one, one])
    across = jnp.where(
        (lax.broadcasted_iota(jnp.int32, (128, 128), 0) < HDIM) != left, 1.0, 0.0
    ).astype(BF)

    def pair(p, carry):
        cols = pl.ds(pl.multiple_of(p * 128, 128), 128)
        q = q_at(cols) * 0.125
        k, v, g = k_at(cols), v_at(cols), g_at(cols)
        logs = split_three(pltpu.roll(log_ref[:, cols], HDIM, 1))
        q_extra = lanes_of([-x for x in logs] + [one])
        product = g.astype(F32) * o_at(cols).astype(F32)
        high = product.astype(BF)
        low = (product - high.astype(F32)).astype(BF)
        g_extra = lanes_of([-x for x in split_three(dot(high, across) + dot(low, across))])
        for half in range(2):
            own = left if half == 0 else ~left
            score_ref[half] = dot_nt(jnp.where(own, k, k_extra), jnp.where(own, q, q_extra))
            grad_ref[half] = dot_nt(jnp.where(own, v, v_extra), jnp.where(own, g, g_extra))
        d_q, d_k, d_v = [], [], []
        for half in range(2):
            for start in range(0, size, CHUNK):
                rows = slice(start, start + CHUNK)
                prob = jnp.exp(score_ref[half, rows, :])
                prob_ref[half, rows, :] = prob.astype(BF)
                ds_ref[half, rows, :] = (prob * grad_ref[half, rows, :]).astype(BF)
            d_scores = ds_ref[half]
            d_v.append(dot(prob_ref[half], g))
            d_k.append(dot(d_scores, q))
            d_q.append(dot_tn(d_scores, k))
        dq_ref[:, cols] = (jnp.where(left, d_q[0], d_q[1]) * 0.125).astype(BF)
        dk_ref[:, cols] = jnp.where(left, d_k[0], d_k[1]).astype(BF)
        dv_ref[:, cols] = jnp.where(left, d_v[0], d_v[1]).astype(BF)
        return carry

    lax.fori_loop(0, log_ref.shape[1] // 128, pair, 0)


def weight_loads(hbm, width, sems, wqkv=None, wo=None, wu=None, wd=None, layer=0):
    wqkv_hbm, wo_hbm, wu_hbm, wd_hbm, ad_hbm, b_hbm = hbm
    pieces = {}
    if wqkv is not None:
        pieces["qkv"] = [
            (wqkv_hbm.at[layer], wqkv.at[:width, :]),
            (b_hbm.at[layer, :, pl.ds(0, 3 * width)], wqkv.at[width:, :]),
        ]
    if wo is not None:
        pieces["o"] = [
            (wo_hbm.at[layer], wo.at[:width, :]),
            (b_hbm.at[layer, :, pl.ds(3 * width, width)], wo.at[width:, :]),
        ]
    if wd is not None:
        pieces["down"] = [
            (wd_hbm.at[layer], wd.at[:, :width]),
            (ad_hbm.at[layer], wd.at[:, width:]),
        ]
    if wu is not None:
        pieces["up"] = [
            (wu_hbm.at[layer], wu.at[:width, :]),
            (b_hbm.at[layer, :, pl.ds(5 * width, wu.shape[1])], wu.at[width:, :]),
        ]
    loads, number = {}, 0
    for name, copies in pieces.items():
        loads[name] = []
        for source, target in copies:
            loads[name].append(pltpu.make_async_copy(source, target, sems.at[number]))
            number += 1
    return loads


def start_all(loads):
    for load in loads:
        load.start()


def wait_all(loads):
    for load in loads:
        load.wait()


def merge_inner(inner, inners):
    lane = lax.broadcasted_iota(jnp.int32, (1, 128), 1) % 64 // 8
    return jnp.where(
        lane < 3, inner, jnp.where(lane == 3, inners[0], jnp.where(lane == 4, inners[1], inners[2]))
    )


def upper_kernel(size, width, wide, gain_ref, gain, hidden, attn, x_ref, sum_ref, part, active, slope, wo, wu, wd,
                 a_ref, bd_ref, waits, hat1_ref, rstd1_ref, hat2_ref, rstd2_ref, slope_done):
    inner_o = dot(attn[:, :width], a_ref[...]).astype(BF)
    attn[:, width:] = inner_o
    waits("o")
    sum_ref[...] = dot(attn[...], wo[...])

    def middle(r):
        hat, rstd = norm_parts(hidden[r, :] + sum_ref[r, :])
        value = hat * gain_ref[gain : gain + 1, :]
        hidden[r, :] = value
        x_ref[r, :width] = value.astype(BF)
        hat1_ref[r, :] = hat.astype(BF)
        rstd1_ref[r, :] = jnp.broadcast_to(rstd, (CHUNK, 128))

    chunked(size, middle)
    inner_u = dot(x_ref[:, :width], a_ref[...]).astype(BF)
    x_ref[:, width:] = inner_u
    waits("up")
    waits("down")
    steps = wide // width

    def upper(j):
        part[j % 2] = dot(x_ref[...], wu[:, j * width : (j + 1) * width])

    total = None
    upper(0)
    for j in range(steps):
        if j + 1 < steps:
            upper(j + 1)
        cols = slice(j * width, (j + 1) * width)

        def bend(r):
            value, rise = gelu_both(part[j % 2, r, :])
            active[j % 2, r, :] = value.astype(BF)
            slope[r, cols] = rise.astype(BF)

        chunked(size, bend)
        down = dot(active[j % 2], wd[cols, :])
        if j == 0:
            sum_ref[...] = down[:, :width]
            total = down[:, width:]
        else:
            sum_ref[...] += down[:, :width]
            total = total + down[:, width:]
    slope_done()
    inner_d = total.astype(BF)
    sum_ref[...] += dot(inner_d, bd_ref[...])

    def last(r):
        hat, rstd = norm_parts(hidden[r, :] + sum_ref[r, :])
        hidden[r, :] = hat * gain_ref[gain + 1 : gain + 2, :]
        hat2_ref[r, :] = hat.astype(BF)
        rstd2_ref[r, :] = jnp.broadcast_to(rstd, (CHUNK, 128))

    chunked(size, last)
    return inner_o, inner_u, inner_d


def first_layer_kernel(
    length_ref, rows_ref, pos_ref, gain_ref, wqkv_hbm, wo_hbm, wu_hbm, wd_hbm, ad_hbm, b_hbm, a_ref, bd_ref,
    high_ref, low_ref, qkv_hbm, log_hbm, attn_hbm, inner_ref, hat1_ref, rstd1_ref, slope_hbm, hat2_ref, rstd2_ref,
    wqkv, wo, wu, wd, hidden, x_ref, qkv, log_ref, attn, sum_ref, part, active, slope, score, prob, sems,
):
    size, width = rows_ref.shape
    wide = wu.shape[1]
    hbm = (wqkv_hbm, wo_hbm, wu_hbm, wd_hbm, ad_hbm, b_hbm)
    loads = weight_loads(hbm, width, sems, wqkv, wo, wu, wd)
    for name in ("qkv", "o", "up", "down"):
        start_all(loads[name])
    def embed(r):
        hat, _ = norm_parts(rows_ref[r, :].astype(F32) + pos_ref[r, :].astype(F32))
        value = hat * gain_ref[0:1, :]
        hidden[r, :] = value
        x_ref[r, :width] = value.astype(BF)

    chunked(size, embed)
    inner = dot(x_ref[:, :width], a_ref[...]).astype(BF)
    x_ref[:, width:] = inner
    wait_all(loads["qkv"])
    for i in range(3):
        cols = slice(i * width, (i + 1) * width)
        qkv[:, cols] = dot(x_ref[...], wqkv[:, cols]).astype(BF)
    store_qkv = pltpu.make_async_copy(qkv, qkv_hbm, sems.at[8])
    store_qkv.start()
    attend_kernel(
        size, length_ref[0], size,
        lambda c: qkv[:, c],
        lambda c: qkv[:, pl.ds(c.start + width, 128)],
        lambda c: qkv[:, pl.ds(c.start + 2 * width, 128)],
        attn, log_ref, score, prob,
    )
    store_log = pltpu.make_async_copy(log_ref, log_hbm, sems.at[9])
    store_log.start()
    store_attn = pltpu.make_async_copy(attn.at[:, :width], attn_hbm, sems.at[10])
    store_attn.start()
    store_slope = pltpu.make_async_copy(slope, slope_hbm, sems.at[11])
    inners = upper_kernel(
        size, width, wide, gain_ref, 1, hidden, attn, x_ref, sum_ref, part, active, slope, wo, wu, wd, a_ref, bd_ref,
        lambda name: wait_all(loads[name]), hat1_ref, rstd1_ref, hat2_ref, rstd2_ref, store_slope.start,
    )
    inner_ref[...] = merge_inner(inner, inners)

    def last(r):
        value = hidden[r, :]
        high = value.astype(BF)
        high_ref[r, :] = high
        low_ref[r, :] = (value - high.astype(F32)).astype(BF)

    chunked(size, last)
    store_qkv.wait()
    store_log.wait()
    store_attn.wait()
    store_slope.wait()


def first_layer(length, rows, positions, gains, weights):
    wqkv, wo, wu, wd, a_all, a_down, b_all = weights
    size, width = rows.shape
    wide = wu.shape[2]
    shapes = [
        ((size, width), BF), ((size, width), BF), ((size, 3 * width), BF), ((size, width), F32), ((size, width), BF),
        ((size, 128), BF), ((size, width), BF), ((size, 128), F32), ((size, wide), BF), ((size, width), BF),
        ((size, 128), F32),
    ]
    v, a = VMEM_SPEC, ANY_SPEC
    high, low, *saved = pl.pallas_call(
        first_layer_kernel,
        out_shape=[jax.ShapeDtypeStruct(*s) for s in shapes],
        in_specs=[SMEM_SPEC, v, v, v] + [a] * 6 + [v] * 2,
        out_specs=[v, v, a, a, a, v, v, v, a, v, v],
        scratch_shapes=[
            pltpu.VMEM((width + EXTRA, 3 * width), BF), pltpu.VMEM((width + EXTRA, width), BF),
            pltpu.VMEM((width + EXTRA, wide), BF), pltpu.VMEM((wide, width + EXTRA), BF),
            pltpu.VMEM((size, width), F32), pltpu.VMEM((size, width + EXTRA), BF),
            pltpu.VMEM((size, 3 * width), BF), pltpu.VMEM((size, width), F32),
            pltpu.VMEM((size, width + EXTRA), BF), pltpu.VMEM((size, width), F32),
            pltpu.VMEM((2, size, width), F32), pltpu.VMEM((2, size, width), BF), pltpu.VMEM((size, wide), BF),
            pltpu.VMEM((2, size, size), F32), pltpu.VMEM((2, size, size), BF),
            pltpu.SemaphoreType.DMA((12,)),
        ],
        compiler_params=PARAMS,
    )(length.reshape(1), rows, positions, gains, wqkv, wo, wu, wd, a_down, b_all, a_all[0],
      b_all[0, :, 4 * width : 5 * width])
    return (high, low), tuple(saved)


def upper_back_kernel(size, width, wide, inner_t, grad_at, gain_ref, gain, hat2_ref, rstd2_ref, slope, hat1_ref, rstd1_ref,
                      wo, wu, wd, a_ref, bd_ref, out_ref, waits, grad2, x_ref, sum_ref, part, active, grad1_at):
    def second(r):
        value = norm_back(grad_at(r) * gain_ref[gain + 1 : gain + 2, :], hat2_ref[r, :].astype(F32), rstd2_ref[r, 0:1])
        grad2[r, :] = value
        x_ref[r, :width] = value.astype(BF)

    chunked(size, second)
    low = x_ref[:, :width]
    x_ref[:, width:] = dot_nt(low, bd_ref[...]).astype(BF)
    out_ref[:, 4 * width : 5 * width] = ADAPTER_SCALE * dot(inner_t[32:48], low)[8:]
    waits("down")
    waits("up")
    steps = wide // width

    def inward(j):
        part[j % 2] = dot_nt(x_ref[...], wd[j * width : (j + 1) * width, :])

    total = None
    inward(0)
    for j in range(steps):
        if j + 1 < steps:
            inward(j + 1)
        cols = slice(j * width, (j + 1) * width)

        def bend(r):
            active[j % 2, r, :] = (part[j % 2, r, :] * slope[r, cols].astype(F32)).astype(BF)

        chunked(size, bend)
        piece = dot_nt(active[j % 2], wu[:, cols])
        out_ref[:, (5 + j) * width : (6 + j) * width] = (
            ADAPTER_SCALE * dot(inner_t[32:48], active[j % 2])[:8]
        )
        if j == 0:
            sum_ref[...] = piece[:, :width]
            total = piece[:, width:]
        else:
            sum_ref[...] += piece[:, :width]
            total = total + piece[:, width:]
    sum_ref[...] += dot_nt(total.astype(BF), a_ref[...])

    def first(r):
        value = norm_back(
            (grad2[r, :] + sum_ref[r, :]) * gain_ref[gain : gain + 1, :], hat1_ref[r, :].astype(F32), rstd1_ref[r, 0:1]
        )
        x_ref[r, :width] = value.astype(BF)
        if grad1_at is not None:
            grad1_at[r, :] = value

    chunked(size, first)
    low = x_ref[:, :width]
    waits("o")
    both = dot_nt(low, wo[...])
    out_ref[:, 3 * width : 4 * width] = ADAPTER_SCALE * dot(inner_t[16:32], low)[8:]
    return (both[:, :width] + dot_nt(both[:, width:].astype(BF), a_ref[...])).astype(BF)


def first_back_kernel(
    length_ref, grad_ref, gain_ref, qkv_hbm, log_hbm, attn_hbm, inner_ref, hat1_ref, rstd1_ref, slope_hbm, hat2_ref,
    rstd2_ref, wqkv_hbm, wo_hbm, wu_hbm, wd_hbm, ad_hbm, b_hbm, a_ref, bd_ref,
    out_ref,
    wo, wu, wd, qkv, log_ref, attn, slope, grad2, x_ref, sum_ref, part, active, d_attn, dq, dk, dv, score, dscore,
    prob, ds, sems,
):
    size, width = grad_ref.shape
    wide = wu.shape[1]
    hbm = (wqkv_hbm, wo_hbm, wu_hbm, wd_hbm, ad_hbm, b_hbm)
    loads = weight_loads(hbm, width, sems, None, wo, wu, wd)
    loads["down"].append(pltpu.make_async_copy(slope_hbm, slope, sems.at[6]))
    loads["qkv"] = [
        pltpu.make_async_copy(source, target, sems.at[7 + i])
        for i, (source, target) in enumerate([(qkv_hbm, qkv), (log_hbm, log_ref), (attn_hbm, attn)])
    ]
    for name in ("down", "up", "o", "qkv"):
        start_all(loads[name])
    inner_t = inner_ref[...].T
    d_attn[...] = upper_back_kernel(
        size, width, wide, inner_t, lambda r: grad_ref[r, :], gain_ref, 1, hat2_ref, rstd2_ref, slope, hat1_ref,
        rstd1_ref, wo, wu, wd, a_ref, bd_ref, out_ref, lambda name: wait_all(loads[name]), grad2, x_ref, sum_ref,
        part, active, None,
    )
    wait_all(loads["qkv"])
    attend_back_kernel(
        size, length_ref[0], size,
        lambda c: qkv[:, c],
        lambda c: qkv[:, pl.ds(c.start + width, 128)],
        lambda c: qkv[:, pl.ds(c.start + 2 * width, 128)],
        lambda c: attn[:, c],
        lambda c: d_attn[:, c],
        log_ref, dq, dk, dv, score, dscore, prob, ds,
    )
    for i, ref in enumerate((dq, dk, dv)):
        start = 8 * i // 16 * 16
        out_ref[:, i * width : (i + 1) * width] = (
            ADAPTER_SCALE * dot(inner_t[start : start + 16], ref[...])[8 * i - start : 8 * i - start + 8]
        )


def first_back(length, grad, saved, weights, gains):
    wqkv, wo, wu, wd, a_all, a_down, b_all = weights
    qkv, log_total, attn, inner, hat1, rstd1, slope, hat2, rstd2 = saved
    size, width = grad.shape
    wide = wu.shape[2]
    v, a = VMEM_SPEC, ANY_SPEC
    low = pltpu.VMEM((size, width), BF)
    full = pltpu.VMEM((size, width), F32)
    return pl.pallas_call(
        first_back_kernel,
        out_shape=jax.ShapeDtypeStruct((8, b_all.shape[2]), F32),
        in_specs=[SMEM_SPEC, v, v, a, a, a, v, v, v, a, v, v] + [a] * 6 + [v, v],
        out_specs=v,
        scratch_shapes=[
            pltpu.VMEM((width + EXTRA, width), BF), pltpu.VMEM((width + EXTRA, wide), BF),
            pltpu.VMEM((wide, width + EXTRA), BF),
            pltpu.VMEM(qkv.shape, BF), full, low, pltpu.VMEM((size, wide), BF),
            full, pltpu.VMEM((size, width + EXTRA), BF), full, pltpu.VMEM((2, size, width), F32),
            pltpu.VMEM((2, size, width), BF), low, low, low, low,
            pltpu.VMEM((2, size, size), F32), pltpu.VMEM((2, size, size), F32),
            pltpu.VMEM((2, size, size), BF), pltpu.VMEM((2, size, size), BF),
            pltpu.SemaphoreType.DMA((10,)),
        ],
        compiler_params=PARAMS,
    )(length.reshape(1), grad, gains, qkv, log_total, attn, inner, hat1, rstd1, slope, hat2, rstd2,
      wqkv, wo, wu, wd, a_down, b_all, a_all[0], b_all[0, :, 4 * width : 5 * width])


def last_layer_kernel(
    length_ref, pick_ref, high0_ref, low0_ref, high1_ref, low1_ref, gain_ref,
    wqkv_hbm, wo_hbm, wu_hbm, wd_hbm, ad_hbm, b_hbm, map_hbm, a_ref, bd_ref,
    final_ref, z_ref, head_hat_ref, head_rstd_ref, head_slope_ref,
    q_ref, kv_hbm, log_ref, attn_out_ref, inner_ref, inner_kv_ref, hat1_ref, rstd1_ref, slope, hat2_ref, rstd2_ref,
    wqkv, wo, wu, wd, map_ref, hidden, x_ref, x_kv, kv, attn, sum_ref, part, active, score, prob, sems,
):
    count = len_items = kv.shape[0]
    size, width = high0_ref.shape
    rows = hidden.shape[0]
    picks = rows // count
    wide = wu.shape[1]
    hbm = (wqkv_hbm, wo_hbm, wu_hbm, wd_hbm, ad_hbm, b_hbm)
    loads = weight_loads(hbm, width, sems, wqkv, wo, wu, wd, 1)
    loads["map"] = [pltpu.make_async_copy(map_hbm.at[0], map_ref, sems.at[8])]
    for name in ("qkv", "o", "up", "down", "map"):
        start_all(loads[name])
    highs, lows = (high0_ref, high1_ref), (low0_ref, low1_ref)
    for i in range(count):
        r = slice(i * picks, (i + 1) * picks)
        hot = (pick_ref[r, :] == lax.broadcasted_iota(jnp.int32, (1, size), 1)).astype(BF)
        x = dot(hot, highs[i][...])
        x_ref[r, :width] = x.astype(BF)
        hidden[r, :] = x + dot(hot, lows[i][...])
        inner_kv = dot(highs[i][...], a_ref[...]).astype(BF)
        inner_kv_ref[i] = inner_kv
        x_kv[i, :, :width] = highs[i][...]
        x_kv[i, :, width:] = inner_kv
    inner = dot(x_ref[:, :width], a_ref[...]).astype(BF)
    x_ref[:, width:] = inner
    wait_all(loads["qkv"])
    q_ref[...] = dot(x_ref[...], wqkv[:, :width]).astype(BF)
    for i in range(count):
        for j in range(2):
            kv[i, :, j * width : (j + 1) * width] = dot(
                x_kv[i], wqkv[:, (j + 1) * width : (j + 2) * width]
            ).astype(BF)
    store_kv = pltpu.make_async_copy(kv, kv_hbm, sems.at[9])
    store_kv.start()
    for i in range(count):
        r = slice(i * picks, (i + 1) * picks)
        attend_kernel(
            size, length_ref[i], picks,
            lambda c: q_ref[r, c],
            lambda c: kv[i, :, c],
            lambda c: kv[i, :, pl.ds(c.start + width, 128)],
            attn.at[r], log_ref.at[r], score, prob,
        )
    attn_out_ref[...] = attn[:, :width]
    inners = upper_kernel(
        rows, width, wide, gain_ref, 3, hidden, attn, x_ref, sum_ref, part, active, slope, wo, wu, wd, a_ref, bd_ref,
        lambda name: wait_all(loads[name]), hat1_ref, rstd1_ref, hat2_ref, rstd2_ref, lambda: None,
    )
    inner_ref[...] = merge_inner(inner, inners)
    final_ref[...] = hidden[...].astype(BF)
    wait_all(loads["map"])
    sum_ref[...] = dot(final_ref[...], map_ref[...])

    def head(r):
        value, rise = gelu_both(sum_ref[r, :])
        hat, rstd = norm_parts(value)
        head_slope_ref[r, :] = rise
        head_hat_ref[r, :] = hat
        head_rstd_ref[r, :] = jnp.broadcast_to(rstd, (CHUNK, 128))
        z_ref[r, :] = (hat * gain_ref[5:6, :]).astype(BF)

    chunked(rows, head)
    store_kv.wait()


def last_layer(lengths, picks, hidden, gains, weights, maps):
    wqkv, wo, wu, wd, a_all, a_down, b_all = weights
    (high0, low0), (high1, low1) = hidden
    size, width = high0.shape
    wide = wu.shape[2]
    count = 2
    rows = picks.shape[0]
    shapes = [
        ((rows, width), BF), ((rows, width), BF), ((rows, width), F32), ((rows, 128), F32), ((rows, width), F32),
        ((rows, width), BF), ((count, size, 2 * width), BF), ((rows, width), F32), ((rows, width), BF),
        ((rows, 128), BF), ((count, size, 128), BF), ((rows, width), BF), ((rows, 128), F32), ((rows, wide), BF),
        ((rows, width), BF), ((rows, 128), F32),
    ]
    v, a = VMEM_SPEC, ANY_SPEC
    final, *saved = pl.pallas_call(
        last_layer_kernel,
        out_shape=[jax.ShapeDtypeStruct(*s) for s in shapes],
        in_specs=[SMEM_SPEC] + [v] * 6 + [a] * 7 + [v] * 2,
        out_specs=[v] * 6 + [a] + [v] * 9,
        scratch_shapes=[
            pltpu.VMEM((width + EXTRA, 3 * width), BF), pltpu.VMEM((width + EXTRA, width), BF),
            pltpu.VMEM((width + EXTRA, wide), BF), pltpu.VMEM((wide, width + EXTRA), BF),
            pltpu.VMEM((width, width), BF),
            pltpu.VMEM((rows, width), F32), pltpu.VMEM((rows, width + EXTRA), BF),
            pltpu.VMEM((count, size, width + EXTRA), BF), pltpu.VMEM((count, size, 2 * width), BF),
            pltpu.VMEM((rows, width + EXTRA), BF), pltpu.VMEM((rows, width), F32),
            pltpu.VMEM((2, rows, width), F32), pltpu.VMEM((2, rows, width), BF),
            pltpu.VMEM((2, rows // count, size), F32), pltpu.VMEM((2, rows // count, size), BF),
            pltpu.SemaphoreType.DMA((10,)),
        ],
        compiler_params=PARAMS,
    )(lengths, picks, high0, low0, high1, low1, gains, wqkv, wo, wu, wd, a_down, b_all, maps, a_all[1],
      b_all[1, :, 4 * width : 5 * width])
    return final, tuple(saved[:4]), tuple(saved[4:])


def last_back_kernel(
    length_ref, pick_ref, dz_ref, target_ref, live_ref, class_ref, gain_ref,
    z_ref, head_hat_ref, head_rstd_ref, head_slope_ref,
    q_ref, kv_hbm, log_ref, attn_ref, inner_ref, inner_kv_ref, hat1_ref, rstd1_ref, slope, hat2_ref, rstd2_ref,
    wqkv_hbm, wo_hbm, wu_hbm, wd_hbm, ad_hbm, b_hbm, map_hbm, a_ref, bd_ref,
    out0_ref, out1_ref, adapter_ref, loss_ref,
    wqkv, wo, wu, wd, map_ref, kv, grad, grad1, grad2, x_ref, sum_ref, part, active, d_attn, dq, dkv,
    score, dscore, prob, ds, sems,
):
    count, size, _ = kv.shape
    rows, width = grad.shape
    picks = rows // count
    wide = wu.shape[1]
    hbm = (wqkv_hbm, wo_hbm, wu_hbm, wd_hbm, ad_hbm, b_hbm)
    loads = weight_loads(hbm, width, sems, wqkv, wo, wu, wd, 1)
    loads["map"] = [pltpu.make_async_copy(map_hbm.at[0], map_ref, sems.at[8])]
    loads["kv"] = [pltpu.make_async_copy(kv_hbm, kv, sems.at[9])]
    for name in ("map", "down", "up", "o", "kv", "qkv"):
        start_all(loads[name])

    def head(r):
        live = live_ref[r, 0:1]
        target = target_ref[r, :].astype(F32)
        logit = jnp.sum(z_ref[r, :].astype(F32) * target, -1, keepdims=True)
        loss_ref[r, :] = jnp.broadcast_to(live * (live_ref[r, 1:2] - logit), (CHUNK, 128))
        grad_z = live * (dz_ref[r, :].astype(F32) - target)
        value = norm_back(grad_z * gain_ref[5:6, :], head_hat_ref[r, :], head_rstd_ref[r, 0:1])
        x_ref[r, :width] = (value * head_slope_ref[r, :]).astype(BF)

    chunked(rows, head)
    wait_all(loads["map"])
    grad[...] = dot_nt(x_ref[:, :width], map_ref[...]) + class_ref[...]
    inner_t = inner_ref[...].T
    d_attn[...] = upper_back_kernel(
        rows, width, wide, inner_t, lambda r: grad[r, :], gain_ref, 3, hat2_ref, rstd2_ref, slope, hat1_ref,
        rstd1_ref, wo, wu, wd, a_ref, bd_ref, adapter_ref, lambda name: wait_all(loads[name]), grad2, x_ref, sum_ref,
        part, active, grad1,
    )
    wait_all(loads["kv"])
    for i in range(count):
        r = slice(i * picks, (i + 1) * picks)
        attend_back_kernel(
            size, length_ref[i], picks,
            lambda c: q_ref[r, c],
            lambda c: kv[i, :, c],
            lambda c: kv[i, :, pl.ds(c.start + width, 128)],
            lambda c: attn_ref[r, c],
            lambda c: d_attn[r, c],
            log_ref.at[r], dq.at[r], dkv.at[i, :, :width], dkv.at[i, :, width:], score, dscore, prob, ds,
        )
    wait_all(loads["qkv"])
    both = dot_nt(dq[...], wqkv[:, :width])
    grad1[...] += both[:, :width] + dot_nt(both[:, width:].astype(BF), a_ref[...])
    adapter_ref[:, :width] = ADAPTER_SCALE * dot(inner_t[0:16], dq[...])[:8]
    total = None
    for i, out_ref in enumerate((out0_ref, out1_ref)):
        r = slice(i * picks, (i + 1) * picks)
        hot = (pick_ref[r, :] == lax.broadcasted_iota(jnp.int32, (1, size), 1)).astype(BF)
        value = grad1[r, :]
        high = value.astype(BF)
        low = (value - high.astype(F32)).astype(BF)
        both = dot_nt(dkv[i], wqkv[:, width:])
        out_ref[...] = (
            both[:, :width]
            + dot_nt(both[:, width:].astype(BF), a_ref[...])
            + dot_tn(jnp.concatenate([hot, hot], 0), jnp.concatenate([high, low], 0))
        )
        piece = dot(inner_kv_ref[i].T[0:32], dkv[i])
        total = piece if total is None else total + piece
    adapter_ref[:, width : 2 * width] = ADAPTER_SCALE * total[8:16, :width]
    adapter_ref[:, 2 * width : 3 * width] = ADAPTER_SCALE * total[16:24, width:]


def last_back(lengths, picks, dz, targets, live, class_grad, head, saved, gains, weights, maps):
    wqkv, wo, wu, wd, a_all, a_down, b_all = weights
    kv = saved[1]
    rows, width = dz.shape
    count, size, _ = kv.shape
    wide = wu.shape[2]
    v, a = VMEM_SPEC, ANY_SPEC
    low = pltpu.VMEM((rows, width), BF)
    full = pltpu.VMEM((rows, width), F32)
    return pl.pallas_call(
        last_back_kernel,
        out_shape=[
            jax.ShapeDtypeStruct((size, width), F32), jax.ShapeDtypeStruct((size, width), F32),
            jax.ShapeDtypeStruct((8, b_all.shape[2]), F32), jax.ShapeDtypeStruct((rows, 128), F32),
        ],
        in_specs=[SMEM_SPEC] + [v] * 11 + [a] + [v] * 9 + [a] * 7 + [v] * 2,
        out_specs=[v] * 4,
        scratch_shapes=[
            pltpu.VMEM((width + EXTRA, 3 * width), BF), pltpu.VMEM((width + EXTRA, width), BF),
            pltpu.VMEM((width + EXTRA, wide), BF), pltpu.VMEM((wide, width + EXTRA), BF),
            pltpu.VMEM((width, width), BF), pltpu.VMEM(kv.shape, BF),
            full, full, full, pltpu.VMEM((rows, width + EXTRA), BF), full, pltpu.VMEM((2, rows, width), F32),
            pltpu.VMEM((2, rows, width), BF), low, low, pltpu.VMEM(kv.shape, BF),
            pltpu.VMEM((2, size, rows // count), F32), pltpu.VMEM((2, size, rows // count), F32),
            pltpu.VMEM((2, size, rows // count), BF), pltpu.VMEM((2, size, rows // count), BF),
            pltpu.SemaphoreType.DMA((10,)),
        ],
        compiler_params=PARAMS,
    )(lengths, picks, dz, targets, live, class_grad, gains, *head, *saved, wqkv, wo, wu, wd, a_down, b_all, maps,
      a_all[1], b_all[1, :, 4 * width : 5 * width])


def class_kernel(row_ref, final_ref, map_ref, projection_ref, grad_ref, out_ref):
    width = final_ref.shape[1]
    classes = 3
    label = row_ref[...]
    live = label >= 0
    pooled = jnp.tanh(dot(final_ref[...], map_ref[...]))
    logits = [
        jnp.sum(pooled * projection_ref[c : c + 1, :width], -1, keepdims=True)
        + projection_ref[c : c + 1, width : width + 1]
        for c in range(classes)
    ]
    top = functools.reduce(jnp.maximum, logits)
    exponents = [jnp.exp(x - top) for x in logits]
    total = functools.reduce(jnp.add, exponents)
    loss = top + jnp.log(total)
    pulled = 0.0
    outs = []
    for c in range(classes):
        hit = (label == c).astype(F32)
        loss = loss - logits[c] * hit
        grad = jnp.where(live, exponents[c] / total - hit, 0.0)
        pulled = pulled + grad * projection_ref[c : c + 1, :width]
        outs.append((jnp.sum(pooled * grad, 0, keepdims=True), jnp.sum(grad, 0, keepdims=True)))
    grad_ref[...] = dot_nt((pulled * (1.0 - pooled * pooled)).astype(BF), map_ref[...])
    out_ref[...] = jnp.zeros(out_ref.shape, F32)
    for c in range(classes):
        out_ref[c : c + 1, :width] = outs[c][0]
        out_ref[c : c + 1, width:] = jnp.broadcast_to(outs[c][1], (1, 128))
    out_ref[classes : classes + 1, width:] = jnp.broadcast_to(
        jnp.sum(jnp.where(live, loss, 0.0), 0, keepdims=True), (1, 128)
    )


def class_head(rows, final, maps, projection):
    width = final.shape[1]
    turned = jnp.pad(projection.T, ((0, 8 - projection.shape[1]), (0, EXTRA - 1)))
    return pl.pallas_call(
        class_kernel,
        out_shape=[jax.ShapeDtypeStruct(final.shape, F32), jax.ShapeDtypeStruct((8, width + EXTRA), F32)],
        in_specs=[VMEM_SPEC] * 4,
        out_specs=[VMEM_SPEC] * 2,
        compiler_params=PARAMS,
    )(rows, final, maps[1], turned)


BLOCK = 1024


def table_kernel(z_ref, table_hbm, acc_ref, stat_ref, table, acc, score, prob, top, total, sems):
    rows = z_ref.shape[0]
    length = table.shape[0]
    blocks = length // BLOCK // 2 * 2
    tail = length - blocks * BLOCK
    loads = [
        pltpu.make_async_copy(
            table_hbm.at[pl.ds(i * BLOCK, BLOCK), :], table.at[pl.ds(i * BLOCK, BLOCK), :], sems.at[i]
        )
        for i in range(blocks)
    ]
    if tail:
        loads.append(
            pltpu.make_async_copy(
                table_hbm.at[pl.ds(blocks * BLOCK, tail), :], table.at[pl.ds(blocks * BLOCK, tail), :],
                sems.at[blocks],
            )
        )
    start_all(loads)
    top[...] = jnp.full(top.shape, NEG_FILL, F32)
    total[...] = jnp.zeros(total.shape, F32)
    acc[...] = jnp.zeros(acc.shape, F32)
    z = z_ref[...]

    def scores(start, size, slot):
        score[slot, :, :size] = dot_nt(z, table[pl.ds(start, size), :])

    def fold(start, size, slot):
        for first in range(0, rows, CHUNK):
            r = slice(first, first + CHUNK)
            value = score[slot, r, :size]
            before = top[r, :]
            now = jnp.maximum(before, jnp.max(value, -1, keepdims=True))
            exponent = jnp.exp(value - now[:, :1])
            prob[slot, r, :size] = exponent.astype(BF)
            shrink = jnp.exp(before - now)
            total[r, :] = total[r, :] * shrink + jnp.sum(exponent, -1, keepdims=True)
            top[r, :] = now
            acc[r, :] = acc[r, :] * shrink[:, :1]
        acc[...] += dot(prob[slot, :, :size], table[pl.ds(start, size), :])

    loads[0].wait()
    scores(0, BLOCK, 0)

    def two(i, carry):
        start = pl.multiple_of(i * 2 * BLOCK, BLOCK)
        wait_block(2 * i + 1)
        scores(start + BLOCK, BLOCK, 1)
        fold(start, BLOCK, 0)

        @pl.when(i + 1 < blocks // 2)
        def _():
            wait_block(2 * i + 2)

        scores(jnp.minimum(start + 2 * BLOCK, (blocks - 1) * BLOCK), BLOCK, 0)
        fold(start + BLOCK, BLOCK, 1)
        return carry

    def wait_block(i):
        pltpu.make_async_copy(
            table_hbm.at[pl.ds(0, BLOCK), :], table.at[pl.ds(0, BLOCK), :], sems.at[i]
        ).wait()

    lax.fori_loop(0, blocks // 2, two, 0)
    if tail:
        loads[-1].wait()
        scores(blocks * BLOCK, tail, 0)
        fold(blocks * BLOCK, tail, 0)
    acc_ref[...] = acc[...] / total[:, :1]
    stat_ref[:, :128] = top[...]
    stat_ref[:, 128:] = total[...]


def table_pass(z, table):
    rows, width = z.shape
    length = table.shape[0]
    widest = max(BLOCK, length - length // BLOCK // 2 * 2 * BLOCK)
    widest += -widest % 128
    return pl.pallas_call(
        table_kernel,
        out_shape=[jax.ShapeDtypeStruct((rows, width), F32), jax.ShapeDtypeStruct((rows, 256), F32)],
        in_specs=[VMEM_SPEC, ANY_SPEC],
        out_specs=[VMEM_SPEC] * 2,
        scratch_shapes=[
            pltpu.VMEM((length, width), BF), pltpu.VMEM((rows, width), F32),
            pltpu.VMEM((2, rows, widest), F32), pltpu.VMEM((2, rows, widest), BF),
            pltpu.VMEM((rows, 128), F32), pltpu.VMEM((rows, 128), F32),
            pltpu.SemaphoreType.DMA((length // BLOCK + 1,)),
        ],
        compiler_params=PARAMS,
    )(z, table)


def moment_update(weight, grad, first, second):
    first_new = BETA_ONE * first + (1.0 - BETA_ONE) * grad
    second_new = BETA_TWO * second + (1.0 - BETA_TWO) * grad * grad
    fix_one = 1.0 - BETA_ONE**STEP
    fix_two = 1.0 - BETA_TWO**STEP
    step_size = first_new / fix_one / (jnp.sqrt(second_new / fix_two) + ADAM_EPS)
    return (weight - RATE * (step_size + DECAY * weight), first_new, second_new)


def body(
    input_token_ids,
    lengths,
    masked_positions,
    masked_token_targets,
    labels,
    token_embedding_table,
    position_table,
    norm_gain_table,
    query_key_value_weight,
    output_weight,
    up_weight,
    down_weight,
    adapter_inputs,
    adapter_down_input,
    head_dense_maps,
    adapter_outputs,
    class_projection,
    adapter_moment_first,
    adapter_moment_second,
    class_moment_first,
    class_moment_second,
):
    table_rows, width = token_embedding_table.shape
    seq_len = input_token_ids.shape[2]
    slots = masked_positions.shape[2]
    vocab_size = lax.axis_size("vocab")
    vocab_index = lax.axis_index("vocab")
    vocab_start = vocab_index * table_rows
    count = input_token_ids.shape[0] * input_token_ids.shape[1]
    picks = -(-(slots + 1) // 16) * 16
    rest = picks - slots

    own_lengths = lengths.reshape(count)
    own_labels = labels.reshape(count)
    own_positions = masked_positions.reshape(count, slots)
    packed = jnp.concatenate(
        [
            input_token_ids.reshape(count, seq_len),
            jnp.pad(masked_token_targets.reshape(count, slots), ((0, 0), (0, rest)), constant_values=-1),
        ],
        1,
    )
    items = lax.all_gather(packed, "vocab", axis=0)

    def lookup(ids):
        local = ids - vocab_start
        inside = (local >= 0) & (local < table_rows)
        rows = jnp.take(token_embedding_table, jnp.clip(local, 0, table_rows - 1), axis=0)
        return deliver(jnp.where(inside[..., None], rows, jnp.zeros((), BF)))

    a_all, a_down, b_all = adapter_tables(adapter_inputs, adapter_down_input, adapter_outputs)
    weights = (query_key_value_weight, output_weight, up_weight, down_weight, a_all, a_down, b_all)
    hidden, saved0 = [], []
    for i in range(count):
        rows = lookup(items[:, i, :seq_len])
        out, saved = first_layer(own_lengths[i], rows, position_table, norm_gain_table, weights)
        hidden.append(out)
        saved0.append(saved)
    target_rows = lookup(items[:, :, seq_len:].reshape(vocab_size, -1))
    pick_index = jnp.concatenate(
        [own_positions, jnp.zeros((count, 1), jnp.int32), jnp.full((count, rest - 1), -1, jnp.int32)], 1
    ).reshape(-1, 1)
    final, head, saved1 = last_layer(own_lengths, pick_index, hidden, norm_gain_table, weights, head_dense_maps)

    z = head[0]
    z_all = lax.all_gather(z, "vocab", axis=0, tiled=True)
    summed, stat = table_pass(z_all, token_embedding_table)
    own_slots = count * picks
    stats = lax.all_gather(jnp.stack([stat[:, 0], stat[:, 128]], 1), "vocab", axis=0)
    top_all = jnp.max(stats[:, :, 0], 0)
    total_all = jnp.sum(stats[:, :, 1] * jnp.exp(stats[:, :, 0] - top_all), 0)
    share = stat[:, 128] * jnp.exp(stat[:, 0] - top_all) / total_all
    grad_z = deliver((summed * share[:, None]).astype(BF).reshape(vocab_size, own_slots, width))
    log_total = lax.dynamic_slice_in_dim(top_all + jnp.log(total_all), vocab_index * own_slots, own_slots)
    live = jnp.arange(picks)[None, :] < own_lengths[:, None] * 15 // 100
    live = (live & (jnp.arange(picks)[None, :] < slots)).reshape(-1)
    live_columns = jnp.pad(jnp.stack([live.astype(F32), log_total], 1), ((0, 0), (0, 126)))

    label_rows = jnp.where(jnp.arange(picks)[None, :] == slots, own_labels[:, None], -1).reshape(-1, 1)
    class_grad, class_out = class_head(label_rows, final, head_dense_maps, class_projection)

    classes = class_projection.shape[1]
    out0, out1, grads1, losses = last_back(
        own_lengths, pick_index, grad_z, target_rows, live_columns, class_grad, head, saved1, norm_gain_table,
        weights, head_dense_maps,
    )
    grads0 = 0.0
    for i, grad in enumerate((out0, out1)):
        grads0 = grads0 + first_back(own_lengths[i], grad, saved0[i], weights, norm_gain_table)
    grad_head = class_out[:classes, : width + 1].T
    terms = (jnp.sum(live.astype(jnp.int32)) + count).astype(F32)
    flat = jnp.concatenate(
        [
            grads0.reshape(-1),
            grads1.reshape(-1),
            grad_head.reshape(-1),
            jnp.stack([jnp.sum(losses[:, 0]) + class_out[classes, width], terms]),
        ]
    )
    size = flat.shape[0]
    flat = jnp.pad(flat, (0, -size % 128)).reshape(-1, 128)
    flat = reduce_all(flat).reshape(-1)
    sum_stats = flat[size - 2 : size]
    split = adapter_outputs.size
    adapter_grad = flat[:split].reshape(adapter_outputs.shape) / sum_stats[1]
    grad_head = flat[split : size - 2].reshape(class_projection.shape) / sum_stats[1]
    overall_norm = jnp.sqrt(jnp.sum(adapter_grad * adapter_grad) + jnp.sum(grad_head * grad_head))
    multiplier = CLIP_AT / jnp.maximum(overall_norm, CLIP_AT)
    adapter_new = moment_update(
        adapter_outputs, adapter_grad * multiplier, adapter_moment_first, adapter_moment_second
    )
    class_new = moment_update(
        class_projection, grad_head * multiplier, class_moment_first, class_moment_second
    )
    return (sum_stats, overall_norm.reshape(1)) + adapter_new + class_new


def solution(mesh):
    split = P(None, ("dp", "vocab"), None)
    placed = (split, P(None, ("dp", "vocab")), split, split, P(None, ("dp", "vocab")), P("vocab", None)) + (P(),) * 15
    return jax.shard_map(body, mesh=mesh, in_specs=placed, out_specs=(P(),) * 8, check_vma=False)
```

```python
import functools

import jax
import jax.numpy as jnp
from jax import lax
from jax.experimental import pallas as pl
from jax.experimental.pallas import tpu as pltpu
from jax.sharding import PartitionSpec as P

HDIM = 64
STEP = 10
NORM_EPS = 1e-05
ADAPTER_SCALE = 2.0
NEG_FILL = -1e30
CLIP_AT = 0.001
RATE = 0.03
BETA_ONE = 0.9
BETA_TWO = 0.999
ADAM_EPS = 1e-08
DECAY = 0.01
BF = jnp.bfloat16
F32 = jnp.float32


def dot(left, right):
    return jnp.dot(left, right, preferred_element_type=F32)


def dot_nt(left, right):
    return lax.dot_general(left, right, (((1,), (1,)), ((), ())), preferred_element_type=F32)


def dot_tn(left, right):
    return lax.dot_general(left, right, (((0,), (0,)), ((), ())), preferred_element_type=F32)


def norm_parts(values):
    center = values - jnp.mean(values, -1, keepdims=True)
    spread = jnp.mean(center * center, -1, keepdims=True)
    rstd = lax.rsqrt(spread + NORM_EPS)
    return center * rstd, rstd


def norm_back(grad_hat, hat, rstd):
    first = jnp.mean(grad_hat, -1, keepdims=True)
    second = jnp.mean(grad_hat * hat, -1, keepdims=True)
    return rstd * (grad_hat - first - hat * second)


def gelu_both(values):
    root = 0.7978845608028654
    square = values * values
    bend = jnp.tanh(root * values * (1.0 + 0.044715 * square))
    half = 0.5 * (1.0 + bend)
    slope = half + 0.5 * values * (1.0 - bend * bend) * root * (1.0 + 0.134145 * square)
    return values * half, slope


def high_low(values):
    high = lax.reduce_precision(values, 8, 7)
    return high.astype(BF), (values - high).astype(BF)


def swap(value, axis, mask):
    size = lax.axis_size(axis)
    return lax.ppermute(value, axis, [(i, i ^ mask) for i in range(size)])


def adapter_tables(adapter_inputs, adapter_down_input, adapter_outputs):
    layers, width, columns = adapter_inputs.shape
    rank = adapter_down_input.shape[2]
    total = adapter_outputs.shape[2]
    one = jnp.pad(adapter_inputs, ((0, 0), (0, 0), (0, 64 - columns)))
    a_all = jnp.concatenate([one, one], 2)
    one = jnp.pad(adapter_down_input, ((0, 0), (0, 0), (columns, 64 - columns - rank)))
    a_down = jnp.concatenate([one, one], 2)
    high = lax.reduce_precision(ADAPTER_SCALE * adapter_outputs, 8, 7)
    both = jnp.stack([high, ADAPTER_SCALE * adapter_outputs - high], 1)
    column = jnp.arange(total) // width
    group = jnp.where(column < 4, column, jnp.where(column == 4, 5, 4))
    keep = jnp.arange(8)[:, None] == group[None, :]
    b_all = jnp.where(keep[None, None, :, None, :], both[:, :, None, :, :], 0.0)
    return a_all, a_down, b_all.reshape(layers, 128, total).astype(BF)


VMEM_SPEC = pl.BlockSpec(memory_space=pltpu.VMEM)
SMEM_SPEC = pl.BlockSpec(memory_space=pltpu.SMEM)
ANY_SPEC = pl.BlockSpec(memory_space=pl.ANY)
PARAMS = pltpu.CompilerParams(vmem_limit_bytes=60 * 2**20)
CHUNK = 16
EXTRA = 128


def chunked(rows, body, step=CHUNK):
    for start in range(0, rows, step):
        body(slice(start, start + step))


def lane_half():
    return lax.broadcasted_iota(jnp.int32, (1, 128), 1) < HDIM


def split_three(values):
    high = values.astype(BF)
    rest = values - high.astype(F32)
    middle = rest.astype(BF)
    return high, middle, (rest - middle.astype(F32)).astype(BF)


def lanes_of(parts):
    lane = lax.broadcasted_iota(jnp.int32, (1, 128), 1) % HDIM
    out = jnp.zeros((), BF)
    for i, part in reversed(list(enumerate(parts))):
        out = jnp.where(lane == i, part, out)
    return out


def key_extra(size, length):
    one = jnp.ones((), BF)
    mask = jnp.where(lax.broadcasted_iota(jnp.int32, (size, 1), 0) < length, 0.0, NEG_FILL)
    return lanes_of([one, one, one, jnp.broadcast_to(mask, (size, 128)).astype(BF)])


def attend_kernel(size, length, queries, q_at, k_at, v_at, out_ref, log_ref, score_ref, prob_ref):
    bias = jnp.where(lax.broadcasted_iota(jnp.int32, (1, size), 1) < length, 0.0, NEG_FILL)
    left = lane_half()

    def pair(p, carry):
        cols = pl.ds(pl.multiple_of(p * 128, 128), 128)
        q = q_at(cols) * 0.125
        k_t = k_at(cols).T
        v = v_at(cols)
        zero, one = jnp.zeros((), BF), jnp.ones((), BF)
        outs, tops = [], []
        for half in range(2):
            own = left if half == 0 else ~left
            score_ref[half] = dot(jnp.where(own, q, zero), k_t)
        for half in range(2):
            own = left if half == 0 else ~left
            top = []
            for start in range(0, queries, CHUNK):
                rows = slice(start, start + CHUNK)
                score = score_ref[half, rows, :] + bias
                highest = jnp.max(score, -1, keepdims=True)
                prob_ref[half, rows, :] = jnp.exp(score - highest).astype(BF)
                top.append(highest)
            outs.append(dot(prob_ref[half], jnp.where(own, v, one)))
            tops.append(jnp.concatenate(top, 0))
        total = pltpu.roll(jnp.where(left, outs[1], outs[0]), HDIM, 1)
        out_ref[:, cols] = (jnp.where(left, outs[0], outs[1]) / total).astype(BF)
        log_ref[:, cols] = jnp.where(left, tops[0], tops[1]) + jnp.log(total)
        return carry

    lax.fori_loop(0, log_ref.shape[1] // 128, pair, 0)


def attend_back_kernel(size, length, queries, q_at, k_at, v_at, o_at, g_at, log_ref, dq_ref, dk_ref, dv_ref,
                       score_ref, grad_ref, prob_ref, ds_ref):
    left = lane_half()
    k_extra = key_extra(size, length)
    one = jnp.ones((), BF)
    v_extra = lanes_of([one, one, one])
    across = jnp.where(
        (lax.broadcasted_iota(jnp.int32, (128, 128), 0) < HDIM) != left, 1.0, 0.0
    ).astype(BF)

    def pair(p, carry):
        cols = pl.ds(pl.multiple_of(p * 128, 128), 128)
        q = q_at(cols) * 0.125
        k, v, g = k_at(cols), v_at(cols), g_at(cols)
        logs = split_three(pltpu.roll(log_ref[:, cols], HDIM, 1))
        q_extra = lanes_of([-x for x in logs] + [one])
        product = g.astype(F32) * o_at(cols).astype(F32)
        high = product.astype(BF)
        low = (product - high.astype(F32)).astype(BF)
        g_extra = lanes_of([-x for x in split_three(dot(high, across) + dot(low, across))])
        for half in range(2):
            own = left if half == 0 else ~left
            score_ref[half] = dot_nt(jnp.where(own, k, k_extra), jnp.where(own, q, q_extra))
            grad_ref[half] = dot_nt(jnp.where(own, v, v_extra), jnp.where(own, g, g_extra))
        d_q, d_k, d_v = [], [], []
        for half in range(2):
            for start in range(0, size, CHUNK):
                rows = slice(start, start + CHUNK)
                prob = jnp.exp(score_ref[half, rows, :])
                prob_ref[half, rows, :] = prob.astype(BF)
                ds_ref[half, rows, :] = (prob * grad_ref[half, rows, :]).astype(BF)
            d_scores = ds_ref[half]
            d_v.append(dot(prob_ref[half], g))
            d_k.append(dot(d_scores, q))
            d_q.append(dot_tn(d_scores, k))
        dq_ref[:, cols] = (jnp.where(left, d_q[0], d_q[1]) * 0.125).astype(BF)
        dk_ref[:, cols] = jnp.where(left, d_k[0], d_k[1]).astype(BF)
        dv_ref[:, cols] = jnp.where(left, d_v[0], d_v[1]).astype(BF)
        return carry

    lax.fori_loop(0, log_ref.shape[1] // 128, pair, 0)


def weight_loads(hbm, width, sems, wqkv=None, wo=None, wu=None, wd=None, layer=0):
    wqkv_hbm, wo_hbm, wu_hbm, wd_hbm, ad_hbm, b_hbm = hbm
    pieces = {}
    if wqkv is not None:
        pieces["qkv"] = [
            (wqkv_hbm.at[layer], wqkv.at[:width, :]),
            (b_hbm.at[layer, :, pl.ds(0, 3 * width)], wqkv.at[width:, :]),
        ]
    if wo is not None:
        pieces["o"] = [
            (wo_hbm.at[layer], wo.at[:width, :]),
            (b_hbm.at[layer, :, pl.ds(3 * width, width)], wo.at[width:, :]),
        ]
    if wd is not None:
        pieces["down"] = [
            (wd_hbm.at[layer], wd.at[:, :width]),
            (ad_hbm.at[layer], wd.at[:, width:]),
        ]
    if wu is not None:
        pieces["up"] = [
            (wu_hbm.at[layer], wu.at[:width, :]),
            (b_hbm.at[layer, :, pl.ds(5 * width, wu.shape[1])], wu.at[width:, :]),
        ]
    loads, number = {}, 0
    for name, copies in pieces.items():
        loads[name] = []
        for source, target in copies:
            loads[name].append(pltpu.make_async_copy(source, target, sems.at[number]))
            number += 1
    return loads


def start_all(loads):
    for load in loads:
        load.start()


def wait_all(loads):
    for load in loads:
        load.wait()


def merge_inner(inner, inners):
    lane = lax.broadcasted_iota(jnp.int32, (1, 128), 1) % 64 // 8
    return jnp.where(
        lane < 3, inner, jnp.where(lane == 3, inners[0], jnp.where(lane == 4, inners[1], inners[2]))
    )


def upper_kernel(size, width, wide, gain_ref, gain, hidden, attn, x_ref, sum_ref, part, active, slope, wo, wu, wd,
                 a_ref, bd_ref, waits, hat1_ref, rstd1_ref, hat2_ref, rstd2_ref, slope_done):
    inner_o = dot(attn[:, :width], a_ref[...]).astype(BF)
    attn[:, width:] = inner_o
    waits("o")
    sum_ref[...] = dot(attn[...], wo[...])

    def middle(r):
        hat, rstd = norm_parts(hidden[r, :] + sum_ref[r, :])
        value = hat * gain_ref[gain : gain + 1, :]
        hidden[r, :] = value
        x_ref[r, :width] = value.astype(BF)
        hat1_ref[r, :] = hat.astype(BF)
        rstd1_ref[r, :] = jnp.broadcast_to(rstd, (CHUNK, 128))

    chunked(size, middle)
    inner_u = dot(x_ref[:, :width], a_ref[...]).astype(BF)
    x_ref[:, width:] = inner_u
    waits("up")
    waits("down")
    steps = wide // width

    def upper(j):
        part[j % 2] = dot(x_ref[...], wu[:, j * width : (j + 1) * width])

    total = None
    upper(0)
    for j in range(steps):
        if j + 1 < steps:
            upper(j + 1)
        cols = slice(j * width, (j + 1) * width)

        def bend(r):
            value, rise = gelu_both(part[j % 2, r, :])
            active[j % 2, r, :] = value.astype(BF)
            slope[r, cols] = rise.astype(BF)

        chunked(size, bend)
        down = dot(active[j % 2], wd[cols, :])
        if j == 0:
            sum_ref[...] = down[:, :width]
            total = down[:, width:]
        else:
            sum_ref[...] += down[:, :width]
            total = total + down[:, width:]
    slope_done()
    inner_d = total.astype(BF)
    sum_ref[...] += dot(inner_d, bd_ref[...])

    def last(r):
        hat, rstd = norm_parts(hidden[r, :] + sum_ref[r, :])
        hidden[r, :] = hat * gain_ref[gain + 1 : gain + 2, :]
        hat2_ref[r, :] = hat.astype(BF)
        rstd2_ref[r, :] = jnp.broadcast_to(rstd, (CHUNK, 128))

    chunked(size, last)
    return inner_o, inner_u, inner_d


def first_layer_kernel(
    length_ref, rows_ref, pos_ref, gain_ref, wqkv_hbm, wo_hbm, wu_hbm, wd_hbm, ad_hbm, b_hbm, a_ref, bd_ref,
    high_ref, low_ref, qkv_hbm, log_hbm, attn_hbm, inner_ref, hat1_ref, rstd1_ref, slope_hbm, hat2_ref, rstd2_ref,
    wqkv, wo, wu, wd, hidden, x_ref, qkv, log_ref, attn, sum_ref, part, active, slope, score, prob, sems,
):
    size, width = rows_ref.shape
    wide = wu.shape[1]
    hbm = (wqkv_hbm, wo_hbm, wu_hbm, wd_hbm, ad_hbm, b_hbm)
    loads = weight_loads(hbm, width, sems, wqkv, wo, wu, wd)
    for name in ("qkv", "o", "up", "down"):
        start_all(loads[name])
    def embed(r):
        hat, _ = norm_parts(rows_ref[r, :].astype(F32) + pos_ref[r, :].astype(F32))
        value = hat * gain_ref[0:1, :]
        hidden[r, :] = value
        x_ref[r, :width] = value.astype(BF)

    chunked(size, embed)
    inner = dot(x_ref[:, :width], a_ref[...]).astype(BF)
    x_ref[:, width:] = inner
    wait_all(loads["qkv"])
    for i in range(3):
        cols = slice(i * width, (i + 1) * width)
        qkv[:, cols] = dot(x_ref[...], wqkv[:, cols]).astype(BF)
    store_qkv = pltpu.make_async_copy(qkv, qkv_hbm, sems.at[8])
    store_qkv.start()
    attend_kernel(
        size, length_ref[0], size,
        lambda c: qkv[:, c],
        lambda c: qkv[:, pl.ds(c.start + width, 128)],
        lambda c: qkv[:, pl.ds(c.start + 2 * width, 128)],
        attn, log_ref, score, prob,
    )
    store_log = pltpu.make_async_copy(log_ref, log_hbm, sems.at[9])
    store_log.start()
    store_attn = pltpu.make_async_copy(attn.at[:, :width], attn_hbm, sems.at[10])
    store_attn.start()
    store_slope = pltpu.make_async_copy(slope, slope_hbm, sems.at[11])
    inners = upper_kernel(
        size, width, wide, gain_ref, 1, hidden, attn, x_ref, sum_ref, part, active, slope, wo, wu, wd, a_ref, bd_ref,
        lambda name: wait_all(loads[name]), hat1_ref, rstd1_ref, hat2_ref, rstd2_ref, store_slope.start,
    )
    inner_ref[...] = merge_inner(inner, inners)

    def last(r):
        value = hidden[r, :]
        high = value.astype(BF)
        high_ref[r, :] = high
        low_ref[r, :] = (value - high.astype(F32)).astype(BF)

    chunked(size, last)
    store_qkv.wait()
    store_log.wait()
    store_attn.wait()
    store_slope.wait()


def first_layer(length, rows, positions, gains, weights):
    wqkv, wo, wu, wd, a_all, a_down, b_all = weights
    size, width = rows.shape
    wide = wu.shape[2]
    shapes = [
        ((size, width), BF), ((size, width), BF), ((size, 3 * width), BF), ((size, width), F32), ((size, width), BF),
        ((size, 128), BF), ((size, width), BF), ((size, 128), F32), ((size, wide), BF), ((size, width), BF),
        ((size, 128), F32),
    ]
    v, a = VMEM_SPEC, ANY_SPEC
    high, low, *saved = pl.pallas_call(
        first_layer_kernel,
        out_shape=[jax.ShapeDtypeStruct(*s) for s in shapes],
        in_specs=[SMEM_SPEC, v, v, v] + [a] * 6 + [v] * 2,
        out_specs=[v, v, a, a, a, v, v, v, a, v, v],
        scratch_shapes=[
            pltpu.VMEM((width + EXTRA, 3 * width), BF), pltpu.VMEM((width + EXTRA, width), BF),
            pltpu.VMEM((width + EXTRA, wide), BF), pltpu.VMEM((wide, width + EXTRA), BF),
            pltpu.VMEM((size, width), F32), pltpu.VMEM((size, width + EXTRA), BF),
            pltpu.VMEM((size, 3 * width), BF), pltpu.VMEM((size, width), F32),
            pltpu.VMEM((size, width + EXTRA), BF), pltpu.VMEM((size, width), F32),
            pltpu.VMEM((2, size, width), F32), pltpu.VMEM((2, size, width), BF), pltpu.VMEM((size, wide), BF),
            pltpu.VMEM((2, size, size), F32), pltpu.VMEM((2, size, size), BF),
            pltpu.SemaphoreType.DMA((12,)),
        ],
        compiler_params=PARAMS,
    )(length.reshape(1), rows, positions, gains, wqkv, wo, wu, wd, a_down, b_all, a_all[0],
      b_all[0, :, 4 * width : 5 * width])
    return (high, low), tuple(saved)


def upper_back_kernel(size, width, wide, inner_t, grad_at, gain_ref, gain, hat2_ref, rstd2_ref, slope, hat1_ref, rstd1_ref,
                      wo, wu, wd, a_ref, bd_ref, out_ref, waits, grad2, x_ref, sum_ref, part, active, grad1_at):
    def second(r):
        value = norm_back(grad_at(r) * gain_ref[gain + 1 : gain + 2, :], hat2_ref[r, :].astype(F32), rstd2_ref[r, 0:1])
        grad2[r, :] = value
        x_ref[r, :width] = value.astype(BF)

    chunked(size, second)
    low = x_ref[:, :width]
    x_ref[:, width:] = dot_nt(low, bd_ref[...]).astype(BF)
    out_ref[:, 4 * width : 5 * width] = ADAPTER_SCALE * dot(inner_t[32:48], low)[8:]
    waits("down")
    waits("up")
    steps = wide // width

    def inward(j):
        part[j % 2] = dot_nt(x_ref[...], wd[j * width : (j + 1) * width, :])

    total = None
    inward(0)
    for j in range(steps):
        if j + 1 < steps:
            inward(j + 1)
        cols = slice(j * width, (j + 1) * width)

        def bend(r):
            active[j % 2, r, :] = (part[j % 2, r, :] * slope[r, cols].astype(F32)).astype(BF)

        chunked(size, bend)
        piece = dot_nt(active[j % 2], wu[:, cols])
        out_ref[:, (5 + j) * width : (6 + j) * width] = (
            ADAPTER_SCALE * dot(inner_t[32:48], active[j % 2])[:8]
        )
        if j == 0:
            sum_ref[...] = piece[:, :width]
            total = piece[:, width:]
        else:
            sum_ref[...] += piece[:, :width]
            total = total + piece[:, width:]
    sum_ref[...] += dot_nt(total.astype(BF), a_ref[...])

    def first(r):
        value = norm_back(
            (grad2[r, :] + sum_ref[r, :]) * gain_ref[gain : gain + 1, :], hat1_ref[r, :].astype(F32), rstd1_ref[r, 0:1]
        )
        x_ref[r, :width] = value.astype(BF)
        if grad1_at is not None:
            grad1_at[r, :] = value

    chunked(size, first)
    low = x_ref[:, :width]
    waits("o")
    both = dot_nt(low, wo[...])
    out_ref[:, 3 * width : 4 * width] = ADAPTER_SCALE * dot(inner_t[16:32], low)[8:]
    return (both[:, :width] + dot_nt(both[:, width:].astype(BF), a_ref[...])).astype(BF)


def first_back_kernel(
    length_ref, grad_ref, gain_ref, qkv_hbm, log_hbm, attn_hbm, inner_ref, hat1_ref, rstd1_ref, slope_hbm, hat2_ref,
    rstd2_ref, wqkv_hbm, wo_hbm, wu_hbm, wd_hbm, ad_hbm, b_hbm, a_ref, bd_ref,
    out_ref,
    wo, wu, wd, qkv, log_ref, attn, slope, grad2, x_ref, sum_ref, part, active, d_attn, dq, dk, dv, score, dscore,
    prob, ds, sems,
):
    size, width = grad_ref.shape
    wide = wu.shape[1]
    hbm = (wqkv_hbm, wo_hbm, wu_hbm, wd_hbm, ad_hbm, b_hbm)
    loads = weight_loads(hbm, width, sems, None, wo, wu, wd)
    loads["down"].append(pltpu.make_async_copy(slope_hbm, slope, sems.at[6]))
    loads["qkv"] = [
        pltpu.make_async_copy(source, target, sems.at[7 + i])
        for i, (source, target) in enumerate([(qkv_hbm, qkv), (log_hbm, log_ref), (attn_hbm, attn)])
    ]
    for name in ("down", "up", "o", "qkv"):
        start_all(loads[name])
    inner_t = inner_ref[...].T
    d_attn[...] = upper_back_kernel(
        size, width, wide, inner_t, lambda r: grad_ref[r, :], gain_ref, 1, hat2_ref, rstd2_ref, slope, hat1_ref,
        rstd1_ref, wo, wu, wd, a_ref, bd_ref, out_ref, lambda name: wait_all(loads[name]), grad2, x_ref, sum_ref,
        part, active, None,
    )
    wait_all(loads["qkv"])
    attend_back_kernel(
        size, length_ref[0], size,
        lambda c: qkv[:, c],
        lambda c: qkv[:, pl.ds(c.start + width, 128)],
        lambda c: qkv[:, pl.ds(c.start + 2 * width, 128)],
        lambda c: attn[:, c],
        lambda c: d_attn[:, c],
        log_ref, dq, dk, dv, score, dscore, prob, ds,
    )
    for i, ref in enumerate((dq, dk, dv)):
        start = 8 * i // 16 * 16
        out_ref[:, i * width : (i + 1) * width] = (
            ADAPTER_SCALE * dot(inner_t[start : start + 16], ref[...])[8 * i - start : 8 * i - start + 8]
        )


def first_back(length, grad, saved, weights, gains):
    wqkv, wo, wu, wd, a_all, a_down, b_all = weights
    qkv, log_total, attn, inner, hat1, rstd1, slope, hat2, rstd2 = saved
    size, width = grad.shape
    wide = wu.shape[2]
    v, a = VMEM_SPEC, ANY_SPEC
    low = pltpu.VMEM((size, width), BF)
    full = pltpu.VMEM((size, width), F32)
    return pl.pallas_call(
        first_back_kernel,
        out_shape=jax.ShapeDtypeStruct((8, b_all.shape[2]), F32),
        in_specs=[SMEM_SPEC, v, v, a, a, a, v, v, v, a, v, v] + [a] * 6 + [v, v],
        out_specs=v,
        scratch_shapes=[
            pltpu.VMEM((width + EXTRA, width), BF), pltpu.VMEM((width + EXTRA, wide), BF),
            pltpu.VMEM((wide, width + EXTRA), BF),
            pltpu.VMEM(qkv.shape, BF), full, low, pltpu.VMEM((size, wide), BF),
            full, pltpu.VMEM((size, width + EXTRA), BF), full, pltpu.VMEM((2, size, width), F32),
            pltpu.VMEM((2, size, width), BF), low, low, low, low,
            pltpu.VMEM((2, size, size), F32), pltpu.VMEM((2, size, size), F32),
            pltpu.VMEM((2, size, size), BF), pltpu.VMEM((2, size, size), BF),
            pltpu.SemaphoreType.DMA((10,)),
        ],
        compiler_params=PARAMS,
    )(length.reshape(1), grad, gains, qkv, log_total, attn, inner, hat1, rstd1, slope, hat2, rstd2,
      wqkv, wo, wu, wd, a_down, b_all, a_all[0], b_all[0, :, 4 * width : 5 * width])


def last_layer_kernel(
    length_ref, pick_ref, high0_ref, low0_ref, high1_ref, low1_ref, gain_ref,
    wqkv_hbm, wo_hbm, wu_hbm, wd_hbm, ad_hbm, b_hbm, map_hbm, a_ref, bd_ref,
    final_ref, z_ref, head_hat_ref, head_rstd_ref, head_slope_ref,
    q_ref, kv_hbm, log_ref, attn_out_ref, inner_ref, inner_kv_ref, hat1_ref, rstd1_ref, slope, hat2_ref, rstd2_ref,
    wqkv, wo, wu, wd, map_ref, hidden, x_ref, x_kv, kv, attn, sum_ref, part, active, score, prob, sems,
):
    count = len_items = kv.shape[0]
    size, width = high0_ref.shape
    rows = hidden.shape[0]
    picks = rows // count
    wide = wu.shape[1]
    hbm = (wqkv_hbm, wo_hbm, wu_hbm, wd_hbm, ad_hbm, b_hbm)
    loads = weight_loads(hbm, width, sems, wqkv, wo, wu, wd, 1)
    loads["map"] = [pltpu.make_async_copy(map_hbm.at[0], map_ref, sems.at[8])]
    for name in ("qkv", "o", "up", "down", "map"):
        start_all(loads[name])
    highs, lows = (high0_ref, high1_ref), (low0_ref, low1_ref)
    for i in range(count):
        r = slice(i * picks, (i + 1) * picks)
        hot = (pick_ref[r, :] == lax.broadcasted_iota(jnp.int32, (1, size), 1)).astype(BF)
        x = dot(hot, highs[i][...])
        x_ref[r, :width] = x.astype(BF)
        hidden[r, :] = x + dot(hot, lows[i][...])
        inner_kv = dot(highs[i][...], a_ref[...]).astype(BF)
        inner_kv_ref[i] = inner_kv
        x_kv[i, :, :width] = highs[i][...]
        x_kv[i, :, width:] = inner_kv
    inner = dot(x_ref[:, :width], a_ref[...]).astype(BF)
    x_ref[:, width:] = inner
    wait_all(loads["qkv"])
    q_ref[...] = dot(x_ref[...], wqkv[:, :width]).astype(BF)
    for i in range(count):
        for j in range(2):
            kv[i, :, j * width : (j + 1) * width] = dot(
                x_kv[i], wqkv[:, (j + 1) * width : (j + 2) * width]
            ).astype(BF)
    store_kv = pltpu.make_async_copy(kv, kv_hbm, sems.at[9])
    store_kv.start()
    for i in range(count):
        r = slice(i * picks, (i + 1) * picks)
        attend_kernel(
            size, length_ref[i], picks,
            lambda c: q_ref[r, c],
            lambda c: kv[i, :, c],
            lambda c: kv[i, :, pl.ds(c.start + width, 128)],
            attn.at[r], log_ref.at[r], score, prob,
        )
    attn_out_ref[...] = attn[:, :width]
    inners = upper_kernel(
        rows, width, wide, gain_ref, 3, hidden, attn, x_ref, sum_ref, part, active, slope, wo, wu, wd, a_ref, bd_ref,
        lambda name: wait_all(loads[name]), hat1_ref, rstd1_ref, hat2_ref, rstd2_ref, lambda: None,
    )
    inner_ref[...] = merge_inner(inner, inners)
    final_ref[...] = hidden[...].astype(BF)
    wait_all(loads["map"])
    sum_ref[...] = dot(final_ref[...], map_ref[...])

    def head(r):
        value, rise = gelu_both(sum_ref[r, :])
        hat, rstd = norm_parts(value)
        head_slope_ref[r, :] = rise
        head_hat_ref[r, :] = hat
        head_rstd_ref[r, :] = jnp.broadcast_to(rstd, (CHUNK, 128))
        z_ref[r, :] = (hat * gain_ref[5:6, :]).astype(BF)

    chunked(rows, head)
    store_kv.wait()


def last_layer(lengths, picks, hidden, gains, weights, maps):
    wqkv, wo, wu, wd, a_all, a_down, b_all = weights
    (high0, low0), (high1, low1) = hidden
    size, width = high0.shape
    wide = wu.shape[2]
    count = 2
    rows = picks.shape[0]
    shapes = [
        ((rows, width), BF), ((rows, width), BF), ((rows, width), F32), ((rows, 128), F32), ((rows, width), F32),
        ((rows, width), BF), ((count, size, 2 * width), BF), ((rows, width), F32), ((rows, width), BF),
        ((rows, 128), BF), ((count, size, 128), BF), ((rows, width), BF), ((rows, 128), F32), ((rows, wide), BF),
        ((rows, width), BF), ((rows, 128), F32),
    ]
    v, a = VMEM_SPEC, ANY_SPEC
    final, *saved = pl.pallas_call(
        last_layer_kernel,
        out_shape=[jax.ShapeDtypeStruct(*s) for s in shapes],
        in_specs=[SMEM_SPEC] + [v] * 6 + [a] * 7 + [v] * 2,
        out_specs=[v] * 6 + [a] + [v] * 9,
        scratch_shapes=[
            pltpu.VMEM((width + EXTRA, 3 * width), BF), pltpu.VMEM((width + EXTRA, width), BF),
            pltpu.VMEM((width + EXTRA, wide), BF), pltpu.VMEM((wide, width + EXTRA), BF),
            pltpu.VMEM((width, width), BF),
            pltpu.VMEM((rows, width), F32), pltpu.VMEM((rows, width + EXTRA), BF),
            pltpu.VMEM((count, size, width + EXTRA), BF), pltpu.VMEM((count, size, 2 * width), BF),
            pltpu.VMEM((rows, width + EXTRA), BF), pltpu.VMEM((rows, width), F32),
            pltpu.VMEM((2, rows, width), F32), pltpu.VMEM((2, rows, width), BF),
            pltpu.VMEM((2, rows // count, size), F32), pltpu.VMEM((2, rows // count, size), BF),
            pltpu.SemaphoreType.DMA((10,)),
        ],
        compiler_params=PARAMS,
    )(lengths, picks, high0, low0, high1, low1, gains, wqkv, wo, wu, wd, a_down, b_all, maps, a_all[1],
      b_all[1, :, 4 * width : 5 * width])
    return final, tuple(saved[:4]), tuple(saved[4:])


def last_back_kernel(
    part_count, *refs
):
    last_back_run(refs[:part_count], *refs[part_count:])


def last_back_run(
    part_refs, length_ref, pick_ref, target_ref, live_ref, class_ref, gain_ref,
    z_ref, head_hat_ref, head_rstd_ref, head_slope_ref,
    q_ref, kv_hbm, log_ref, attn_ref, inner_ref, inner_kv_ref, hat1_ref, rstd1_ref, slope, hat2_ref, rstd2_ref,
    wqkv_hbm, wo_hbm, wu_hbm, wd_hbm, ad_hbm, b_hbm, map_hbm, a_ref, bd_ref,
    out0_ref, out1_ref, adapter_ref, loss_ref,
    wqkv, wo, wu, wd, map_ref, kv, grad, grad1, grad2, x_ref, sum_ref, part, active, d_attn, dq, dkv,
    score, dscore, prob, ds, sems,
):
    count, size, _ = kv.shape
    rows, width = grad.shape
    picks = rows // count
    wide = wu.shape[1]
    hbm = (wqkv_hbm, wo_hbm, wu_hbm, wd_hbm, ad_hbm, b_hbm)
    loads = weight_loads(hbm, width, sems, wqkv, wo, wu, wd, 1)
    loads["map"] = [pltpu.make_async_copy(map_hbm.at[0], map_ref, sems.at[8])]
    loads["kv"] = [pltpu.make_async_copy(kv_hbm, kv, sems.at[9])]
    for name in ("map", "down", "up", "o", "kv", "qkv"):
        start_all(loads[name])

    def head(r):
        live = live_ref[r, :]
        target = target_ref[r, :].astype(F32)
        logs = [jnp.sum(part_ref[r, width:].astype(F32), -1, keepdims=True) for part_ref in part_refs]
        top = functools.reduce(jnp.maximum, logs)
        shares = [jnp.exp(log - top) for log in logs]
        total = functools.reduce(jnp.add, shares)
        mean = functools.reduce(
            jnp.add, [part_ref[r, :width].astype(F32) * share for part_ref, share in zip(part_refs, shares)]
        )
        logit = jnp.sum(z_ref[r, :].astype(F32) * target, -1, keepdims=True)
        loss_ref[r, :] = jnp.broadcast_to(live * (top + jnp.log(total) - logit), (CHUNK, 128))
        grad_z = live * (mean / total - target)
        value = norm_back(grad_z * gain_ref[5:6, :], head_hat_ref[r, :], head_rstd_ref[r, 0:1])
        x_ref[r, :width] = (value * head_slope_ref[r, :]).astype(BF)

    chunked(rows, head)
    wait_all(loads["map"])
    grad[...] = dot_nt(x_ref[:, :width], map_ref[...]) + class_ref[...]
    inner_t = inner_ref[...].T
    d_attn[...] = upper_back_kernel(
        rows, width, wide, inner_t, lambda r: grad[r, :], gain_ref, 3, hat2_ref, rstd2_ref, slope, hat1_ref,
        rstd1_ref, wo, wu, wd, a_ref, bd_ref, adapter_ref, lambda name: wait_all(loads[name]), grad2, x_ref, sum_ref,
        part, active, grad1,
    )
    wait_all(loads["kv"])
    for i in range(count):
        r = slice(i * picks, (i + 1) * picks)
        attend_back_kernel(
            size, length_ref[i], picks,
            lambda c: q_ref[r, c],
            lambda c: kv[i, :, c],
            lambda c: kv[i, :, pl.ds(c.start + width, 128)],
            lambda c: attn_ref[r, c],
            lambda c: d_attn[r, c],
            log_ref.at[r], dq.at[r], dkv.at[i, :, :width], dkv.at[i, :, width:], score, dscore, prob, ds,
        )
    wait_all(loads["qkv"])
    both = dot_nt(dq[...], wqkv[:, :width])
    grad1[...] += both[:, :width] + dot_nt(both[:, width:].astype(BF), a_ref[...])
    adapter_ref[:, :width] = ADAPTER_SCALE * dot(inner_t[0:16], dq[...])[:8]
    total = None
    for i, out_ref in enumerate((out0_ref, out1_ref)):
        r = slice(i * picks, (i + 1) * picks)
        hot = (pick_ref[r, :] == lax.broadcasted_iota(jnp.int32, (1, size), 1)).astype(BF)
        value = grad1[r, :]
        high = value.astype(BF)
        low = (value - high.astype(F32)).astype(BF)
        both = dot_nt(dkv[i], wqkv[:, width:])
        out_ref[...] = (
            both[:, :width]
            + dot_nt(both[:, width:].astype(BF), a_ref[...])
            + dot_tn(jnp.concatenate([hot, hot], 0), jnp.concatenate([high, low], 0))
        )
        piece = dot(inner_kv_ref[i].T[0:32], dkv[i])
        total = piece if total is None else total + piece
    adapter_ref[:, width : 2 * width] = ADAPTER_SCALE * total[8:16, :width]
    adapter_ref[:, 2 * width : 3 * width] = ADAPTER_SCALE * total[16:24, width:]


def last_back(parts, lengths, picks, targets, live, class_grad, head, saved, gains, weights, maps):
    wqkv, wo, wu, wd, a_all, a_down, b_all = weights
    kv = saved[1]
    rows, width = targets.shape
    count, size, _ = kv.shape
    wide = wu.shape[2]
    v, a = VMEM_SPEC, ANY_SPEC
    low = pltpu.VMEM((rows, width), BF)
    full = pltpu.VMEM((rows, width), F32)
    return pl.pallas_call(
        functools.partial(last_back_kernel, len(parts)),
        out_shape=[
            jax.ShapeDtypeStruct((size, width), F32), jax.ShapeDtypeStruct((size, width), F32),
            jax.ShapeDtypeStruct((8, b_all.shape[2]), F32), jax.ShapeDtypeStruct((rows, 128), F32),
        ],
        in_specs=[v] * len(parts) + [SMEM_SPEC] + [v] * 10 + [a] + [v] * 9 + [a] * 7 + [v] * 2,
        out_specs=[v] * 4,
        scratch_shapes=[
            pltpu.VMEM((width + EXTRA, 3 * width), BF), pltpu.VMEM((width + EXTRA, width), BF),
            pltpu.VMEM((width + EXTRA, wide), BF), pltpu.VMEM((wide, width + EXTRA), BF),
            pltpu.VMEM((width, width), BF), pltpu.VMEM(kv.shape, BF),
            full, full, full, pltpu.VMEM((rows, width + EXTRA), BF), full, pltpu.VMEM((2, rows, width), F32),
            pltpu.VMEM((2, rows, width), BF), low, low, pltpu.VMEM(kv.shape, BF),
            pltpu.VMEM((2, size, rows // count), F32), pltpu.VMEM((2, size, rows // count), F32),
            pltpu.VMEM((2, size, rows // count), BF), pltpu.VMEM((2, size, rows // count), BF),
            pltpu.SemaphoreType.DMA((10,)),
        ],
        compiler_params=PARAMS,
    )(*parts, lengths, picks, targets, live, class_grad, gains, *head, *saved, wqkv, wo, wu, wd, a_down, b_all, maps,
      a_all[1], b_all[1, :, 4 * width : 5 * width])


def class_kernel(row_ref, final_ref, map_ref, projection_ref, grad_ref, out_ref):
    width = final_ref.shape[1]
    classes = 3
    label = row_ref[...]
    live = label >= 0
    pooled = jnp.tanh(dot(final_ref[...], map_ref[...]))
    logits = [
        jnp.sum(pooled * projection_ref[c : c + 1, :width], -1, keepdims=True)
        + projection_ref[c : c + 1, width : width + 1]
        for c in range(classes)
    ]
    top = functools.reduce(jnp.maximum, logits)
    exponents = [jnp.exp(x - top) for x in logits]
    total = functools.reduce(jnp.add, exponents)
    loss = top + jnp.log(total)
    pulled = 0.0
    outs = []
    for c in range(classes):
        hit = (label == c).astype(F32)
        loss = loss - logits[c] * hit
        grad = jnp.where(live, exponents[c] / total - hit, 0.0)
        pulled = pulled + grad * projection_ref[c : c + 1, :width]
        outs.append((jnp.sum(pooled * grad, 0, keepdims=True), jnp.sum(grad, 0, keepdims=True)))
    grad_ref[...] = dot_nt((pulled * (1.0 - pooled * pooled)).astype(BF), map_ref[...])
    out_ref[...] = jnp.zeros(out_ref.shape, F32)
    for c in range(classes):
        out_ref[c : c + 1, :width] = outs[c][0]
        out_ref[c : c + 1, width:] = jnp.broadcast_to(outs[c][1], (1, 128))
    out_ref[classes : classes + 1, width:] = jnp.broadcast_to(
        jnp.sum(jnp.where(live, loss, 0.0), 0, keepdims=True), (1, 128)
    )


def class_head(rows, final, maps, projection):
    width = final.shape[1]
    turned = jnp.pad(projection.T, ((0, 8 - projection.shape[1]), (0, EXTRA - 1)))
    return pl.pallas_call(
        class_kernel,
        out_shape=[jax.ShapeDtypeStruct(final.shape, F32), jax.ShapeDtypeStruct((8, width + EXTRA), F32)],
        in_specs=[VMEM_SPEC] * 4,
        out_specs=[VMEM_SPEC] * 2,
        compiler_params=PARAMS,
    )(rows, final, maps[1], turned)


BLOCK = 1024


def table_kernel(z_ref, table_hbm, out_ref, table, acc, score, prob, top, total, sems):
    rows = z_ref.shape[0]
    length = table.shape[0]
    blocks = length // BLOCK // 2 * 2
    tail = length - blocks * BLOCK
    loads = [
        pltpu.make_async_copy(
            table_hbm.at[pl.ds(i * BLOCK, BLOCK), :], table.at[pl.ds(i * BLOCK, BLOCK), :], sems.at[i]
        )
        for i in range(blocks)
    ]
    if tail:
        loads.append(
            pltpu.make_async_copy(
                table_hbm.at[pl.ds(blocks * BLOCK, tail), :], table.at[pl.ds(blocks * BLOCK, tail), :],
                sems.at[blocks],
            )
        )
    start_all(loads)
    top[...] = jnp.full(top.shape, NEG_FILL, F32)
    total[...] = jnp.zeros(total.shape, F32)
    acc[...] = jnp.zeros(acc.shape, F32)
    z = z_ref[...]

    def scores(start, size, slot):
        score[slot, :, :size] = dot_nt(z, table[pl.ds(start, size), :])

    def fold(start, size, slot):
        for first in range(0, rows, CHUNK):
            r = slice(first, first + CHUNK)
            value = score[slot, r, :size]
            before = top[r, :]
            now = jnp.maximum(before, jnp.max(value, -1, keepdims=True))
            exponent = jnp.exp(value - now[:, :1])
            prob[slot, r, :size] = exponent.astype(BF)
            shrink = jnp.exp(before - now)
            total[r, :] = total[r, :] * shrink + jnp.sum(exponent, -1, keepdims=True)
            top[r, :] = now
            acc[r, :] = acc[r, :] * shrink[:, :1]
        acc[...] += dot(prob[slot, :, :size], table[pl.ds(start, size), :])

    loads[0].wait()
    scores(0, BLOCK, 0)

    def two(i, carry):
        start = pl.multiple_of(i * 2 * BLOCK, BLOCK)
        wait_block(2 * i + 1)
        scores(start + BLOCK, BLOCK, 1)
        fold(start, BLOCK, 0)

        @pl.when(i + 1 < blocks // 2)
        def _():
            wait_block(2 * i + 2)

        scores(jnp.minimum(start + 2 * BLOCK, (blocks - 1) * BLOCK), BLOCK, 0)
        fold(start + BLOCK, BLOCK, 1)
        return carry

    def wait_block(i):
        pltpu.make_async_copy(
            table_hbm.at[pl.ds(0, BLOCK), :], table.at[pl.ds(0, BLOCK), :], sems.at[i]
        ).wait()

    lax.fori_loop(0, blocks // 2, two, 0)
    if tail:
        loads[-1].wait()
        scores(blocks * BLOCK, tail, 0)
        fold(blocks * BLOCK, tail, 0)
    width = z_ref.shape[1]
    out_ref[:, :width] = (acc[...] / total[:, :1]).astype(BF)
    out_ref[:, width:] = lanes_of(split_three(top[...] + jnp.log(total[...])))


def table_pass(z, table):
    rows, width = z.shape
    length = table.shape[0]
    widest = max(BLOCK, length - length // BLOCK // 2 * 2 * BLOCK)
    widest += -widest % 128
    return pl.pallas_call(
        table_kernel,
        out_shape=jax.ShapeDtypeStruct((rows, width + EXTRA), BF),
        in_specs=[VMEM_SPEC, ANY_SPEC],
        out_specs=VMEM_SPEC,
        scratch_shapes=[
            pltpu.VMEM((length, width), BF), pltpu.VMEM((rows, width), F32),
            pltpu.VMEM((2, rows, widest), F32), pltpu.VMEM((2, rows, widest), BF),
            pltpu.VMEM((rows, 128), F32), pltpu.VMEM((rows, 128), F32),
            pltpu.SemaphoreType.DMA((length // BLOCK + 1,)),
        ],
        compiler_params=PARAMS,
    )(z, table)


def moment_update(weight, grad, first, second):
    first_new = BETA_ONE * first + (1.0 - BETA_ONE) * grad
    second_new = BETA_TWO * second + (1.0 - BETA_TWO) * grad * grad
    fix_one = 1.0 - BETA_ONE**STEP
    fix_two = 1.0 - BETA_TWO**STEP
    step_size = first_new / fix_one / (jnp.sqrt(second_new / fix_two) + ADAM_EPS)
    return (weight - RATE * (step_size + DECAY * weight), first_new, second_new)


def after(value, *others):
    return lax.optimization_barrier((value,) + others)[0]


def merge_two(left, right):
    width = left.shape[-1] - EXTRA
    logs = [jnp.sum(x[..., width : width + 3].astype(F32), -1, keepdims=True) for x in (left, right)]
    top = jnp.maximum(logs[0], logs[1])
    shares = [jnp.exp(log - top) for log in logs]
    total = shares[0] + shares[1]
    mean = (left[..., :width].astype(F32) * shares[0] + right[..., :width].astype(F32) * shares[1]) / total
    log = top + jnp.log(total)
    high = lax.reduce_precision(log, 8, 7)
    middle = lax.reduce_precision(log - high, 8, 7)
    low = log - high - middle
    tail = jnp.pad(jnp.concatenate([high, middle, low], -1), [(0, 0)] * (left.ndim - 1) + [(0, EXTRA - 3)])
    return jnp.concatenate([mean.astype(BF), tail.astype(BF)], -1)


def reduce_all(flat):
    rows = flat.shape[0]
    body = jnp.pad(flat[:-1], ((0, -(rows - 1) % 32), (0, 0)))
    half = body.shape[0] // 2
    core = lax.axis_index("vocab") % 2
    keep = lax.dynamic_slice_in_dim(body, core * half, half)
    send = lax.dynamic_slice_in_dim(body, (1 - core) * half, half)
    exact = jnp.broadcast_to(flat[-1:], (8, 128))
    got = swap(jnp.concatenate([send, exact]), "vocab", 1)
    keep, exact = keep + got[:half], exact + got[half:]
    steps = [("vocab", 2 << i) for i in range((lax.axis_size("vocab") // 2).bit_length() - 1)]
    steps += [("dp", 1 << i) for i in range(lax.axis_size("dp").bit_length() - 1)]
    for axis, mask in steps:
        high = lax.reduce_precision(exact, 8, 7)
        middle = lax.reduce_precision(exact - high, 8, 7)
        mine = jnp.concatenate([lax.reduce_precision(keep, 8, 7), high, middle, exact - high - middle])
        other = swap(mine.astype(BF), axis, mask).astype(F32)
        keep = mine[:half] + other[:half]
        mine, other = mine[half:].reshape(3, 8, 128), other[half:].reshape(3, 8, 128)
        exact = (mine[0] + other[0]) + ((mine[1] + other[1]) + (mine[2] + other[2]))
    got = swap(keep, "vocab", 1)
    body = jnp.where(core == 0, jnp.concatenate([keep, got]), jnp.concatenate([got, keep]))
    return jnp.concatenate([body[: rows - 1], exact[:1]])


def body(
    input_token_ids,
    lengths,
    masked_positions,
    masked_token_targets,
    labels,
    token_embedding_table,
    position_table,
    norm_gain_table,
    query_key_value_weight,
    output_weight,
    up_weight,
    down_weight,
    adapter_inputs,
    adapter_down_input,
    head_dense_maps,
    adapter_outputs,
    class_projection,
    adapter_moment_first,
    adapter_moment_second,
    class_moment_first,
    class_moment_second,
):
    table_rows, width = token_embedding_table.shape
    seq_len = input_token_ids.shape[2]
    slots = masked_positions.shape[2]
    vocab_size = lax.axis_size("vocab")
    vocab_index = lax.axis_index("vocab")
    vocab_start = vocab_index * table_rows
    count = input_token_ids.shape[0] * input_token_ids.shape[1]
    picks = -(-(slots + 1) // 16) * 16
    rest = picks - slots

    own_lengths = lengths.reshape(count)
    own_labels = labels.reshape(count)
    own_positions = masked_positions.reshape(count, slots)
    packed = jnp.concatenate(
        [
            input_token_ids.reshape(count, seq_len),
            jnp.pad(masked_token_targets.reshape(count, slots), ((0, 0), (0, rest)), constant_values=-1),
        ],
        1,
    )
    items = lax.all_gather(packed, "vocab", axis=0)
    items = jnp.stack(
        [lax.dynamic_index_in_dim(items, vocab_index ^ mask, 0, keepdims=False) for mask in range(vocab_size)]
    )

    def lookup(ids):
        local = ids - vocab_start
        inside = (local >= 0) & (local < table_rows)
        rows = jnp.take(token_embedding_table, jnp.clip(local, 0, table_rows - 1), axis=0)
        rows = jnp.where(inside[..., None], rows, jnp.zeros((), BF))
        rows = rows.reshape((vocab_size // 2, 2) + rows.shape[1:])
        return rows[:, 0], swap(rows[:, 1], "vocab", 1)

    def spread(pair):
        own = pair[0] + pair[1]
        return [own[0]] + [swap(own[mask], "vocab", 2 * mask) for mask in range(1, vocab_size // 2)]

    def add(parts):
        return functools.reduce(jnp.add, parts)

    a_all, a_down, b_all = adapter_tables(adapter_inputs, adapter_down_input, adapter_outputs)
    weights = (query_key_value_weight, output_weight, up_weight, down_weight, a_all, a_down, b_all)
    half = seq_len // 2
    piece0 = lookup(items[:, 0, :half])
    piece1 = lookup(after(items[:, 0, half:seq_len], piece0[0]))
    parts0 = spread(piece0)
    parts1 = spread(piece1)
    piece2 = lookup(after(items[:, 1, :seq_len], parts0[0], piece1[0]))
    parts2 = spread(piece2)
    rows0 = jnp.concatenate([add(parts0), add(parts1)])
    out0, saved_first = first_layer(
        own_lengths[0], after(rows0, parts2[0]), position_table, norm_gain_table, weights
    )
    rows1 = add(parts2)
    out1, saved_second = first_layer(
        own_lengths[1], after(rows1, out0[0]), position_table, norm_gain_table, weights
    )
    hidden, saved0 = [out0, out1], [saved_first, saved_second]
    pick_index = jnp.concatenate(
        [own_positions, jnp.zeros((count, 1), jnp.int32), jnp.full((count, rest - 1), -1, jnp.int32)], 1
    ).reshape(-1, 1)
    final, head, saved1 = last_layer(own_lengths, pick_index, hidden, norm_gain_table, weights, head_dense_maps)

    z = head[0]
    far = jnp.stack([z] + [swap(z, "vocab", 2 * mask) for mask in range(1, vocab_size // 2)])
    target_piece = lookup(after(items[:, :, seq_len:], z).reshape(vocab_size, -1))
    label_rows = jnp.where(jnp.arange(picks)[None, :] == slots, own_labels[:, None], -1).reshape(-1, 1)
    class_grad, class_out = class_head(label_rows, final, head_dense_maps, class_projection)
    z_all = jnp.stack([far, swap(far, "vocab", 1)], 1).reshape(-1, width)
    target_rows = add(spread(target_piece))
    summed = table_pass(z_all, token_embedding_table)
    own_slots = count * picks
    summed = summed.reshape(vocab_size // 2, 2, own_slots, width + EXTRA)
    merged = merge_two(summed[:, 0], swap(summed[:, 1], "vocab", 1))
    parts = [merged[0]] + [swap(merged[mask], "vocab", 2 * mask) for mask in range(1, vocab_size // 2)]
    live = jnp.arange(picks)[None, :] < own_lengths[:, None] * 15 // 100
    live = (live & (jnp.arange(picks)[None, :] < slots)).reshape(-1)

    classes = class_projection.shape[1]
    grad0, grad1, grads1, losses = last_back(
        parts, own_lengths, pick_index, target_rows, live.astype(F32)[:, None], class_grad, head, saved1, norm_gain_table,
        weights, head_dense_maps,
    )
    grads0 = 0.0
    for i, grad in enumerate((grad0, grad1)):
        grads0 = grads0 + first_back(own_lengths[i], grad, saved0[i], weights, norm_gain_table)
    grad_head = class_out[:classes, : width + 1].T
    terms = (jnp.sum(live.astype(jnp.int32)) + count).astype(F32)
    flat = jnp.concatenate([grads0.reshape(-1), grads1.reshape(-1), grad_head.reshape(-1)])
    size = flat.shape[0]
    flat = jnp.pad(flat, (0, -size % 128)).reshape(-1, 128)
    sum_stats = jnp.stack([jnp.sum(losses[:, 0]) + class_out[classes, width], terms])
    flat = reduce_all(jnp.concatenate([flat, jnp.pad(sum_stats, (0, 126))[None]]))
    sum_stats = flat[-1, :2]
    flat = flat[:-1].reshape(-1)
    split = adapter_outputs.size
    adapter_grad = flat[:split].reshape(adapter_outputs.shape) / sum_stats[1]
    grad_head = flat[split:size].reshape(class_projection.shape) / sum_stats[1]
    overall_norm = jnp.sqrt(jnp.sum(adapter_grad * adapter_grad) + jnp.sum(grad_head * grad_head))
    multiplier = CLIP_AT / jnp.maximum(overall_norm, CLIP_AT)
    adapter_new = moment_update(
        adapter_outputs, adapter_grad * multiplier, adapter_moment_first, adapter_moment_second
    )
    class_new = moment_update(
        class_projection, grad_head * multiplier, class_moment_first, class_moment_second
    )
    return (sum_stats, overall_norm.reshape(1)) + adapter_new + class_new


def solution(mesh):
    split = P(None, ("dp", "vocab"), None)
    placed = (split, P(None, ("dp", "vocab")), split, split, P(None, ("dp", "vocab")), P("vocab", None)) + (P(),) * 15
    return jax.shard_map(body, mesh=mesh, in_specs=placed, out_specs=(P(),) * 8, check_vma=False)
```

```python
import functools

import jax
import jax.numpy as jnp
from jax import lax
from jax.experimental import pallas as pl
from jax.experimental.pallas import tpu as pltpu
from jax.sharding import PartitionSpec as P

HDIM = 64
STEP = 10
NORM_EPS = 1e-05
ADAPTER_SCALE = 2.0
NEG_FILL = -1e30
CLIP_AT = 0.001
RATE = 0.03
BETA_ONE = 0.9
BETA_TWO = 0.999
ADAM_EPS = 1e-08
DECAY = 0.01
BF = jnp.bfloat16
F32 = jnp.float32


def dot(left, right):
    return jnp.dot(left, right, preferred_element_type=F32)


def dot_nt(left, right):
    return lax.dot_general(left, right, (((1,), (1,)), ((), ())), preferred_element_type=F32)


def dot_tn(left, right):
    return lax.dot_general(left, right, (((0,), (0,)), ((), ())), preferred_element_type=F32)


def norm_parts(values):
    center = values - jnp.mean(values, -1, keepdims=True)
    spread = jnp.mean(center * center, -1, keepdims=True)
    rstd = lax.rsqrt(spread + NORM_EPS)
    return center * rstd, rstd


def norm_back(grad_hat, hat, rstd):
    first = jnp.mean(grad_hat, -1, keepdims=True)
    second = jnp.mean(grad_hat * hat, -1, keepdims=True)
    return rstd * (grad_hat - first - hat * second)


def gelu_both(values):
    root = 0.7978845608028654
    square = values * values
    bend = jnp.tanh(root * values * (1.0 + 0.044715 * square))
    half = 0.5 * (1.0 + bend)
    slope = half + 0.5 * values * (1.0 - bend * bend) * root * (1.0 + 0.134145 * square)
    return values * half, slope


def high_low(values):
    high = lax.reduce_precision(values, 8, 7)
    return high.astype(BF), (values - high).astype(BF)


def swap(value, axis, mask):
    size = lax.axis_size(axis)
    return lax.ppermute(value, axis, [(i, i ^ mask) for i in range(size)])


def adapter_tables(adapter_inputs, adapter_down_input, adapter_outputs):
    layers, width, columns = adapter_inputs.shape
    rank = adapter_down_input.shape[2]
    total = adapter_outputs.shape[2]
    one = jnp.pad(adapter_inputs, ((0, 0), (0, 0), (0, 64 - columns)))
    a_all = jnp.concatenate([one, one], 2)
    one = jnp.pad(adapter_down_input, ((0, 0), (0, 0), (columns, 64 - columns - rank)))
    a_down = jnp.concatenate([one, one], 2)
    high = lax.reduce_precision(ADAPTER_SCALE * adapter_outputs, 8, 7)
    both = jnp.stack([high, ADAPTER_SCALE * adapter_outputs - high], 1)
    column = jnp.arange(total) // width
    group = jnp.where(column < 4, column, jnp.where(column == 4, 5, 4))
    keep = jnp.arange(8)[:, None] == group[None, :]
    b_all = jnp.where(keep[None, None, :, None, :], both[:, :, None, :, :], 0.0)
    return a_all, a_down, b_all.reshape(layers, 128, total).astype(BF)


def moment_update(weight, grad, first, second):
    first_new = BETA_ONE * first + (1.0 - BETA_ONE) * grad
    second_new = BETA_TWO * second + (1.0 - BETA_TWO) * grad * grad
    fix_one = 1.0 - BETA_ONE**STEP
    fix_two = 1.0 - BETA_TWO**STEP
    step_size = first_new / fix_one / (jnp.sqrt(second_new / fix_two) + ADAM_EPS)
    return (weight - RATE * (step_size + DECAY * weight), first_new, second_new)


VMEM_SPEC = pl.BlockSpec(memory_space=pltpu.VMEM)
SMEM_SPEC = pl.BlockSpec(memory_space=pltpu.SMEM)
ANY_SPEC = pl.BlockSpec(memory_space=pl.ANY)
PARAMS = pltpu.CompilerParams(vmem_limit_bytes=63 * 2**20)
CHUNK = 16
EXTRA = 128


def chunked(rows, body, step=CHUNK):
    for start in range(0, rows, step):
        body(slice(start, start + step))


def lane_half():
    return lax.broadcasted_iota(jnp.int32, (1, 128), 1) < HDIM


def split_three(values):
    high = values.astype(BF)
    rest = values - high.astype(F32)
    middle = rest.astype(BF)
    return high, middle, (rest - middle.astype(F32)).astype(BF)


def lanes_of(parts):
    lane = lax.broadcasted_iota(jnp.int32, (1, 128), 1) % HDIM
    out = jnp.zeros((), BF)
    for i, part in reversed(list(enumerate(parts))):
        out = jnp.where(lane == i, part, out)
    return out


def key_extra(size, length):
    one = jnp.ones((), BF)
    mask = jnp.where(lax.broadcasted_iota(jnp.int32, (size, 1), 0) < length, 0.0, NEG_FILL)
    return lanes_of([one, one, one, jnp.broadcast_to(mask, (size, 128)).astype(BF)])


def attend_kernel(size, length, queries, q_at, k_at, v_at, out_ref, log_ref, score_ref, prob_ref):
    bias = jnp.where(lax.broadcasted_iota(jnp.int32, (1, size), 1) < length, 0.0, NEG_FILL)
    left = lane_half()
    lane = lax.broadcasted_iota(jnp.int32, (1, 128), 1)
    log_ref[...] = jnp.zeros(log_ref.shape, BF)

    def pair(p, carry):
        cols = pl.ds(pl.multiple_of(p * 128, 128), 128)
        q = q_at(cols) * 0.125
        k_t = k_at(cols).T
        v = v_at(cols)
        zero, one = jnp.zeros((), BF), jnp.ones((), BF)
        outs, tops = [], []
        for half in range(2):
            own = left if half == 0 else ~left
            score_ref[half] = dot(jnp.where(own, q, zero), k_t)
        for half in range(2):
            own = left if half == 0 else ~left
            top = []
            for start in range(0, queries, CHUNK):
                rows = slice(start, start + CHUNK)
                score = score_ref[half, rows, :] + bias
                highest = jnp.max(score, -1, keepdims=True)
                prob_ref[half, rows, :] = jnp.exp(score - highest).astype(BF)
                top.append(highest)
            outs.append(dot(prob_ref[half], jnp.where(own, v, one)))
            tops.append(jnp.concatenate(top, 0))
        total = pltpu.roll(jnp.where(left, outs[1], outs[0]), HDIM, 1)
        out_ref[:, cols] = (jnp.where(left, outs[0], outs[1]) / total).astype(BF)
        log = jnp.where(left, tops[0], tops[1]) + jnp.log(total)
        packed = log_ref[...]
        for half, value in enumerate((log, pltpu.roll(log, HDIM, 1))):
            for i, piece in enumerate(split_three(value)):
                packed = jnp.where(lane == 6 * p + 3 * half + i, piece, packed)
        log_ref[...] = packed
        return carry

    lax.fori_loop(0, out_ref.shape[1] // 128, pair, 0)


def attend_back_kernel(size, length, queries, q_at, k_at, v_at, o_at, g_at, log_ref, dq_ref, dk_ref, dv_ref,
                       score_ref, grad_ref, prob_ref, ds_ref):
    left = lane_half()
    k_extra = key_extra(size, length)
    one = jnp.ones((), BF)
    v_extra = lanes_of([one, one, one])
    lane = lax.broadcasted_iota(jnp.int32, (1, 128), 1)
    row = lax.broadcasted_iota(jnp.int32, (128, 128), 0)
    col = lax.broadcasted_iota(jnp.int32, (128, 128), 1)
    across = jnp.where(
        (lax.broadcasted_iota(jnp.int32, (128, 128), 0) < HDIM) != left, 1.0, 0.0
    ).astype(BF)

    def pair(p, carry):
        cols = pl.ds(pl.multiple_of(p * 128, 128), 128)
        q = q_at(cols) * 0.125
        k, v, g = k_at(cols), v_at(cols), g_at(cols)
        place = jnp.where(
            (col < 3) & (row == 6 * p + 3 + col) | (col >= HDIM) & (col < HDIM + 3) & (row == 6 * p + col - HDIM),
            -1.0,
            0.0,
        ).astype(BF)
        q_extra = jnp.where(lane % HDIM == 3, one, dot(log_ref[...], place).astype(BF))
        product = g.astype(F32) * o_at(cols).astype(F32)
        high = product.astype(BF)
        low = (product - high.astype(F32)).astype(BF)
        g_extra = lanes_of([-x for x in split_three(dot(high, across) + dot(low, across))])
        for half in range(2):
            own = left if half == 0 else ~left
            score_ref[half, :, :queries] = dot_nt(jnp.where(own, k, k_extra), jnp.where(own, q, q_extra))
            grad_ref[half, :, :queries] = dot_nt(jnp.where(own, v, v_extra), jnp.where(own, g, g_extra))
        d_q, d_k, d_v = [], [], []
        for half in range(2):
            for start in range(0, size, CHUNK):
                rows = slice(start, start + CHUNK)
                prob = jnp.exp(score_ref[half, rows, :queries])
                prob_ref[half, rows, :queries] = prob.astype(BF)
                ds_ref[half, rows, :queries] = (prob * grad_ref[half, rows, :queries]).astype(BF)
            d_scores = ds_ref[half, :, :queries]
            d_v.append(dot(prob_ref[half, :, :queries], g))
            d_k.append(dot(d_scores, q))
            d_q.append(dot_tn(d_scores, k))
        dq_ref[:, cols] = (jnp.where(left, d_q[0], d_q[1]) * 0.125).astype(BF)
        dk_ref[:, cols] = jnp.where(left, d_k[0], d_k[1]).astype(BF)
        dv_ref[:, cols] = jnp.where(left, d_v[0], d_v[1]).astype(BF)
        return carry

    lax.fori_loop(0, dq_ref.shape[1] // 128, pair, 0)


def weight_loads(hbm, width, sems, wqkv, wo, wu, wd, layer=0):
    wqkv_hbm, wo_hbm, wu_hbm, wd_hbm, ad_hbm, b_hbm = hbm
    pieces = {}
    if wqkv is not None:
        pieces["qkv"] = 0, [
            (wqkv_hbm.at[layer], wqkv.at[:width, :]),
            (b_hbm.at[layer, :, pl.ds(0, 3 * width)], wqkv.at[width:, :]),
        ]
    pieces["o"] = 2, [
        (wo_hbm.at[layer], wo.at[:width, :]),
        (b_hbm.at[layer, :, pl.ds(3 * width, width)], wo.at[width:, :]),
    ]
    pieces["down"] = 4, [
        (wd_hbm.at[layer], wd.at[:, :width]),
        (ad_hbm.at[layer], wd.at[:, width:]),
    ]
    pieces["up"] = 6, [
        (wu_hbm.at[layer], wu.at[:width, :]),
        (b_hbm.at[layer, :, pl.ds(5 * width, wu.shape[1])], wu.at[width:, :]),
    ]
    return {
        name: [
            pltpu.make_async_copy(source, target, sems.at[first + n]) for n, (source, target) in enumerate(copies)
        ]
        for name, (first, copies) in pieces.items()
    }


def start_all(loads):
    for load in loads:
        load.start()


def wait_all(loads):
    for load in loads:
        load.wait()


def merge_inner(inner, inners):
    lane = lax.broadcasted_iota(jnp.int32, (1, 128), 1) % 64 // 8
    return jnp.where(
        lane < 3, inner, jnp.where(lane == 3, inners[0], jnp.where(lane == 4, inners[1], inners[2]))
    )


def upper_kernel(size, width, wide, gain_ref, gain, hidden, attn, x_ref, sum_ref, part, active, slope, wo, wu, wd,
                 a_ref, bd_ref, waits, hat1_ref, rstd1_ref, rstd2_ref, slope_done):
    inner_o = dot(attn[:, :width], a_ref[...]).astype(BF)
    attn[:, width:] = inner_o
    waits("o")
    sum_ref[...] = dot(attn[...], wo[...])

    def middle(r):
        hat, rstd = norm_parts(hidden[r, :] + sum_ref[r, :])
        value = hat * gain_ref[gain : gain + 1, :]
        hidden[r, :] = value
        x_ref[r, :width] = value.astype(BF)
        hat1_ref[r, :] = hat.astype(BF)
        rstd1_ref[r, :] = jnp.broadcast_to(rstd, (CHUNK, 128))

    chunked(size, middle)
    inner_u = dot(x_ref[:, :width], a_ref[...]).astype(BF)
    x_ref[:, width:] = inner_u
    waits("up")
    waits("down")
    steps = wide // width

    def upper(j):
        part[j % 2] = dot(x_ref[...], wu[:, j * width : (j + 1) * width])

    total = None
    upper(0)
    for j in range(steps):
        if j + 1 < steps:
            upper(j + 1)
        cols = slice(j * width, (j + 1) * width)

        def bend(r):
            value, rise = gelu_both(part[j % 2, r, :])
            active[j % 2, r, :] = value.astype(BF)
            slope[r, cols] = rise.astype(BF)

        chunked(size, bend)
        down = dot(active[j % 2], wd[cols, :])
        if j == 0:
            sum_ref[...] = down[:, :width]
            total = down[:, width:]
        else:
            sum_ref[...] += down[:, :width]
            total = total + down[:, width:]
    slope_done()
    inner_d = total.astype(BF)
    sum_ref[...] += dot(inner_d, bd_ref[...])

    def last(r):
        hat, rstd = norm_parts(hidden[r, :] + sum_ref[r, :])
        hidden[r, :] = hat * gain_ref[gain + 1 : gain + 2, :]
        rstd2_ref[r, :] = jnp.broadcast_to(rstd, (CHUNK, 128))

    chunked(size, last)
    return inner_o, inner_u, inner_d


def first_run(
    length, rows_ref, pos_ref, gain_ref, loads, freed, a_ref, bd_ref, qkv_done, attn_done, slope_done,
    log_ref, inner_ref, hat1_ref, rstd1_ref, rstd2_ref,
    wqkv, wo, wu, wd, hidden, x_ref, qkv, attn, sum_ref, part, active, slope, score, prob,
):
    size, width = rows_ref.shape
    wide = wu.shape[1]

    def embed(r):
        hat, _ = norm_parts(rows_ref[r, :].astype(F32) + pos_ref[r, :].astype(F32))
        value = hat * gain_ref[0:1, :]
        hidden[r, :] = value
        x_ref[r, :width] = value.astype(BF)

    chunked(size, embed)
    inner = dot(x_ref[:, :width], a_ref[...]).astype(BF)
    x_ref[:, width:] = inner
    wait_all(loads["qkv"])
    for i in range(3):
        cols = slice(i * width, (i + 1) * width)
        qkv[:, cols] = dot(x_ref[...], wqkv[:, cols]).astype(BF)
    freed("qkv")
    qkv_done()
    attend_kernel(
        size, length, size,
        lambda c: qkv[:, c],
        lambda c: qkv[:, pl.ds(c.start + width, 128)],
        lambda c: qkv[:, pl.ds(c.start + 2 * width, 128)],
        attn.at[:, pl.ds(0, width)], log_ref, score, prob,
    )
    attn_done()
    inners = upper_kernel(
        size, width, wide, gain_ref, 1, hidden, attn, x_ref, sum_ref, part, active, slope, wo, wu, wd, a_ref, bd_ref,
        lambda name: wait_all(loads[name]), hat1_ref, rstd1_ref, rstd2_ref, slope_done,
    )
    for name in ("o", "up", "down"):
        freed(name)
    inner_ref[...] = merge_inner(inner, inners)


def pick_rows(pick_ref, r, hidden, high_ref, size):
    lows = []
    for start in range(0, size, 128):
        s = slice(start, start + 128)
        value = hidden[s, :]
        high = value.astype(BF)
        high_ref[s, :] = high
        lows.append((value - high.astype(F32)).astype(BF))
    hot = (pick_ref[r, :] == lax.broadcasted_iota(jnp.int32, (1, size), 1)).astype(BF)
    return dot(hot, high_ref[...]) + dot(hot, jnp.concatenate(lows, 0))


def first_layer_kernel(
    length_ref, pick_ref, rows_ref, pos_ref, gain_ref, wqkv_hbm, wo_hbm, wu_hbm, wd_hbm, ad_hbm, b_hbm, a_ref, bd_ref,
    picked_ref, high_ref, qkv_hbm, log_ref, attn_hbm, inner_ref, hat1_ref, rstd1_ref, slope_hbm, rstd2_ref,
    wqkv, wo, wu, wd, hidden, x_ref, qkv, attn, sum_ref, part, active, slope, score, prob, sems,
):
    size, width = rows_ref.shape
    hbm = (wqkv_hbm, wo_hbm, wu_hbm, wd_hbm, ad_hbm, b_hbm)
    loads = weight_loads(hbm, width, sems, wqkv, wo, wu, wd)
    for name in ("qkv", "o", "up", "down"):
        start_all(loads[name])
    stores = [
        pltpu.make_async_copy(qkv, qkv_hbm, sems.at[8]),
        pltpu.make_async_copy(attn.at[:, pl.ds(0, width)], attn_hbm, sems.at[9]),
        pltpu.make_async_copy(slope, slope_hbm, sems.at[10]),
    ]
    first_run(
        length_ref[0], rows_ref, pos_ref, gain_ref, loads, lambda name: None, a_ref, bd_ref, stores[0].start,
        stores[1].start, stores[2].start, log_ref, inner_ref, hat1_ref, rstd1_ref, rstd2_ref,
        wqkv, wo, wu, wd, hidden, x_ref, qkv, attn, sum_ref, part, active, slope, score, prob,
    )
    picked_ref[...] = pick_rows(pick_ref, slice(0, picked_ref.shape[0]), hidden, high_ref, size)
    wait_all(stores)


def saved_shapes(size, width, wide):
    return [
        ((size, width), BF), ((size, 3 * width), BF), ((size, 128), BF), ((size, width), BF),
        ((size, 128), BF), ((size, width), BF), ((size, 128), F32), ((size, wide), BF), ((size, 128), F32),
    ]


def saved_specs():
    v, a = VMEM_SPEC, ANY_SPEC
    return [v, a, v, a, v, v, v, a, v]


def first_scratch(size, width, wide):
    return [
        pltpu.VMEM((width + EXTRA, 3 * width), BF), pltpu.VMEM((width + EXTRA, width), BF),
        pltpu.VMEM((width + EXTRA, wide), BF), pltpu.VMEM((wide, width + EXTRA), BF),
        pltpu.VMEM((size, width), F32), pltpu.VMEM((size, width + EXTRA), BF),
        pltpu.VMEM((size, 3 * width), BF),
        pltpu.VMEM((size, width + EXTRA), BF), pltpu.VMEM((size, width), F32),
        pltpu.VMEM((2, size, width), F32), pltpu.VMEM((2, size, width), BF), pltpu.VMEM((size, wide), BF),
        pltpu.VMEM((2, size, size), F32), pltpu.VMEM((2, size, size), BF),
    ]


def first_layer(length, picks, rows, positions, gains, weights):
    wqkv, wo, wu, wd, a_all, a_down, b_all = weights
    size, width = rows.shape
    wide = wu.shape[2]
    shapes = [((picks.shape[0], width), F32)] + saved_shapes(size, width, wide)
    v, a = VMEM_SPEC, ANY_SPEC
    picked, *saved = pl.pallas_call(
        first_layer_kernel,
        out_shape=[jax.ShapeDtypeStruct(*s) for s in shapes],
        in_specs=[SMEM_SPEC, v, v, v, v] + [a] * 6 + [v] * 2,
        out_specs=[v] + saved_specs(),
        scratch_shapes=first_scratch(size, width, wide) + [pltpu.SemaphoreType.DMA((11,))],
        compiler_params=PARAMS,
    )(length.reshape(1), picks, rows, positions, gains, wqkv, wo, wu, wd, a_down, b_all, a_all[0],
      b_all[0, :, 4 * width : 5 * width])
    return picked, tuple(saved)


def upper_back_kernel(size, width, wide, inner_t, grad_at, gain_ref, gain, high_ref, rstd2_ref, slope, hat1_ref, rstd1_ref,
                      wo, wu, wd, a_ref, bd_ref, out_ref, waits, grad2, x_ref, sum_ref, part, active, grad1_at, more=False):
    def second(r):
        scale = gain_ref[gain + 1 : gain + 2, :]
        value = norm_back(grad_at(r) * scale, high_ref[r, :].astype(F32) * (1.0 / scale), rstd2_ref[r, 0:1])
        grad2[r, :] = value
        x_ref[r, :width] = value.astype(BF)

    def put(cols, value):
        out_ref[:, cols] = out_ref[:, cols] + value if more else value

    chunked(size, second)
    low = x_ref[:, :width]
    x_ref[:, width:] = dot_nt(low, bd_ref[...]).astype(BF)
    put(slice(4 * width, 5 * width), ADAPTER_SCALE * dot(inner_t[32:48], low)[8:])
    waits("down")
    waits("up")
    steps = wide // width

    def inward(j):
        part[j % 2] = dot_nt(x_ref[...], wd[j * width : (j + 1) * width, :])

    total = None
    inward(0)
    for j in range(steps):
        if j + 1 < steps:
            inward(j + 1)
        cols = slice(j * width, (j + 1) * width)

        def bend(r):
            active[j % 2, r, :] = (part[j % 2, r, :] * slope[r, cols].astype(F32)).astype(BF)

        chunked(size, bend)
        piece = dot_nt(active[j % 2], wu[:, cols])
        put(slice((5 + j) * width, (6 + j) * width), ADAPTER_SCALE * dot(inner_t[32:48], active[j % 2])[:8])
        if j == 0:
            sum_ref[...] = piece[:, :width]
            total = piece[:, width:]
        else:
            sum_ref[...] += piece[:, :width]
            total = total + piece[:, width:]
    sum_ref[...] += dot_nt(total.astype(BF), a_ref[...])

    def first(r):
        value = norm_back(
            (grad2[r, :] + sum_ref[r, :]) * gain_ref[gain : gain + 1, :], hat1_ref[r, :].astype(F32), rstd1_ref[r, 0:1]
        )
        x_ref[r, :width] = value.astype(BF)
        if grad1_at is not None:
            grad1_at[r, :] = value

    chunked(size, first)
    low = x_ref[:, :width]
    waits("o")
    both = dot_nt(low, wo[...])
    put(slice(3 * width, 4 * width), ADAPTER_SCALE * dot(inner_t[16:32], low)[8:])
    return (both[:, :width] + dot_nt(both[:, width:].astype(BF), a_ref[...])).astype(BF)


def two_layers_kernel(
    length_ref, pick_ref, rows_ref, pos_ref, picked0_ref, high0_ref, gain_ref,
    wqkv_hbm, wo_hbm, wu_hbm, wd_hbm, ad_hbm, b_hbm, map_hbm, a0_ref, bd0_ref, a1_ref, bd1_ref,
    high1_ref, qkv_hbm, log_ref, attn_hbm, inner_ref, hat1_ref, rstd1_ref, slope_hbm, rstd2_ref,
    final_ref, z_ref, head_hat_ref, head_rstd_ref, head_slope_ref,
    q_ref, kv_hbm, top_log_ref, attn_out_ref, top_inner_ref, inner_kv_ref, top_hat1_ref, top_rstd1_ref, top_slope,
    top_rstd2_ref,
    wqkv, wo, wu, wd, hidden, x_ref, qkv, attn, sum_ref, part, active, slope, score, prob, map_ref, x_kv, kv, sems,
):
    count = kv.shape[0]
    size, width = rows_ref.shape
    rows = final_ref.shape[0]
    picks = rows // count
    wide = wu.shape[1]
    hbm = (wqkv_hbm, wo_hbm, wu_hbm, wd_hbm, ad_hbm, b_hbm)
    loads = weight_loads(hbm, width, sems, wqkv, wo, wu, wd)
    later = weight_loads(hbm, width, sems, wqkv, wo, wu, wd, 1)
    load_map = pltpu.make_async_copy(map_hbm.at[0], map_ref, sems.at[8])
    for name in ("qkv", "o", "up", "down"):
        start_all(loads[name])
    load_map.start()
    stores = [
        pltpu.make_async_copy(qkv, qkv_hbm, sems.at[9]),
        pltpu.make_async_copy(attn.at[:, pl.ds(0, width)], attn_hbm, sems.at[10]),
        pltpu.make_async_copy(slope, slope_hbm, sems.at[11]),
        pltpu.make_async_copy(kv, kv_hbm, sems.at[12]),
    ]
    first_run(
        length_ref[1], rows_ref, pos_ref, gain_ref, loads, lambda name: start_all(later[name]), a0_ref, bd0_ref,
        stores[0].start, stores[1].start, stores[2].start, log_ref, inner_ref, hat1_ref, rstd1_ref, rstd2_ref,
        wqkv, wo, wu, wd, hidden, x_ref, qkv, attn, sum_ref, part, active, slope, score, prob,
    )
    picked = [picked0_ref[...], pick_rows(pick_ref, slice(picks, rows), hidden, high1_ref, size)]
    stores[1].wait()
    top_hidden, top_x, top_attn = hidden.at[pl.ds(0, rows)], x_ref.at[pl.ds(0, rows)], attn.at[pl.ds(0, rows)]
    top_sum = sum_ref.at[pl.ds(0, rows)]
    for i, high_ref in enumerate((high0_ref, high1_ref)):
        r = slice(i * picks, (i + 1) * picks)
        hidden[r, :] = picked[i]
        x_ref[r, :width] = picked[i].astype(BF)
        x_kv[i, :, :width] = high_ref[...]
        inner_kv = dot(high_ref[...], a1_ref[...]).astype(BF)
        inner_kv_ref[i] = inner_kv
        x_kv[i, :, width:] = inner_kv
    inner = dot(top_x[:, :width], a1_ref[...]).astype(BF)
    x_ref[:rows, width:] = inner
    wait_all(later["qkv"])
    q_ref[...] = dot(top_x[...], wqkv[:, :width]).astype(BF)
    for i in range(count):
        for j in range(2):
            kv[i, :, j * width : (j + 1) * width] = dot(
                x_kv[i], wqkv[:, (j + 1) * width : (j + 2) * width]
            ).astype(BF)
    stores[3].start()
    for i in range(count):
        r = slice(i * picks, (i + 1) * picks)
        attend_kernel(
            size, length_ref[i], picks,
            lambda c: q_ref[r, c],
            lambda c: kv[i, :, c],
            lambda c: kv[i, :, pl.ds(c.start + width, 128)],
            attn.at[pl.ds(i * picks, picks), pl.ds(0, width)], top_log_ref.at[pl.ds(i * picks, picks)],
            score.at[:, pl.ds(0, picks)], prob.at[:, pl.ds(0, picks)],
        )
    attn_out_ref[...] = attn[:rows, :width]
    inners = upper_kernel(
        rows, width, wide, gain_ref, 3, top_hidden, top_attn, top_x, top_sum, part.at[:, pl.ds(0, rows)],
        active.at[:, pl.ds(0, rows)], top_slope, wo, wu, wd, a1_ref, bd1_ref, lambda name: wait_all(later[name]),
        top_hat1_ref, top_rstd1_ref, top_rstd2_ref, lambda: None,
    )
    top_inner_ref[...] = merge_inner(inner, inners)
    final_ref[...] = hidden[:rows, :].astype(BF)
    load_map.wait()
    sum_ref[:rows, :] = dot(final_ref[...], map_ref[...])

    def head(r):
        value, rise = gelu_both(sum_ref[r, :])
        hat, rstd = norm_parts(value)
        head_slope_ref[r, :] = rise
        head_hat_ref[r, :] = hat
        head_rstd_ref[r, :] = jnp.broadcast_to(rstd, (CHUNK, 128))
        z_ref[r, :] = (hat * gain_ref[5:6, :]).astype(BF)

    chunked(rows, head)
    stores[0].wait()
    stores[2].wait()
    stores[3].wait()


def two_layers(lengths, picks, rows, positions, first, gains, weights, maps):
    wqkv, wo, wu, wd, a_all, a_down, b_all = weights
    picked0, high0 = first
    size, width = rows.shape
    wide = wu.shape[2]
    count = 2
    total = picks.shape[0]
    shapes = saved_shapes(size, width, wide) + [
        ((total, width), BF), ((total, width), BF), ((total, width), F32), ((total, 128), F32), ((total, width), F32),
        ((total, width), BF), ((count, size, 2 * width), BF), ((total, 128), BF), ((total, width), BF),
        ((total, 128), BF), ((count, size, 128), BF), ((total, width), BF), ((total, 128), F32), ((total, wide), BF),
        ((total, 128), F32),
    ]
    v, a = VMEM_SPEC, ANY_SPEC
    bd = b_all[:, :, 4 * width : 5 * width]
    out = pl.pallas_call(
        two_layers_kernel,
        out_shape=[jax.ShapeDtypeStruct(*s) for s in shapes],
        in_specs=[SMEM_SPEC] + [v] * 6 + [a] * 7 + [v] * 4,
        out_specs=saved_specs() + [v] * 6 + [a] + [v] * 8,
        scratch_shapes=first_scratch(size, width, wide) + [
            pltpu.VMEM((width, width), BF), pltpu.VMEM((count, size, width + EXTRA), BF),
            pltpu.VMEM((count, size, 2 * width), BF), pltpu.SemaphoreType.DMA((13,)),
        ],
        compiler_params=PARAMS,
    )(lengths, picks, rows, positions, picked0, high0, gains, wqkv, wo, wu, wd, a_down, b_all, maps, a_all[0], bd[0],
      a_all[1], bd[1])
    return tuple(out[:9]), out[9], tuple(out[10:14]), tuple(out[14:])


def backward_kernel(part_count, *refs):
    backward_run(refs[:part_count], *refs[part_count:])


def backward_run(
    part_refs, length_ref, pick_ref, target_ref, live_ref, class_ref, class_out_ref, gain_ref,
    z_ref, head_hat_ref, head_rstd_ref, head_slope_ref, final_ref,
    q_ref, kv_hbm, log_ref, attn_ref, inner_ref, inner_kv_ref, hat1_ref, rstd1_ref, slope, rstd2_ref,
    high0_hbm, qkv0_hbm, log0_hbm, attn0_hbm, inner0_hbm, hat0_hbm, rstd0_hbm, slope0_hbm, rrstd0_hbm,
    high1_hbm, qkv1_hbm, log1_hbm, attn1_hbm, inner1_hbm, hat1_hbm, rstd1_hbm, slope1_hbm, rrstd1_hbm,
    wqkv_hbm, wo_hbm, wu_hbm, wd_hbm, ad_hbm, b_hbm, map_hbm, a0_ref, bd0_ref, a1_ref, bd1_ref,
    adapter0_ref, adapter1_ref, term_ref,
    wqkv, wo, wu, wd, kv, grads, grad1, grad2, x_ref, sum_ref, part, active, d_attn, dq, dkv,
    score, dscore, prob, ds, s_high, s_log, s_attn, s_inner, s_hat1, s_rstd1, s_slope, s_rstd2, sems,
):
    count, size, _ = kv.shape
    rows, width = z_ref.shape
    picks = rows // count
    wide = wu.shape[1]
    hbm = (wqkv_hbm, wo_hbm, wu_hbm, wd_hbm, ad_hbm, b_hbm)
    loads = weight_loads(hbm, width, sems, wqkv, wo, wu, wd, 1)
    lower = weight_loads(hbm, width, sems, None, wo, wu, wd, 0)
    map_ref = wqkv.at[pl.ds(0, width), pl.ds(0, width)]
    loads["map"] = [pltpu.make_async_copy(map_hbm.at[0], map_ref, sems.at[8])]
    loads["kv"] = [pltpu.make_async_copy(kv_hbm, kv, sems.at[9])]
    kept = (s_high, None, s_log, s_attn, s_inner, s_hat1, s_rstd1, s_slope, s_rstd2)
    items = []
    for source_refs in (
        (high0_hbm, qkv0_hbm, log0_hbm, attn0_hbm, inner0_hbm, hat0_hbm, rstd0_hbm, slope0_hbm, rrstd0_hbm),
        (high1_hbm, qkv1_hbm, log1_hbm, attn1_hbm, inner1_hbm, hat1_hbm, rstd1_hbm, slope1_hbm, rrstd1_hbm),
    ):
        copies = [
            pltpu.make_async_copy(source, target, sems.at[10 + n])
            for n, (source, target) in enumerate(zip(source_refs, kept))
            if target is not None
        ]
        qkv_hbm = source_refs[1]
        copies.append(pltpu.make_async_copy(qkv_hbm.at[:, pl.ds(0, 2 * width)], kv.at[0], sems.at[11]))
        copies.append(
            pltpu.make_async_copy(
                qkv_hbm.at[:, pl.ds(2 * width, width)], kv.at[1, :, pl.ds(0, width)], sems.at[19]
            )
        )
        items.append(copies)
    early, late = (0, 3, 4, 5, 6, 7), (1, 2, 8, 9)
    for name in ("map", "down", "up", "o", "kv"):
        start_all(loads[name])
    for n in early:
        items[0][n].start()
    part_rows = pl.ds(0, rows)

    def head(r):
        live = live_ref[r, :]
        target = target_ref[r, :].astype(F32)
        mean, log_total = mean_of(part_refs, r, width)
        logit = jnp.sum(z_ref[r, :].astype(F32) * target, -1, keepdims=True)
        losses.append(jnp.sum(live * (log_total - logit), 0, keepdims=True))
        lives.append(jnp.sum(live, 0, keepdims=True))
        grad_z = live * (mean - target)
        value = norm_back(grad_z * gain_ref[5:6, :], head_hat_ref[r, :], head_rstd_ref[r, 0:1])
        x_ref[r, :width] = (value * head_slope_ref[r, :]).astype(BF)

    losses, lives = [class_out_ref[3:4, width : width + 1]], [jnp.full((1, 1), count, F32)]
    chunked(rows, head)
    lane = lax.broadcasted_iota(jnp.int32, (8, 128), 1)
    term_ref[...] = jnp.where(lane == 0, functools.reduce(jnp.add, losses), functools.reduce(jnp.add, lives))
    wait_all(loads["map"])
    sum_ref[:rows, :] = dot_nt(x_ref[:rows, :width], map_ref[...]) + class_ref[...]
    start_all(loads["qkv"])
    grads[0, :rows, :] = sum_ref[:rows, :]
    inner_t = inner_ref[...].T
    d_attn[:rows, :] = upper_back_kernel(
        rows, width, wide, inner_t, lambda r: grads[0, r, :], gain_ref, 3, final_ref, rstd2_ref, slope, hat1_ref,
        rstd1_ref, wo, wu, wd, a1_ref, bd1_ref, adapter1_ref, lambda name: wait_all(loads[name]),
        grad2.at[part_rows], x_ref.at[part_rows], sum_ref.at[part_rows], part.at[:, part_rows],
        active.at[:, part_rows], grad1,
    )
    for name in ("down", "up", "o"):
        start_all(lower[name])
    wait_all(loads["kv"])
    for i in range(count):
        r = slice(i * picks, (i + 1) * picks)
        view = pl.ds(i * picks, picks)
        attend_back_kernel(
            size, length_ref[i], picks,
            lambda c: q_ref[r, c],
            lambda c: kv[i, :, c],
            lambda c: kv[i, :, pl.ds(c.start + width, 128)],
            lambda c: attn_ref[r, c],
            lambda c: d_attn[r, c],
            log_ref.at[view], dq.at[view], dkv.at[i, :, pl.ds(0, width)], dkv.at[i, :, pl.ds(width, width)],
            score, dscore, prob, ds,
        )
    for n in late:
        items[0][n].start()
    wait_all(loads["qkv"])
    both = dot_nt(dq[:rows, :], wqkv[:, :width])
    grad1[...] += both[:, :width] + dot_nt(both[:, width:].astype(BF), a1_ref[...])
    adapter1_ref[:, :width] = ADAPTER_SCALE * dot(inner_t[0:16], dq[:rows, :])[:8]
    total = None
    for i in range(count):
        r = slice(i * picks, (i + 1) * picks)
        hot = (pick_ref[r, :] == lax.broadcasted_iota(jnp.int32, (1, size), 1)).astype(BF)
        value = grad1[r, :]
        high = value.astype(BF)
        low = (value - high.astype(F32)).astype(BF)
        both = dot_nt(dkv[i], wqkv[:, width:])
        grads[i] = (
            both[:, :width]
            + dot_nt(both[:, width:].astype(BF), a1_ref[...])
            + dot_tn(jnp.concatenate([hot, hot], 0), jnp.concatenate([high, low], 0))
        )
        piece = dot(inner_kv_ref[i].T[0:32], dkv[i])
        total = piece if total is None else total + piece
    adapter1_ref[:, width : 2 * width] = ADAPTER_SCALE * total[8:16, :width]
    adapter1_ref[:, 2 * width : 3 * width] = ADAPTER_SCALE * total[16:24, width:]

    for i in range(count):
        for n in early:
            items[i][n].wait()
        inner_t = s_inner[...].T
        d_attn[...] = upper_back_kernel(
            size, width, wide, inner_t, lambda r: grads[i, r, :], gain_ref, 1, s_high, s_rstd2, s_slope, s_hat1,
            s_rstd1, wo, wu, wd, a0_ref, bd0_ref, adapter0_ref,
            lambda name: wait_all(lower[name]) if i == 0 else None, grad2, x_ref, sum_ref, part, active, None, i > 0,
        )
        if i + 1 < count:
            for n in early:
                items[i + 1][n].start()
        for n in late:
            items[i][n].wait()
        attend_back_kernel(
            size, length_ref[i], size,
            lambda c: kv[0, :, c],
            lambda c: kv[0, :, pl.ds(c.start + width, 128)],
            lambda c: kv[1, :, c],
            lambda c: s_attn[:, c],
            lambda c: d_attn[:, c],
            s_log, dq, dkv.at[0, :, pl.ds(0, width)], dkv.at[0, :, pl.ds(width, width)], score, dscore, prob, ds,
        )
        if i + 1 < count:
            for n in late:
                items[i + 1][n].start()
        for j, value in enumerate((dq[...], dkv[0, :, :width], dkv[0, :, width:])):
            start = 8 * j // 16 * 16
            cols = slice(j * width, (j + 1) * width)
            piece = ADAPTER_SCALE * dot(inner_t[start : start + 16], value)[8 * j - start : 8 * j - start + 8]
            adapter0_ref[:, cols] = piece if i == 0 else adapter0_ref[:, cols] + piece


def backward(parts, lengths, picks, targets, live, class_grad, class_out, head, final, top, saved, gains, weights, maps):
    wqkv, wo, wu, wd, a_all, a_down, b_all = weights
    kv = top[1]
    rows, width = targets.shape
    count, size, _ = kv.shape
    wide = wu.shape[2]
    v, a = VMEM_SPEC, ANY_SPEC
    low = pltpu.VMEM((size, width), BF)
    full = pltpu.VMEM((size, width), F32)
    bd = b_all[:, :, 4 * width : 5 * width]
    return pl.pallas_call(
        functools.partial(backward_kernel, len(parts)),
        out_shape=[jax.ShapeDtypeStruct((8, b_all.shape[2]), F32)] * 2 + [jax.ShapeDtypeStruct((8, 128), F32)],
        in_specs=[v] * len(parts) + [SMEM_SPEC] + [v] * 12 + [a] + [v] * 8 + [a] * 18 + [a] * 7 + [v] * 4,
        out_specs=[v] * 3,
        scratch_shapes=[
            pltpu.VMEM((width + EXTRA, 3 * width), BF), pltpu.VMEM((width + EXTRA, width), BF),
            pltpu.VMEM((width + EXTRA, wide), BF), pltpu.VMEM((wide, width + EXTRA), BF),
            pltpu.VMEM(kv.shape, BF),
            pltpu.VMEM((count, size, width), F32), pltpu.VMEM((rows, width), F32), full,
            pltpu.VMEM((size, width + EXTRA), BF), full, pltpu.VMEM((2, size, width), F32),
            pltpu.VMEM((2, size, width), BF), low, low, pltpu.VMEM(kv.shape, BF),
            pltpu.VMEM((2, size, size), F32), pltpu.VMEM((2, size, size), F32),
            pltpu.VMEM((2, size, size), BF), pltpu.VMEM((2, size, size), BF),
        ] + [pltpu.VMEM(*s) for n, s in enumerate(saved_shapes(size, width, wide)) if n != 1] + [
            pltpu.SemaphoreType.DMA((20,))
        ],
        compiler_params=PARAMS,
    )(*parts, lengths, picks, targets, live, class_grad, class_out, gains, *head, final, *top, *saved[0], *saved[1],
      wqkv, wo, wu, wd, a_down, b_all, maps, a_all[0], bd[0], a_all[1], bd[1])


def class_kernel(row_ref, final_ref, map_ref, projection_ref, grad_ref, out_ref):
    width = final_ref.shape[1]
    classes = 3
    label = row_ref[...]
    live = label >= 0
    pooled = jnp.tanh(dot(final_ref[...], map_ref[...]))
    logits = [
        jnp.sum(pooled * projection_ref[c : c + 1, :width], -1, keepdims=True)
        + projection_ref[c : c + 1, width : width + 1]
        for c in range(classes)
    ]
    top = functools.reduce(jnp.maximum, logits)
    exponents = [jnp.exp(x - top) for x in logits]
    total = functools.reduce(jnp.add, exponents)
    loss = top + jnp.log(total)
    pulled = 0.0
    outs = []
    for c in range(classes):
        hit = (label == c).astype(F32)
        loss = loss - logits[c] * hit
        grad = jnp.where(live, exponents[c] / total - hit, 0.0)
        pulled = pulled + grad * projection_ref[c : c + 1, :width]
        outs.append((jnp.sum(pooled * grad, 0, keepdims=True), jnp.sum(grad, 0, keepdims=True)))
    grad_ref[...] = dot_nt((pulled * (1.0 - pooled * pooled)).astype(BF), map_ref[...])
    out_ref[...] = jnp.zeros(out_ref.shape, F32)
    for c in range(classes):
        out_ref[c : c + 1, :width] = outs[c][0]
        out_ref[c : c + 1, width:] = jnp.broadcast_to(outs[c][1], (1, 128))
    out_ref[classes : classes + 1, width:] = jnp.broadcast_to(
        jnp.sum(jnp.where(live, loss, 0.0), 0, keepdims=True), (1, 128)
    )


def class_head(rows, final, maps, projection):
    width = final.shape[1]
    turned = jnp.pad(projection.T, ((0, 8 - projection.shape[1]), (0, EXTRA - 1)))
    return pl.pallas_call(
        class_kernel,
        out_shape=[jax.ShapeDtypeStruct(final.shape, F32), jax.ShapeDtypeStruct((8, width + EXTRA), F32)],
        in_specs=[VMEM_SPEC] * 4,
        out_specs=[VMEM_SPEC] * 2,
        compiler_params=PARAMS,
    )(rows, final, maps[1], turned)


BLOCK = 1024


def table_kernel(near_ref, far_ref, table_hbm, near_out, far_out, z_ref, table, acc, score, prob, top, total, sems):
    rows, width = z_ref.shape
    half = rows // 2
    length = table.shape[0]
    blocks = length // BLOCK // 2 * 2
    tail = length - blocks * BLOCK
    loads = [
        pltpu.make_async_copy(
            table_hbm.at[pl.ds(i * BLOCK, BLOCK), :], table.at[pl.ds(i * BLOCK, BLOCK), :], sems.at[i]
        )
        for i in range(blocks)
    ]
    if tail:
        loads.append(
            pltpu.make_async_copy(
                table_hbm.at[pl.ds(blocks * BLOCK, tail), :], table.at[pl.ds(blocks * BLOCK, tail), :],
                sems.at[blocks],
            )
        )
    start_all(loads)
    top[...] = jnp.full(top.shape, NEG_FILL, F32)
    total[...] = jnp.zeros(total.shape, F32)
    acc[...] = jnp.zeros(acc.shape, F32)
    z_ref[:half, :] = near_ref[...]
    z_ref[half:, :] = far_ref[...]

    def scores(start, size, slot):
        score[slot, :, :size] = dot_nt(z_ref[...], table[pl.ds(start, size), :])

    def fold(start, size, slot):
        for first in range(0, rows, CHUNK):
            r = slice(first, first + CHUNK)
            value = score[slot, r, :size]
            before = top[r, :]
            now = jnp.maximum(before, jnp.max(value, -1, keepdims=True))
            exponent = jnp.exp(value - now[:, :1])
            prob[slot, r, :size] = exponent.astype(BF)
            shrink = jnp.exp(before - now)
            total[r, :] = total[r, :] * shrink + jnp.sum(exponent, -1, keepdims=True)
            top[r, :] = now
            acc[r, :] = acc[r, :] * shrink[:, :1]
        acc[...] += dot(prob[slot, :, :size], table[pl.ds(start, size), :])

    loads[0].wait()
    scores(0, BLOCK, 0)

    def two(i, carry):
        start = pl.multiple_of(i * 2 * BLOCK, BLOCK)
        wait_block(2 * i + 1)
        scores(start + BLOCK, BLOCK, 1)
        fold(start, BLOCK, 0)

        @pl.when(i + 1 < blocks // 2)
        def _():
            wait_block(2 * i + 2)

        scores(jnp.minimum(start + 2 * BLOCK, (blocks - 1) * BLOCK), BLOCK, 0)
        fold(start + BLOCK, BLOCK, 1)
        return carry

    def wait_block(i):
        pltpu.make_async_copy(
            table_hbm.at[pl.ds(0, BLOCK), :], table.at[pl.ds(0, BLOCK), :], sems.at[i]
        ).wait()

    lax.fori_loop(0, blocks // 2, two, 0)
    if tail:
        loads[-1].wait()
        scores(blocks * BLOCK, tail, 0)
        fold(blocks * BLOCK, tail, 0)
    for out_ref, r in ((near_out, slice(0, half)), (far_out, slice(half, rows))):
        out_ref[:, :width] = (acc[r, :] / total[r, :1]).astype(BF)
        out_ref[:, width:] = lanes_of(split_three(top[r, :] + jnp.log(total[r, :])))


def table_pass(near, far, table):
    half, width = near.shape
    rows = 2 * half
    length = table.shape[0]
    widest = max(BLOCK, length - length // BLOCK // 2 * 2 * BLOCK)
    widest += -widest % 128
    return pl.pallas_call(
        table_kernel,
        out_shape=[jax.ShapeDtypeStruct((half, width + EXTRA), BF)] * 2,
        in_specs=[VMEM_SPEC, VMEM_SPEC, ANY_SPEC],
        out_specs=[VMEM_SPEC] * 2,
        scratch_shapes=[
            pltpu.VMEM((rows, width), BF), pltpu.VMEM((length, width), BF), pltpu.VMEM((rows, width), F32),
            pltpu.VMEM((2, rows, widest), F32), pltpu.VMEM((2, rows, widest), BF),
            pltpu.VMEM((rows, 128), F32), pltpu.VMEM((rows, 128), F32),
            pltpu.SemaphoreType.DMA((length // BLOCK + 1,)),
        ],
        compiler_params=PARAMS,
    )(near, far, table)


def mean_of(part_refs, r, width):
    logs = [
        jnp.sum(part_ref[r, width : width + HDIM].astype(F32), -1, keepdims=True) for part_ref in part_refs
    ]
    top = functools.reduce(jnp.maximum, logs)
    shares = [jnp.exp(log - top) for log in logs]
    total = functools.reduce(jnp.add, shares)
    mean = functools.reduce(
        jnp.add, [part_ref[r, :width].astype(F32) * share for part_ref, share in zip(part_refs, shares)]
    )
    return mean / total, top + jnp.log(total)


def merge_kernel(left_ref, right_ref, *out_refs):
    rows, columns = out_refs[0].shape
    width = columns - EXTRA
    for i, out_ref in enumerate(out_refs):
        for start in range(0, rows, CHUNK):
            r = slice(start, start + CHUNK)
            mean, log = mean_of((left_ref, right_ref), slice(i * rows + start, i * rows + start + CHUNK), width)
            out_ref[r, :width] = mean.astype(BF)
            out_ref[r, width:] = lanes_of(split_three(jnp.broadcast_to(log, (CHUNK, EXTRA))))


def merge(left, right, count):
    rows, columns = left.shape
    return pl.pallas_call(
        merge_kernel,
        out_shape=[jax.ShapeDtypeStruct((rows // count, columns), BF)] * count,
        in_specs=[VMEM_SPEC] * 2,
        out_specs=[VMEM_SPEC] * count,
        compiler_params=PARAMS,
    )(left, right)


def update_kernel(core_ref, keep_ref, got_ref, term_ref, w_ref, m_ref, s_ref, cw_ref, cm_ref, cs_ref,
                  sum_ref, norm_ref, wo_ref, mo_ref, so_ref, cwo_ref, cmo_ref, cso_ref, grads):
    total = w_ref.shape[2]
    classes, rows = cw_ref.shape
    count = term_ref[0:1, 1:2]
    first = core_ref[0] == 0
    step = rows - 1
    square = 0.0
    for start in range(0, total, step):
        cols = slice(start, start + step)
        keep, got = keep_ref[:, cols] / count, got_ref[:, cols] / count
        square = square + (keep * keep + got * got)
        grads[0, :, cols] = jnp.where(first, keep, got)
        grads[1, :, cols] = jnp.where(first, got, keep)
    head = jnp.where(first, keep_ref[:, total:], got_ref[:, total:]) / count
    inside = (lax.broadcasted_iota(jnp.int32, head.shape, 0) < classes) & (
        lax.broadcasted_iota(jnp.int32, head.shape, 1) < rows
    )
    head = jnp.where(inside, head, 0.0)
    norm = jnp.sqrt(
        jnp.sum(jnp.sum(square, 1, keepdims=True), 0, keepdims=True)
        + jnp.sum(jnp.sum(head * head, 1, keepdims=True), 0, keepdims=True)
    )
    multiplier = CLIP_AT / jnp.maximum(norm, CLIP_AT)
    sum_ref[0] = term_ref[0, 0]
    sum_ref[1] = term_ref[0, 1]
    norm_ref[0] = norm[0, 0]
    for layer in range(2):
        for start in range(0, total, step):
            at = (layer, slice(None), slice(start, start + step))
            wo_ref[at], mo_ref[at], so_ref[at] = moment_update(
                w_ref[at], grads[at] * multiplier, m_ref[at], s_ref[at]
            )
    turned = (head * multiplier)[:classes, :rows]
    cwo_ref[...], cmo_ref[...], cso_ref[...] = moment_update(cw_ref[...], turned, cm_ref[...], cs_ref[...])


def update(core, keep, got, terms, trained, classes):
    classes = [x.T for x in classes]
    v = VMEM_SPEC
    shape = jax.ShapeDtypeStruct(trained[0].shape, F32)
    class_shape = jax.ShapeDtypeStruct(classes[0].shape, F32)
    *out, first, second, third = pl.pallas_call(
        update_kernel,
        out_shape=[jax.ShapeDtypeStruct((2,), F32), jax.ShapeDtypeStruct((1,), F32)] + [shape] * 3 + [class_shape] * 3,
        in_specs=[SMEM_SPEC] + [v] * 9,
        out_specs=[SMEM_SPEC] * 2 + [v] * 6,
        scratch_shapes=[pltpu.VMEM(trained[0].shape, F32)],
        compiler_params=PARAMS,
    )(core, keep, got, terms, *trained, *classes)
    return tuple(out) + (first.T, second.T, third.T)


def after(value, *others):
    return lax.optimization_barrier((value,) + others)[0]


def reduce_all(layers, terms):
    width = layers[0].shape[1]
    core = lax.axis_index("vocab") % 2
    keep = jnp.where(core == 0, layers[0], layers[1])
    send = jnp.where(core == 0, layers[1], layers[0])
    got = swap(jnp.concatenate([send, terms], 1), "vocab", 1)
    keep, terms = keep + got[:, :width], terms + got[:, width:]
    steps = [("vocab", 2 << i) for i in range((lax.axis_size("vocab") // 2).bit_length() - 1)]
    steps += [("dp", 1 << i) for i in range(lax.axis_size("dp").bit_length() - 1)]
    for axis, mask in steps:
        high = lax.reduce_precision(terms, 8, 7)
        middle = lax.reduce_precision(terms - high, 8, 7)
        mine = jnp.concatenate([lax.reduce_precision(keep, 8, 7), high, middle, terms - high - middle], 1)
        other = swap(mine.astype(BF), axis, mask).astype(F32)
        both = mine + other
        keep = both[:, :width]
        terms = both[:, width : width + 128] + (both[:, width + 128 : width + 256] + both[:, width + 256 :])
    return core, keep, swap(keep, "vocab", 1), terms


def body(
    input_token_ids,
    lengths,
    masked_positions,
    masked_token_targets,
    labels,
    token_embedding_table,
    position_table,
    norm_gain_table,
    query_key_value_weight,
    output_weight,
    up_weight,
    down_weight,
    adapter_inputs,
    adapter_down_input,
    head_dense_maps,
    adapter_outputs,
    class_projection,
    adapter_moment_first,
    adapter_moment_second,
    class_moment_first,
    class_moment_second,
):
    table_rows, width = token_embedding_table.shape
    seq_len = input_token_ids.shape[2]
    slots = masked_positions.shape[2]
    vocab_size = lax.axis_size("vocab")
    vocab_index = lax.axis_index("vocab")
    vocab_start = vocab_index * table_rows
    count = input_token_ids.shape[0] * input_token_ids.shape[1]
    picks = -(-(slots + 1) // 16) * 16
    rest = picks - slots

    own_lengths = lengths.reshape(count)
    own_labels = labels.reshape(count)
    own_positions = masked_positions.reshape(count, slots)
    packed = jnp.concatenate(
        [
            input_token_ids.reshape(count, seq_len),
            jnp.pad(masked_token_targets.reshape(count, slots), ((0, 0), (0, rest)), constant_values=-1),
        ],
        1,
    )
    items = lax.all_gather(packed, "vocab", axis=0)
    items = jnp.stack(
        [lax.dynamic_index_in_dim(items, vocab_index ^ mask, 0, keepdims=False) for mask in range(vocab_size)]
    )

    def own_rows(ids):
        local = ids - vocab_start
        inside = (local >= 0) & (local < table_rows)
        rows = jnp.take(token_embedding_table, jnp.clip(local, 0, table_rows - 1), axis=0)
        return jnp.where(inside[..., None], rows, jnp.zeros((), BF))

    def core_sum(rows):
        rows = rows.reshape((vocab_size // 2, 2) + rows.shape[1:])
        sent = swap(rows[:, 1], "vocab", 1)
        return [rows[mask, 0] + sent[mask] for mask in range(vocab_size // 2)]

    def gather_pair(ids):
        return core_sum(own_rows(ids))

    def spread(own):
        return [own[0]] + [swap(own[mask], "vocab", 2 * mask) for mask in range(1, vocab_size // 2)]

    def add(parts):
        return functools.reduce(jnp.add, parts)

    a_all, a_down, b_all = adapter_tables(adapter_inputs, adapter_down_input, adapter_outputs)
    weights = (query_key_value_weight, output_weight, up_weight, down_weight, a_all, a_down, b_all)
    pick_index = jnp.concatenate(
        [own_positions, jnp.zeros((count, 1), jnp.int32), jnp.full((count, rest - 1), -1, jnp.int32)], 1
    ).reshape(-1, 1)
    own0 = gather_pair(items[:, 0, :seq_len])
    second = after(items[:, 1], own0[1:], weights[4:], pick_index)
    second = jnp.concatenate([second, items[:, 0, seq_len:]], 1)

    def exchange(own, ids):
        return spread(own), own_rows(ids)

    parts0, own1 = lax.cond(
        own_lengths[0] > 0, exchange, lambda own, ids: (own, jnp.zeros(ids.shape + (width,), BF)), own0, second
    )
    own1 = core_sum(own1)
    parts1 = spread(own1)
    rows0 = add(parts0)
    picked0, saved_first = first_layer(
        own_lengths[0], pick_index[:picks], after(rows0, parts1[0]), position_table, norm_gain_table, weights
    )
    rows1 = add([after(part, picked0) for part in parts1])
    target_rows = jnp.concatenate([rows1[seq_len + picks :], rows1[seq_len : seq_len + picks]])
    saved_second, final, head, top = two_layers(
        own_lengths, pick_index, rows1[:seq_len], position_table, (picked0, saved_first[0]), norm_gain_table, weights,
        head_dense_maps,
    )

    z = head[0]
    near = jnp.concatenate([z] + [swap(z, "vocab", 2 * mask) for mask in range(1, vocab_size // 2)])
    label_rows = jnp.where(jnp.arange(picks)[None, :] == slots, own_labels[:, None], -1).reshape(-1, 1)
    class_grad, class_out = class_head(label_rows, final, head_dense_maps, class_projection)
    near_sum, far_sum = table_pass(
        after(near, class_out), swap(near, "vocab", 1), token_embedding_table
    )
    merged = merge(near_sum, swap(far_sum, "vocab", 1), vocab_size // 2)
    parts = [merged[0]] + [swap(merged[mask], "vocab", 2 * mask) for mask in range(1, vocab_size // 2)]
    live = jnp.arange(picks)[None, :] < own_lengths[:, None] * 15 // 100
    live = (live & (jnp.arange(picks)[None, :] < slots)).reshape(-1)

    grads0, grads1, terms = backward(
        parts, own_lengths, pick_index, target_rows, live.astype(F32)[:, None], class_grad, class_out, head, final,
        top, (saved_first, saved_second), norm_gain_table, weights, head_dense_maps,
    )
    layers = [jnp.concatenate([grads0, class_out], 1), jnp.pad(grads1, ((0, 0), (0, width + EXTRA)))]
    core, keep, got, terms = reduce_all(layers, terms)
    return tuple(
        update(
            core.reshape(1).astype(jnp.int32), keep, got, terms,
            (adapter_outputs, adapter_moment_first, adapter_moment_second),
            (class_projection, class_moment_first, class_moment_second),
        )
    )


def solution(mesh):
    split = P(None, ("dp", "vocab"), None)
    placed = (split, P(None, ("dp", "vocab")), split, split, P(None, ("dp", "vocab")), P("vocab", None)) + (P(),) * 15
    return jax.shard_map(body, mesh=mesh, in_specs=placed, out_specs=(P(),) * 8, check_vma=False)
```

```python
import functools

import jax
import jax.numpy as jnp
from jax import lax
from jax.experimental import pallas as pl
from jax.experimental.pallas import tpu as pltpu
from jax.sharding import PartitionSpec as P

HDIM = 64
STEP = 10
NORM_EPS = 1e-05
ADAPTER_SCALE = 2.0
NEG_FILL = -1e30
CLIP_AT = 0.001
RATE = 0.03
BETA_ONE = 0.9
BETA_TWO = 0.999
ADAM_EPS = 1e-08
DECAY = 0.01
BF = jnp.bfloat16
F32 = jnp.float32


def dot(left, right):
    return jnp.dot(left, right, preferred_element_type=F32)


def dot_nt(left, right):
    return lax.dot_general(left, right, (((1,), (1,)), ((), ())), preferred_element_type=F32)


def dot_tn(left, right):
    return lax.dot_general(left, right, (((0,), (0,)), ((), ())), preferred_element_type=F32)


def norm_parts(values):
    center = values - jnp.mean(values, -1, keepdims=True)
    spread = jnp.mean(center * center, -1, keepdims=True)
    rstd = lax.rsqrt(spread + NORM_EPS)
    return center * rstd, rstd


def norm_back(grad_hat, hat, rstd):
    first = jnp.mean(grad_hat, -1, keepdims=True)
    second = jnp.mean(grad_hat * hat, -1, keepdims=True)
    return rstd * (grad_hat - first - hat * second)


def gelu_both(values):
    root = 0.7978845608028654
    square = values * values
    bend = jnp.tanh(root * values * (1.0 + 0.044715 * square))
    half = 0.5 * (1.0 + bend)
    slope = half + 0.5 * values * (1.0 - bend * bend) * root * (1.0 + 0.134145 * square)
    return values * half, slope


def high_low(values):
    high = lax.reduce_precision(values, 8, 7)
    return high.astype(BF), (values - high).astype(BF)


def swap(value, axis, mask):
    size = lax.axis_size(axis)
    return lax.ppermute(value, axis, [(i, i ^ mask) for i in range(size)])


def adapter_tables(adapter_inputs, adapter_down_input, adapter_outputs):
    layers, width, columns = adapter_inputs.shape
    rank = adapter_down_input.shape[2]
    total = adapter_outputs.shape[2]
    one = jnp.pad(adapter_inputs.transpose(0, 2, 1), ((0, 0), (0, 64 - columns), (0, 0)))
    a_all = jnp.concatenate([one, one], 1)
    one = jnp.pad(adapter_down_input, ((0, 0), (0, 0), (columns, 64 - columns - rank)))
    a_down = jnp.concatenate([one, one], 2)
    high = lax.reduce_precision(ADAPTER_SCALE * adapter_outputs, 8, 7)
    both = jnp.stack([high, ADAPTER_SCALE * adapter_outputs - high], 1)
    column = jnp.arange(total) // width
    group = jnp.where(column < 4, column, jnp.where(column == 4, 5, 4))
    keep = jnp.arange(8)[:, None] == group[None, :]
    b_all = jnp.where(keep[None, None, :, None, :], both[:, :, None, :, :], 0.0)
    return a_all, a_down, b_all.reshape(layers, 128, total).astype(BF)


def moment_update(weight, grad, first, second):
    first_new = BETA_ONE * first + (1.0 - BETA_ONE) * grad
    second_new = BETA_TWO * second + (1.0 - BETA_TWO) * grad * grad
    fix_one = 1.0 - BETA_ONE**STEP
    fix_two = 1.0 - BETA_TWO**STEP
    step_size = first_new / fix_one / (jnp.sqrt(second_new / fix_two) + ADAM_EPS)
    return (weight - RATE * (step_size + DECAY * weight), first_new, second_new)


VMEM_SPEC = pl.BlockSpec(memory_space=pltpu.VMEM)
SMEM_SPEC = pl.BlockSpec(memory_space=pltpu.SMEM)
ANY_SPEC = pl.BlockSpec(memory_space=pl.ANY)
PARAMS = pltpu.CompilerParams(vmem_limit_bytes=63 * 2**20)
CHUNK = 16
EXTRA = 128
ADAPTERS = 9


def chunked(rows, body, step=CHUNK):
    for start in range(0, rows, step):
        body(slice(start, start + step))


def lane_half():
    return lax.broadcasted_iota(jnp.int32, (1, 128), 1) < HDIM


def split_three(values):
    high = values.astype(BF)
    rest = values - high.astype(F32)
    middle = rest.astype(BF)
    return high, middle, (rest - middle.astype(F32)).astype(BF)


def lanes_of(parts):
    lane = lax.broadcasted_iota(jnp.int32, (1, 128), 1) % HDIM
    out = jnp.zeros((), BF)
    for i, part in reversed(list(enumerate(parts))):
        out = jnp.where(lane == i, part, out)
    return out


def key_extra(size, length):
    one = jnp.ones((), BF)
    mask = jnp.where(lax.broadcasted_iota(jnp.int32, (size, 1), 0) < length, 0.0, NEG_FILL)
    return lanes_of([one, one, one, jnp.broadcast_to(mask, (size, 128)).astype(BF)])


def attend_kernel(size, length, queries, q_at, k_at, v_at, out_ref, log_ref, score_ref, prob_ref):
    bias = jnp.where(lax.broadcasted_iota(jnp.int32, (1, size), 1) < length, 0.0, NEG_FILL)
    left = lane_half()
    lane = lax.broadcasted_iota(jnp.int32, (1, 128), 1)
    log_ref[...] = jnp.zeros(log_ref.shape, BF)

    def pair(p, carry):
        cols = pl.ds(pl.multiple_of(p * 128, 128), 128)
        q = q_at(cols) * 0.125
        k_t = k_at(cols).T
        v = v_at(cols)
        zero, one = jnp.zeros((), BF), jnp.ones((), BF)
        outs, tops = [], []
        for half in range(2):
            own = left if half == 0 else ~left
            score_ref[half] = dot(jnp.where(own, q, zero), k_t)
        for half in range(2):
            own = left if half == 0 else ~left
            top = []
            for start in range(0, queries, CHUNK):
                rows = slice(start, start + CHUNK)
                score = score_ref[half, rows, :] + bias
                highest = jnp.max(score, -1, keepdims=True)
                prob_ref[half, rows, :] = jnp.exp(score - highest).astype(BF)
                top.append(highest)
            outs.append(dot(prob_ref[half], jnp.where(own, v, one)))
            tops.append(jnp.concatenate(top, 0))
        total = pltpu.roll(jnp.where(left, outs[1], outs[0]), HDIM, 1)
        out_ref[:, cols] = (jnp.where(left, outs[0], outs[1]) / total).astype(BF)
        log = jnp.where(left, tops[0], tops[1]) + jnp.log(total)
        packed = log_ref[...]
        for half, value in enumerate((log, pltpu.roll(log, HDIM, 1))):
            for i, piece in enumerate(split_three(value)):
                packed = jnp.where(lane == 6 * p + 3 * half + i, piece, packed)
        log_ref[...] = packed
        return carry

    lax.fori_loop(0, out_ref.shape[1] // 128, pair, 0)


def attend_back_kernel(size, length, queries, q_at, k_at, v_at, o_at, g_at, log_ref, dq_ref, dk_ref, dv_ref,
                       score_ref, grad_ref, prob_ref, ds_ref):
    left = lane_half()
    k_extra = key_extra(size, length)
    one = jnp.ones((), BF)
    v_extra = lanes_of([one, one, one])
    lane = lax.broadcasted_iota(jnp.int32, (1, 128), 1)
    row = lax.broadcasted_iota(jnp.int32, (128, 128), 0)
    col = lax.broadcasted_iota(jnp.int32, (128, 128), 1)
    across = jnp.where(
        (lax.broadcasted_iota(jnp.int32, (128, 128), 0) < HDIM) != left, 1.0, 0.0
    ).astype(BF)

    def pair(p, carry):
        cols = pl.ds(pl.multiple_of(p * 128, 128), 128)
        q = q_at(cols) * 0.125
        k, v, g = k_at(cols), v_at(cols), g_at(cols)
        place = jnp.where(
            (col < 3) & (row == 6 * p + 3 + col) | (col >= HDIM) & (col < HDIM + 3) & (row == 6 * p + col - HDIM),
            -1.0,
            0.0,
        ).astype(BF)
        q_extra = jnp.where(lane % HDIM == 3, one, dot(log_ref[...], place).astype(BF))
        product = g.astype(F32) * o_at(cols).astype(F32)
        high = product.astype(BF)
        low = (product - high.astype(F32)).astype(BF)
        g_extra = lanes_of([-x for x in split_three(dot(high, across) + dot(low, across))])
        for half in range(2):
            own = left if half == 0 else ~left
            score_ref[half, :, :queries] = dot_nt(jnp.where(own, k, k_extra), jnp.where(own, q, q_extra))
            grad_ref[half, :, :queries] = dot_nt(jnp.where(own, v, v_extra), jnp.where(own, g, g_extra))
        d_q, d_k, d_v = [], [], []
        for half in range(2):
            for start in range(0, size, CHUNK):
                rows = slice(start, start + CHUNK)
                prob = jnp.exp(score_ref[half, rows, :queries])
                prob_ref[half, rows, :queries] = prob.astype(BF)
                ds_ref[half, rows, :queries] = (prob * grad_ref[half, rows, :queries]).astype(BF)
            d_scores = ds_ref[half, :, :queries]
            d_v.append(dot(prob_ref[half, :, :queries], g))
            d_k.append(dot(d_scores, q))
            d_q.append(dot_tn(d_scores, k))
        dq_ref[:, cols] = (jnp.where(left, d_q[0], d_q[1]) * 0.125).astype(BF)
        dk_ref[:, cols] = jnp.where(left, d_k[0], d_k[1]).astype(BF)
        dv_ref[:, cols] = jnp.where(left, d_v[0], d_v[1]).astype(BF)
        return carry

    lax.fori_loop(0, dq_ref.shape[1] // 128, pair, 0)


def weight_loads(hbm, width, sems, wqkv, wo, wu, wd, bd, layer=0):
    wqkv_hbm, wo_hbm, wu_hbm, wd_hbm, ad_hbm, b_hbm = hbm
    pieces = {}
    if wqkv is not None:
        pieces["qkv"] = 0, [
            (wqkv_hbm.at[layer], wqkv.at[:width, :]),
            (b_hbm.at[layer, :, pl.ds(0, 3 * width)], wqkv.at[width:, :]),
        ]
    pieces["o"] = 2, [
        (wo_hbm.at[layer], wo.at[:width, :]),
        (b_hbm.at[layer, :, pl.ds(3 * width, width)], wo.at[width:, :]),
    ]
    pieces["down"] = 4, [
        (wd_hbm.at[layer], wd.at[:, :width]),
        (ad_hbm.at[layer], wd.at[:, width:]),
        (b_hbm.at[layer, :, pl.ds(4 * width, width)], bd),
    ]
    pieces["up"] = 7, [
        (wu_hbm.at[layer], wu.at[:width, :]),
        (b_hbm.at[layer, :, pl.ds(5 * width, wu.shape[1])], wu.at[width:, :]),
    ]
    return {
        name: [
            pltpu.make_async_copy(source, target, sems.at[first + n]) for n, (source, target) in enumerate(copies)
        ]
        for name, (first, copies) in pieces.items()
    }


def start_all(loads):
    for load in loads:
        load.start()


def wait_all(loads):
    for load in loads:
        load.wait()


def merge_inner(inner, inners):
    lane = lax.broadcasted_iota(jnp.int32, (1, 128), 1) % 64 // 8
    return jnp.where(
        lane < 3, inner, jnp.where(lane == 3, inners[0], jnp.where(lane == 4, inners[1], inners[2]))
    )


def upper_kernel(size, width, wide, gain_ref, gain, hidden, attn, x_ref, sum_ref, part, active, slope, wo, wu, wd,
                 a_ref, bd_ref, waits, hat1_ref, rstd1_ref, rstd2_ref, slope_done):
    inner_o = dot_nt(attn[:, :width], a_ref[...]).astype(BF)
    attn[:, width:] = inner_o
    waits("o")
    sum_ref[...] = dot(attn[...], wo[...])

    def middle(r):
        hat, rstd = norm_parts(hidden[r, :] + sum_ref[r, :])
        value = hat * gain_ref[gain : gain + 1, :]
        hidden[r, :] = value
        x_ref[r, :width] = value.astype(BF)
        hat1_ref[r, :] = hat.astype(BF)
        rstd1_ref[r, :] = jnp.broadcast_to(rstd, (CHUNK, 128))

    chunked(size, middle)
    inner_u = dot_nt(x_ref[:, :width], a_ref[...]).astype(BF)
    x_ref[:, width:] = inner_u
    waits("up")
    waits("down")
    steps = wide // width

    def upper(j):
        part[j % 2] = dot(x_ref[...], wu[:, j * width : (j + 1) * width])

    total = None
    upper(0)
    for j in range(steps):
        if j + 1 < steps:
            upper(j + 1)
        cols = slice(j * width, (j + 1) * width)

        def bend(r):
            value, rise = gelu_both(part[j % 2, r, :])
            active[j % 2, r, :] = value.astype(BF)
            slope[r, cols] = rise.astype(BF)

        chunked(size, bend)
        down = dot(active[j % 2], wd[cols, :])
        if j == 0:
            sum_ref[...] = down[:, :width]
            total = down[:, width:]
        else:
            sum_ref[...] += down[:, :width]
            total = total + down[:, width:]
    slope_done()
    inner_d = total.astype(BF)
    sum_ref[...] += dot(inner_d, bd_ref[...])

    def last(r):
        hat, rstd = norm_parts(hidden[r, :] + sum_ref[r, :])
        hidden[r, :] = hat * gain_ref[gain + 1 : gain + 2, :]
        rstd2_ref[r, :] = jnp.broadcast_to(rstd, (CHUNK, 128))

    chunked(size, last)
    return inner_o, inner_u, inner_d


def first_run(
    length, near_ref, far_ref, pos_ref, gain_ref, loads, freed, a_ref, bd_ref, qkv_done, attn_done, slope_done,
    log_ref, inner_ref, hat1_ref, rstd1_ref, rstd2_ref,
    wqkv, wo, wu, wd, hidden, x_ref, qkv, attn, sum_ref, part, active, slope, score, prob,
):
    size, width = pos_ref.shape
    wide = wu.shape[1]

    def embed(r):
        rows = near_ref[r, :].astype(F32) + far_ref[r, :].astype(F32)
        hat, _ = norm_parts(rows + pos_ref[r, :].astype(F32))
        value = hat * gain_ref[0:1, :]
        hidden[r, :] = value
        x_ref[r, :width] = value.astype(BF)

    chunked(size, embed)
    inner = dot_nt(x_ref[:, :width], a_ref[...]).astype(BF)
    x_ref[:, width:] = inner
    wait_all(loads["qkv"])
    for i in range(3):
        cols = slice(i * width, (i + 1) * width)
        qkv[:, cols] = dot(x_ref[...], wqkv[:, cols]).astype(BF)
    freed("qkv")
    qkv_done()
    attend_kernel(
        size, length, size,
        lambda c: qkv[:, c],
        lambda c: qkv[:, pl.ds(c.start + width, 128)],
        lambda c: qkv[:, pl.ds(c.start + 2 * width, 128)],
        attn.at[:, pl.ds(0, width)], log_ref, score, prob,
    )
    attn_done()
    inners = upper_kernel(
        size, width, wide, gain_ref, 1, hidden, attn, x_ref, sum_ref, part, active, slope, wo, wu, wd, a_ref, bd_ref,
        lambda name: wait_all(loads[name]), hat1_ref, rstd1_ref, rstd2_ref, slope_done,
    )
    for name in ("o", "up", "down"):
        freed(name)
    inner_ref[...] = merge_inner(inner, inners)


def pick_rows(pick_ref, r, hidden, high_ref, size):
    lows = []
    for start in range(0, size, 128):
        s = slice(start, start + 128)
        value = hidden[s, :]
        high = value.astype(BF)
        high_ref[s, :] = high
        lows.append((value - high.astype(F32)).astype(BF))
    hot = (pick_ref[r, :] == lax.broadcasted_iota(jnp.int32, (1, size), 1)).astype(BF)
    return dot(hot, high_ref[...]) + dot(hot, jnp.concatenate(lows, 0))


def first_layer_kernel(
    length_ref, pick_ref, near_ref, far_ref, pos_ref, gain_ref, wqkv_hbm, wo_hbm, wu_hbm, wd_hbm, ad_hbm, b_hbm, a_ref,
    picked_ref, high_ref, qkv_hbm, log_ref, attn_hbm, inner_ref, hat1_ref, rstd1_ref, slope_hbm, rstd2_ref,
    wqkv, wo, wu, wd, bd_ref, hidden, x_ref, qkv, attn, sum_ref, part, active, slope, score, prob, sems,
):
    size, width = near_ref.shape
    hbm = (wqkv_hbm, wo_hbm, wu_hbm, wd_hbm, ad_hbm, b_hbm)
    loads = weight_loads(hbm, width, sems, wqkv, wo, wu, wd, bd_ref)
    a_ref = a_ref.at[0]
    for name in ("qkv", "o", "up", "down"):
        start_all(loads[name])
    stores = [
        pltpu.make_async_copy(qkv, qkv_hbm, sems.at[9]),
        pltpu.make_async_copy(attn.at[:, pl.ds(0, width)], attn_hbm, sems.at[10]),
        pltpu.make_async_copy(slope, slope_hbm, sems.at[11]),
    ]
    first_run(
        length_ref[0], near_ref, far_ref, pos_ref, gain_ref, loads, lambda name: None, a_ref, bd_ref, stores[0].start,
        stores[1].start, stores[2].start, log_ref, inner_ref, hat1_ref, rstd1_ref, rstd2_ref,
        wqkv, wo, wu, wd, hidden, x_ref, qkv, attn, sum_ref, part, active, slope, score, prob,
    )
    picked_ref[...] = pick_rows(pick_ref, slice(0, picked_ref.shape[0]), hidden, high_ref, size)
    wait_all(stores)


def saved_shapes(size, width, wide):
    return [
        ((size, width), BF), ((size, 3 * width), BF), ((size, 128), BF), ((size, width), BF),
        ((size, 128), BF), ((size, width), BF), ((size, 128), F32), ((size, wide), BF), ((size, 128), F32),
    ]


def saved_specs():
    v, a = VMEM_SPEC, ANY_SPEC
    return [v, a, v, a, v, v, v, a, v]


def first_scratch(size, width, wide):
    return [
        pltpu.VMEM((width + EXTRA, 3 * width), BF), pltpu.VMEM((width + EXTRA, width), BF),
        pltpu.VMEM((width + EXTRA, wide), BF), pltpu.VMEM((wide, width + EXTRA), BF), pltpu.VMEM((EXTRA, width), BF),
        pltpu.VMEM((size, width), F32), pltpu.VMEM((size, width + EXTRA), BF),
        pltpu.VMEM((size, 3 * width), BF),
        pltpu.VMEM((size, width + EXTRA), BF), pltpu.VMEM((size, width), F32),
        pltpu.VMEM((2, size, width), F32), pltpu.VMEM((2, size, width), BF), pltpu.VMEM((size, wide), BF),
        pltpu.VMEM((2, size, size), F32), pltpu.VMEM((2, size, size), BF),
    ]


def first_layer(lengths, picks, near, far, positions, gains, weights):
    wqkv, wo, wu, wd, a_all, a_down, b_all = weights
    size, width = positions.shape
    wide = wu.shape[2]
    count = lengths.shape[0]
    shapes = [((picks.shape[0] // count, width), F32)] + saved_shapes(size, width, wide)
    v, a = VMEM_SPEC, ANY_SPEC
    picked, *saved = pl.pallas_call(
        first_layer_kernel,
        out_shape=[jax.ShapeDtypeStruct(*s) for s in shapes],
        in_specs=[SMEM_SPEC] + [v] * 5 + [a] * 6 + [v],
        out_specs=[v] + saved_specs(),
        scratch_shapes=first_scratch(size, width, wide) + [pltpu.SemaphoreType.DMA((12,))],
        compiler_params=PARAMS,
    )(lengths, picks, near, far, positions, gains, wqkv, wo, wu, wd, a_down, b_all, a_all)
    return picked, tuple(saved)


def upper_back_kernel(size, width, wide, inner_t, grad_at, gain_ref, gain, high_ref, rstd2_ref, slope, hat1_ref, rstd1_ref,
                      wo, wu, wd, a_ref, bd_ref, out_ref, waits, grad2, x_ref, sum_ref, part, active, grad1_at, more=False):
    def second(r):
        scale = gain_ref[gain + 1 : gain + 2, :]
        value = norm_back(grad_at(r) * scale, high_ref[r, :].astype(F32) * (1.0 / scale), rstd2_ref[r, 0:1])
        grad2[r, :] = value
        x_ref[r, :width] = value.astype(BF)

    def put(cols, value):
        out_ref[:, cols] = out_ref[:, cols] + value if more else value

    chunked(size, second)
    low = x_ref[:, :width]
    waits("down")
    x_ref[:, width:] = dot_nt(low, bd_ref[...]).astype(BF)
    put(slice(4 * width, 5 * width), ADAPTER_SCALE * dot(inner_t[32:48], low)[8:])
    waits("up")
    steps = wide // width

    def inward(j):
        part[j % 2] = dot_nt(x_ref[...], wd[j * width : (j + 1) * width, :])

    total = None
    inward(0)
    for j in range(steps):
        if j + 1 < steps:
            inward(j + 1)
        cols = slice(j * width, (j + 1) * width)

        def bend(r):
            active[j % 2, r, :] = (part[j % 2, r, :] * slope[r, cols].astype(F32)).astype(BF)

        chunked(size, bend)
        piece = dot_nt(active[j % 2], wu[:, cols])
        put(slice((5 + j) * width, (6 + j) * width), ADAPTER_SCALE * dot(inner_t[32:48], active[j % 2])[:8])
        if j == 0:
            sum_ref[...] = piece[:, :width]
            total = piece[:, width:]
        else:
            sum_ref[...] += piece[:, :width]
            total = total + piece[:, width:]
    sum_ref[...] += dot(total.astype(BF), a_ref[...])

    def first(r):
        value = norm_back(
            (grad2[r, :] + sum_ref[r, :]) * gain_ref[gain : gain + 1, :], hat1_ref[r, :].astype(F32), rstd1_ref[r, 0:1]
        )
        x_ref[r, :width] = value.astype(BF)
        if grad1_at is not None:
            grad1_at[r, :] = value

    chunked(size, first)
    low = x_ref[:, :width]
    waits("o")
    both = dot_nt(low, wo[...])
    put(slice(3 * width, 4 * width), ADAPTER_SCALE * dot(inner_t[16:32], low)[8:])
    return (both[:, :width] + dot(both[:, width:].astype(BF), a_ref[...])).astype(BF)


def two_layers_kernel(
    length_ref, pick_ref, near_ref, far_ref, pos_ref, picked0_ref, high0_ref, gain_ref,
    wqkv_hbm, wo_hbm, wu_hbm, wd_hbm, ad_hbm, b_hbm, map_hbm, a_ref,
    high1_ref, qkv_hbm, log_ref, attn_hbm, inner_ref, hat1_ref, rstd1_ref, slope_hbm, rstd2_ref,
    final_ref, z_ref, head_hat_ref, head_rstd_ref, head_slope_ref,
    q_ref, kv_hbm, top_log_ref, attn_out_ref, top_inner_ref, inner_kv_ref, top_hat1_ref, top_rstd1_ref, top_slope,
    top_rstd2_ref,
    wqkv, wo, wu, wd, bd_ref, hidden, x_ref, qkv, attn, sum_ref, part, active, slope, score, prob, map_ref, x_kv, kv,
    sems,
):
    count = kv.shape[0]
    size, width = pos_ref.shape
    rows = final_ref.shape[0]
    a0_ref, a1_ref = a_ref.at[0], a_ref.at[1]
    picks = rows // count
    wide = wu.shape[1]
    hbm = (wqkv_hbm, wo_hbm, wu_hbm, wd_hbm, ad_hbm, b_hbm)
    loads = weight_loads(hbm, width, sems, wqkv, wo, wu, wd, bd_ref)
    later = weight_loads(hbm, width, sems, wqkv, wo, wu, wd, bd_ref, 1)
    load_map = pltpu.make_async_copy(map_hbm.at[0], map_ref, sems.at[13])
    for name in ("qkv", "o", "up", "down"):
        start_all(loads[name])
    load_map.start()
    stores = [
        pltpu.make_async_copy(qkv, qkv_hbm, sems.at[9]),
        pltpu.make_async_copy(attn.at[:, pl.ds(0, width)], attn_hbm, sems.at[10]),
        pltpu.make_async_copy(slope, slope_hbm, sems.at[11]),
        pltpu.make_async_copy(kv, kv_hbm, sems.at[12]),
    ]
    first_run(
        length_ref[1], near_ref, far_ref, pos_ref, gain_ref, loads, lambda name: start_all(later[name]), a0_ref, bd_ref,
        stores[0].start, stores[1].start, stores[2].start, log_ref, inner_ref, hat1_ref, rstd1_ref, rstd2_ref,
        wqkv, wo, wu, wd, hidden, x_ref, qkv, attn, sum_ref, part, active, slope, score, prob,
    )
    picked = [picked0_ref[...], pick_rows(pick_ref, slice(picks, rows), hidden, high1_ref, size)]
    stores[1].wait()
    top_hidden, top_x, top_attn = hidden.at[pl.ds(0, rows)], x_ref.at[pl.ds(0, rows)], attn.at[pl.ds(0, rows)]
    top_sum = sum_ref.at[pl.ds(0, rows)]
    for i, high_ref in enumerate((high0_ref, high1_ref)):
        r = slice(i * picks, (i + 1) * picks)
        hidden[r, :] = picked[i]
        x_ref[r, :width] = picked[i].astype(BF)
        x_kv[i, :, :width] = high_ref[...]
        inner_kv = dot_nt(high_ref[...], a1_ref[...]).astype(BF)
        inner_kv_ref[i] = inner_kv
        x_kv[i, :, width:] = inner_kv
    inner = dot_nt(top_x[:, :width], a1_ref[...]).astype(BF)
    x_ref[:rows, width:] = inner
    wait_all(later["qkv"])
    q_ref[...] = dot(top_x[...], wqkv[:, :width]).astype(BF)
    for i in range(count):
        for j in range(2):
            kv[i, :, j * width : (j + 1) * width] = dot(
                x_kv[i], wqkv[:, (j + 1) * width : (j + 2) * width]
            ).astype(BF)
    stores[3].start()
    for i in range(count):
        r = slice(i * picks, (i + 1) * picks)
        attend_kernel(
            size, length_ref[i], picks,
            lambda c: q_ref[r, c],
            lambda c: kv[i, :, c],
            lambda c: kv[i, :, pl.ds(c.start + width, 128)],
            attn.at[pl.ds(i * picks, picks), pl.ds(0, width)], top_log_ref.at[pl.ds(i * picks, picks)],
            score.at[:, pl.ds(0, picks)], prob.at[:, pl.ds(0, picks)],
        )
    attn_out_ref[...] = attn[:rows, :width]
    inners = upper_kernel(
        rows, width, wide, gain_ref, 3, top_hidden, top_attn, top_x, top_sum, part.at[:, pl.ds(0, rows)],
        active.at[:, pl.ds(0, rows)], top_slope, wo, wu, wd, a1_ref, bd_ref, lambda name: wait_all(later[name]),
        top_hat1_ref, top_rstd1_ref, top_rstd2_ref, lambda: None,
    )
    top_inner_ref[...] = merge_inner(inner, inners)
    final_ref[...] = hidden[:rows, :].astype(BF)
    load_map.wait()
    sum_ref[:rows, :] = dot(final_ref[...], map_ref[...])

    def head(r):
        value, rise = gelu_both(sum_ref[r, :])
        hat, rstd = norm_parts(value)
        head_slope_ref[r, :] = rise
        head_hat_ref[r, :] = hat
        head_rstd_ref[r, :] = jnp.broadcast_to(rstd, (CHUNK, 128))
        z_ref[r, :] = (hat * gain_ref[5:6, :]).astype(BF)

    chunked(rows, head)
    stores[0].wait()
    stores[2].wait()
    stores[3].wait()


def two_layers(lengths, picks, near, far, positions, first, gains, weights, maps):
    wqkv, wo, wu, wd, a_all, a_down, b_all = weights
    picked0, high0 = first
    size, width = positions.shape
    wide = wu.shape[2]
    count = 2
    total = picks.shape[0]
    shapes = saved_shapes(size, width, wide) + [
        ((total, width), BF), ((total, width), BF), ((total, width), F32), ((total, 128), F32), ((total, width), F32),
        ((total, width), BF), ((count, size, 2 * width), BF), ((total, 128), BF), ((total, width), BF),
        ((total, 128), BF), ((count, size, 128), BF), ((total, width), BF), ((total, 128), F32), ((total, wide), BF),
        ((total, 128), F32),
    ]
    v, a = VMEM_SPEC, ANY_SPEC
    out = pl.pallas_call(
        two_layers_kernel,
        out_shape=[jax.ShapeDtypeStruct(*s) for s in shapes],
        in_specs=[SMEM_SPEC] + [v] * 7 + [a] * 7 + [v],
        out_specs=saved_specs() + [v] * 6 + [a] + [v] * 8,
        scratch_shapes=first_scratch(size, width, wide) + [
            pltpu.VMEM((width, width), BF), pltpu.VMEM((count, size, width + EXTRA), BF),
            pltpu.VMEM((count, size, 2 * width), BF), pltpu.SemaphoreType.DMA((14,)),
        ],
        compiler_params=PARAMS,
    )(lengths, picks, near, far, positions, picked0, high0, gains, wqkv, wo, wu, wd, a_down, b_all, maps, a_all)
    return tuple(out[:9]), out[9], tuple(out[10:14]), tuple(out[14:])


def backward_kernel(part_count, *refs):
    backward_run(refs[:part_count], *refs[part_count:])


def backward_run(
    part_refs, length_ref, pick_ref, near_ref, far_ref, live_ref, label_ref, projection_ref, gain_ref,
    z_ref, head_hat_ref, head_rstd_ref, head_slope_ref, final_ref,
    q_ref, kv_hbm, log_ref, attn_ref, inner_ref, inner_kv_ref, hat1_ref, rstd1_ref, slope, rstd2_ref,
    high0_hbm, qkv0_hbm, log0_hbm, attn0_hbm, inner0_hbm, hat0_hbm, rstd0_hbm, slope0_hbm, rrstd0_hbm,
    high1_hbm, qkv1_hbm, log1_hbm, attn1_hbm, inner1_hbm, hat1_hbm, rstd1_hbm, slope1_hbm, rrstd1_hbm,
    wqkv_hbm, wo_hbm, wu_hbm, wd_hbm, ad_hbm, b_hbm, map_hbm, a_ref,
    layer0_ref, layer1_ref, term_ref,
    wqkv, wo, wu, wd, bd_ref, kv, grads, grad1, grad2, x_ref, sum_ref, part, active, d_attn, dq, dkv,
    score, dscore, prob, ds, s_high, s_log, s_attn, s_inner, s_hat1, s_rstd1, s_slope, s_rstd2, sems,
):
    count, size, _ = kv.shape
    rows, width = z_ref.shape
    picks = rows // count
    wide = wu.shape[1]
    hbm = (wqkv_hbm, wo_hbm, wu_hbm, wd_hbm, ad_hbm, b_hbm)
    loads = weight_loads(hbm, width, sems, wqkv, wo, wu, wd, bd_ref, 1)
    lower = weight_loads(hbm, width, sems, None, wo, wu, wd, bd_ref, 0)
    map_refs = [wqkv.at[pl.ds(0, width), pl.ds(i * width, width)] for i in range(2)]
    loads["map"] = [pltpu.make_async_copy(map_hbm.at[i], map_refs[i], sems.at[20 + i]) for i in range(2)]
    loads["kv"] = [pltpu.make_async_copy(kv_hbm, kv, sems.at[9])]
    total_width = ADAPTERS * width
    adapter0_ref, adapter1_ref = (x.at[:, pl.ds(0, total_width)] for x in (layer0_ref, layer1_ref))
    class_out_ref = layer0_ref.at[:, pl.ds(total_width, width + EXTRA)]
    layer1_ref[:, total_width:] = jnp.zeros((8, width + EXTRA), F32)
    a0_ref, a1_ref = a_ref.at[0], a_ref.at[1]
    first_target = near_ref.shape[0] - rows
    kept = (s_high, None, s_log, s_attn, s_inner, s_hat1, s_rstd1, s_slope, s_rstd2)
    items = []
    for source_refs in (
        (high0_hbm, qkv0_hbm, log0_hbm, attn0_hbm, inner0_hbm, hat0_hbm, rstd0_hbm, slope0_hbm, rrstd0_hbm),
        (high1_hbm, qkv1_hbm, log1_hbm, attn1_hbm, inner1_hbm, hat1_hbm, rstd1_hbm, slope1_hbm, rrstd1_hbm),
    ):
        copies = [
            pltpu.make_async_copy(source, target, sems.at[10 + n])
            for n, (source, target) in enumerate(zip(source_refs, kept))
            if target is not None
        ]
        qkv_hbm = source_refs[1]
        copies.append(pltpu.make_async_copy(qkv_hbm.at[:, pl.ds(0, 2 * width)], kv.at[0], sems.at[11]))
        copies.append(
            pltpu.make_async_copy(
                qkv_hbm.at[:, pl.ds(2 * width, width)], kv.at[1, :, pl.ds(0, width)], sems.at[19]
            )
        )
        items.append(copies)
    early, late = (0, 3, 4, 5, 6, 7), (1, 2, 8, 9)
    for name in ("map", "down", "up", "o", "kv"):
        start_all(loads[name])
    for n in early:
        items[0][n].start()
    part_rows = pl.ds(0, rows)

    def head(r):
        live = live_ref[r, :]
        t = slice(first_target + r.start, first_target + r.stop)
        target = near_ref[t, :].astype(F32) + far_ref[t, :].astype(F32)
        mean, log_total = mean_of(part_refs, r, width)
        logit = jnp.sum(z_ref[r, :].astype(F32) * target, -1, keepdims=True)
        losses.append(jnp.sum(jnp.where(live > 0.0, log_total - logit, 0.0), 0, keepdims=True))
        lives.append(jnp.sum(live, 0, keepdims=True))
        grad_z = jnp.where(live > 0.0, mean - target, 0.0)
        value = norm_back(grad_z * gain_ref[5:6, :], head_hat_ref[r, :], head_rstd_ref[r, 0:1])
        x_ref[r, :width] = (value * head_slope_ref[r, :]).astype(BF)

    wait_all(loads["map"])
    class_part, class_loss = class_head(label_ref, final_ref, map_refs[1], projection_ref, class_out_ref)
    losses, lives = [class_loss], [jnp.full((1, 1), count, F32)]
    chunked(rows, head)
    lane = lax.broadcasted_iota(jnp.int32, (8, 128), 1)
    term_ref[...] = jnp.where(lane == 0, functools.reduce(jnp.add, losses), functools.reduce(jnp.add, lives))
    grads[0, :rows, :] = dot_nt(x_ref[:rows, :width], map_refs[0][...]) + class_part
    start_all(loads["qkv"])
    inner_t = inner_ref[...].T
    d_attn[:rows, :] = upper_back_kernel(
        rows, width, wide, inner_t, lambda r: grads[0, r, :], gain_ref, 3, final_ref, rstd2_ref, slope, hat1_ref,
        rstd1_ref, wo, wu, wd, a1_ref, bd_ref, adapter1_ref, lambda name: wait_all(loads[name]),
        grad2.at[part_rows], x_ref.at[part_rows], sum_ref.at[part_rows], part.at[:, part_rows],
        active.at[:, part_rows], grad1,
    )
    for name in ("down", "up", "o"):
        start_all(lower[name])
    wait_all(loads["kv"])
    for i in range(count):
        r = slice(i * picks, (i + 1) * picks)
        view = pl.ds(i * picks, picks)
        attend_back_kernel(
            size, length_ref[i], picks,
            lambda c: q_ref[r, c],
            lambda c: kv[i, :, c],
            lambda c: kv[i, :, pl.ds(c.start + width, 128)],
            lambda c: attn_ref[r, c],
            lambda c: d_attn[r, c],
            log_ref.at[view], dq.at[view], dkv.at[i, :, pl.ds(0, width)], dkv.at[i, :, pl.ds(width, width)],
            score, dscore, prob, ds,
        )
    for n in late:
        items[0][n].start()
    wait_all(loads["qkv"])
    both = dot_nt(dq[:rows, :], wqkv[:, :width])
    grad1[...] += both[:, :width] + dot(both[:, width:].astype(BF), a1_ref[...])
    adapter1_ref[:, :width] = ADAPTER_SCALE * dot(inner_t[0:16], dq[:rows, :])[:8]
    total = None
    for i in range(count):
        r = slice(i * picks, (i + 1) * picks)
        hot = (pick_ref[r, :] == lax.broadcasted_iota(jnp.int32, (1, size), 1)).astype(BF)
        value = grad1[r, :]
        high = value.astype(BF)
        low = (value - high.astype(F32)).astype(BF)
        both = dot_nt(dkv[i], wqkv[:, width:])
        grads[i] = (
            both[:, :width]
            + dot(both[:, width:].astype(BF), a1_ref[...])
            + dot_tn(jnp.concatenate([hot, hot], 0), jnp.concatenate([high, low], 0))
        )
        piece = dot(inner_kv_ref[i].T[0:32], dkv[i])
        total = piece if total is None else total + piece
    adapter1_ref[:, width : 2 * width] = ADAPTER_SCALE * total[8:16, :width]
    adapter1_ref[:, 2 * width : 3 * width] = ADAPTER_SCALE * total[16:24, width:]

    for i in range(count):
        for n in early:
            items[i][n].wait()
        inner_t = s_inner[...].T
        d_attn[...] = upper_back_kernel(
            size, width, wide, inner_t, lambda r: grads[i, r, :], gain_ref, 1, s_high, s_rstd2, s_slope, s_hat1,
            s_rstd1, wo, wu, wd, a0_ref, bd_ref, adapter0_ref,
            lambda name: wait_all(lower[name]) if i == 0 else None, grad2, x_ref, sum_ref, part, active, None, i > 0,
        )
        if i + 1 < count:
            for n in early:
                items[i + 1][n].start()
        for n in late:
            items[i][n].wait()
        attend_back_kernel(
            size, length_ref[i], size,
            lambda c: kv[0, :, c],
            lambda c: kv[0, :, pl.ds(c.start + width, 128)],
            lambda c: kv[1, :, c],
            lambda c: s_attn[:, c],
            lambda c: d_attn[:, c],
            s_log, dq, dkv.at[0, :, pl.ds(0, width)], dkv.at[0, :, pl.ds(width, width)], score, dscore, prob, ds,
        )
        if i + 1 < count:
            for n in late:
                items[i + 1][n].start()
        for j, value in enumerate((dq[...], dkv[0, :, :width], dkv[0, :, width:])):
            start = 8 * j // 16 * 16
            cols = slice(j * width, (j + 1) * width)
            piece = ADAPTER_SCALE * dot(inner_t[start : start + 16], value)[8 * j - start : 8 * j - start + 8]
            adapter0_ref[:, cols] = piece if i == 0 else adapter0_ref[:, cols] + piece


def backward(parts, lengths, picks, near, far, live, labels, projection, head, final, top, saved, gains, weights, maps):
    wqkv, wo, wu, wd, a_all, a_down, b_all = weights
    kv = top[1]
    rows, width = final.shape
    count, size, _ = kv.shape
    wide = wu.shape[2]
    v, a = VMEM_SPEC, ANY_SPEC
    low = pltpu.VMEM((size, width), BF)
    full = pltpu.VMEM((size, width), F32)
    layer = jax.ShapeDtypeStruct((8, b_all.shape[2] + width + EXTRA), F32)
    return pl.pallas_call(
        functools.partial(backward_kernel, len(parts)),
        out_shape=[layer, layer, jax.ShapeDtypeStruct((8, 128), F32)],
        in_specs=[v] * len(parts) + [SMEM_SPEC] + [v] * 13 + [a] + [v] * 8 + [a] * 18 + [a] * 7 + [v],
        out_specs=[v] * 3,
        scratch_shapes=[
            pltpu.VMEM((width + EXTRA, 3 * width), BF), pltpu.VMEM((width + EXTRA, width), BF),
            pltpu.VMEM((width + EXTRA, wide), BF), pltpu.VMEM((wide, width + EXTRA), BF), pltpu.VMEM((EXTRA, width), BF),
            pltpu.VMEM(kv.shape, BF),
            pltpu.VMEM((count, size, width), F32), pltpu.VMEM((rows, width), F32), full,
            pltpu.VMEM((size, width + EXTRA), BF), full, pltpu.VMEM((2, size, width), F32),
            pltpu.VMEM((2, size, width), BF), low, low, pltpu.VMEM(kv.shape, BF),
            pltpu.VMEM((2, size, size), F32), pltpu.VMEM((2, size, size), F32),
            pltpu.VMEM((2, size, size), BF), pltpu.VMEM((2, size, size), BF),
        ] + [pltpu.VMEM(*s) for n, s in enumerate(saved_shapes(size, width, wide)) if n != 1] + [
            pltpu.SemaphoreType.DMA((22,))
        ],
        compiler_params=PARAMS,
    )(*parts, lengths, picks, near, far, live, labels, projection, gains, *head, final, *top, *saved[0], *saved[1],
      wqkv, wo, wu, wd, a_down, b_all, maps, a_all)


def class_head(label_ref, final_ref, map_ref, projection_ref, out_ref):
    width = final_ref.shape[1]
    classes = projection_ref.shape[0]
    label = label_ref[...]
    live = label >= 0
    pooled = jnp.tanh(dot(final_ref[...], map_ref[...]))
    logits = [
        jnp.sum(pooled * projection_ref[c : c + 1, :width], -1, keepdims=True)
        + projection_ref[c : c + 1, width : width + 1]
        for c in range(classes)
    ]
    top = functools.reduce(jnp.maximum, logits)
    exponents = [jnp.exp(x - top) for x in logits]
    total = functools.reduce(jnp.add, exponents)
    loss = top + jnp.log(total)
    pulled = 0.0
    out_ref[...] = jnp.zeros(out_ref.shape, F32)
    for c in range(classes):
        hit = (label == c).astype(F32)
        loss = loss - logits[c] * hit
        grad = jnp.where(live, exponents[c] / total - hit, 0.0)
        pulled = pulled + grad * projection_ref[c : c + 1, :width]
        out_ref[c : c + 1, :width] = jnp.sum(pooled * grad, 0, keepdims=True)
        out_ref[c : c + 1, width:] = jnp.broadcast_to(jnp.sum(grad, 0, keepdims=True), (1, 128))
    back = dot_nt((pulled * (1.0 - pooled * pooled)).astype(BF), map_ref[...])
    return back, jnp.sum(jnp.where(live, loss, 0.0), 0, keepdims=True)


BLOCK = 1024


def table_kernel(count, *refs):
    table_run(refs[:count], *refs[count:])


def table_run(
    part_refs, live_ref, table_hbm, near_out, far_out, place, z_ref, table, acc, score, prob, base, top, total, flag, sems
):
    rows, width = z_ref.shape
    half = rows // 2
    length = table.shape[0]
    blocks = length // BLOCK // 2 * 2
    tail = length - blocks * BLOCK
    sizes = [BLOCK] * blocks + [tail] * (tail > 0)
    for i, size in enumerate(sizes):
        at = pl.ds(i * BLOCK, size)
        pltpu.make_async_copy(table_hbm.at[at, :], table.at[at, :], sems.at[i]).start()

    def wait(i, size):
        at = pl.ds(0, size)
        pltpu.make_async_copy(table_hbm.at[at, :], table.at[at, :], sems.at[i]).wait()

    own = rows // len(part_refs)
    span = own // 2
    lane = lax.broadcasted_iota(jnp.int32, (1, rows), 1)
    number = jnp.full((1, rows), -1, jnp.int32)
    used = 0
    for i in range(2 * len(part_refs)):
        live = live_ref[i]
        slot = lane - i * span
        number = jnp.where((slot >= 0) & (slot < live), slot + used, number)
        used = used + live
    for first in range(0, rows, 64):
        at = lax.broadcasted_iota(jnp.int32, (64, rows), 0) + first
        place[first : first + 64, :] = (at == number).astype(BF)
    for i, part_ref in enumerate(part_refs):
        prob[0, i * own : (i + 1) * own, :width] = part_ref[...]
    z_ref[...] = dot(place[...], prob[0, :, :width]).astype(BF)

    def scores(rows, start, size, slot):
        score[slot, :rows, :size] = dot_nt(z_ref[:rows, :], table[pl.ds(start, size), :])

    def fold(rows, start, size, slot):
        for first in range(0, rows, CHUNK):
            r = slice(first, first + CHUNK)
            low = base[r, :1]
            best, added = top[r, :], total[r, :]
            for column in range(0, size, 128):
                cols = slice(column, min(column + 128, size))
                value = score[slot, r, cols]
                exponent = jnp.exp(value - low)
                prob[slot, r, cols] = exponent.astype(BF)
                if column + 128 <= size:
                    best = jnp.maximum(best, value)
                    added = added + exponent
                else:
                    best = jnp.maximum(best, jnp.max(value, -1, keepdims=True))
                    here = lax.broadcasted_iota(jnp.int32, added.shape, 1)
                    added = added + jnp.where(here == 0, jnp.sum(exponent, -1, keepdims=True), 0.0)
            top[r, :] = best
            total[r, :] = added
        acc[:rows, :] += dot(prob[slot, :rows, :size], table[pl.ds(start, size), :])

    def first_block(rows):
        scores(rows, 0, BLOCK, 0)
        for first in range(0, rows, CHUNK):
            r = slice(first, first + CHUNK)
            highest = jnp.max(score[0, r, :BLOCK], -1, keepdims=True)
            base[r, :] = jnp.broadcast_to(highest, (CHUNK, 128))

    def even(rows, start):
        scores(rows, start + BLOCK, BLOCK, 1)
        fold(rows, start, BLOCK, 0)

    def odd(rows, start):
        scores(rows, jnp.minimum(start + 2 * BLOCK, (blocks - 1) * BLOCK), BLOCK, 0)
        fold(rows, start + BLOCK, BLOCK, 1)

    def rest(rows):
        scores(rows, blocks * BLOCK, tail, 0)
        fold(rows, blocks * BLOCK, tail, 0)

    few = rows * 3 // 4

    def either(body, *at):
        @pl.when(used <= few)
        def _():
            body(few, *at)

        @pl.when(used > few)
        def _():
            body(rows, *at)

    def clear():
        top[...] = jnp.full(top.shape, NEG_FILL, F32)
        total[...] = jnp.zeros(total.shape, F32)
        acc[...] = jnp.zeros(acc.shape, F32)

    def two(i, carry):
        start = pl.multiple_of(i * 2 * BLOCK, BLOCK)
        wait(2 * i + 1, BLOCK)
        either(even, start)

        @pl.when(i + 1 < blocks // 2)
        def _():
            wait(2 * i + 2, BLOCK)

        either(odd, start)
        return carry

    clear()
    base[...] = jnp.zeros(base.shape, F32)
    wait(0, BLOCK)
    either(first_block)
    lax.fori_loop(0, blocks // 2, two, 0)
    if tail:
        wait(blocks, tail)
        either(rest)

    best = jnp.max(top[...], -1, keepdims=True)
    flag[0] = jnp.max(best - base[:, :1])

    @pl.when(flag[0] > 40.0)
    def _():
        base[...] = jnp.broadcast_to(best, base.shape)
        clear()
        scores(rows, 0, BLOCK, 0)

        def again(i, carry):
            start = pl.multiple_of(i * 2 * BLOCK, BLOCK)
            even(rows, start)
            odd(rows, start)
            return carry

        lax.fori_loop(0, blocks // 2, again, 0)
        if tail:
            rest(rows)

    acc[...] = acc[...] / jnp.maximum(jnp.sum(total[...], -1, keepdims=True), 1e-30)
    z_ref[...] = acc[...].astype(BF)
    logs = jnp.log(jnp.maximum(jnp.sum(total[...], -1, keepdims=True), 1e-30))
    extra = lanes_of(split_three(jnp.broadcast_to(base[:, :1] + logs, (rows, 128))))
    for out_ref, r in ((near_out, slice(0, half)), (far_out, slice(half, rows))):
        out_ref[:, :width] = dot_tn(place[:, r], z_ref[...]).astype(BF)
        out_ref[:, width:] = dot_tn(place[:, r], extra).astype(BF)


def table_pass(parts, live, table):
    own, width = parts[0].shape
    rows = own * len(parts)
    length = table.shape[0]
    widest = max(BLOCK, length - length // BLOCK // 2 * 2 * BLOCK)
    widest += -widest % 128
    return pl.pallas_call(
        functools.partial(table_kernel, len(parts)),
        out_shape=[jax.ShapeDtypeStruct((rows // 2, width + EXTRA), BF)] * 2,
        in_specs=[VMEM_SPEC] * len(parts) + [SMEM_SPEC, ANY_SPEC],
        out_specs=[VMEM_SPEC] * 2,
        scratch_shapes=[
            pltpu.VMEM((rows, rows), BF), pltpu.VMEM((rows, width), BF), pltpu.VMEM((length, width), BF),
            pltpu.VMEM((rows, width), F32),
            pltpu.VMEM((2, rows, widest), F32), pltpu.VMEM((2, rows, widest), BF),
            pltpu.VMEM((rows, 128), F32), pltpu.VMEM((rows, 128), F32), pltpu.VMEM((rows, 128), F32),
            pltpu.SMEM((1,), F32), pltpu.SemaphoreType.DMA((length // BLOCK + 1,)),
        ],
        compiler_params=PARAMS,
    )(*parts, live, table)


def mean_of(part_refs, r, width):
    logs = [
        jnp.sum(part_ref[r, width : width + HDIM].astype(F32), -1, keepdims=True) for part_ref in part_refs
    ]
    top = functools.reduce(jnp.maximum, logs)
    shares = [jnp.exp(log - top) for log in logs]
    total = functools.reduce(jnp.add, shares)
    mean = functools.reduce(
        jnp.add, [part_ref[r, :width].astype(F32) * share for part_ref, share in zip(part_refs, shares)]
    )
    return mean / total, top + jnp.log(total)


def merge_kernel(left_ref, right_ref, *out_refs):
    rows, columns = out_refs[0].shape
    width = columns - EXTRA
    for i, out_ref in enumerate(out_refs):
        for start in range(0, rows, CHUNK):
            r = slice(start, start + CHUNK)
            mean, log = mean_of((left_ref, right_ref), slice(i * rows + start, i * rows + start + CHUNK), width)
            out_ref[r, :width] = mean.astype(BF)
            out_ref[r, width:] = lanes_of(split_three(jnp.broadcast_to(log, (CHUNK, EXTRA))))


def merge(left, right, count):
    rows, columns = left.shape
    return pl.pallas_call(
        merge_kernel,
        out_shape=[jax.ShapeDtypeStruct((rows // count, columns), BF)] * count,
        in_specs=[VMEM_SPEC] * 2,
        out_specs=[VMEM_SPEC] * count,
        compiler_params=PARAMS,
    )(left, right)


def update_kernel(core_ref, keep_ref, got_ref, term_ref, w_ref, m_ref, s_ref, cw_ref, cm_ref, cs_ref,
                  sum_ref, norm_ref, wo_ref, mo_ref, so_ref, cwo_ref, cmo_ref, cso_ref, grads):
    total = w_ref.shape[2]
    classes, rows = cw_ref.shape
    count = term_ref[0:1, 1:2]
    first = core_ref[0] == 0
    step = rows - 1
    square = 0.0
    for start in range(0, total, step):
        cols = slice(start, start + step)
        keep, got = keep_ref[:, cols] / count, got_ref[:, cols] / count
        square = square + (keep * keep + got * got)
        grads[0, :, cols] = jnp.where(first, keep, got)
        grads[1, :, cols] = jnp.where(first, got, keep)
    head = jnp.where(first, keep_ref[:, total:], got_ref[:, total:]) / count
    inside = (lax.broadcasted_iota(jnp.int32, head.shape, 0) < classes) & (
        lax.broadcasted_iota(jnp.int32, head.shape, 1) < rows
    )
    head = jnp.where(inside, head, 0.0)
    norm = jnp.sqrt(
        jnp.sum(jnp.sum(square, 1, keepdims=True), 0, keepdims=True)
        + jnp.sum(jnp.sum(head * head, 1, keepdims=True), 0, keepdims=True)
    )
    multiplier = CLIP_AT / jnp.maximum(norm, CLIP_AT)
    sum_ref[0] = term_ref[0, 0]
    sum_ref[1] = term_ref[0, 1]
    norm_ref[0] = norm[0, 0]
    for layer in range(2):
        for start in range(0, total, step):
            at = (layer, slice(None), slice(start, start + step))
            wo_ref[at], mo_ref[at], so_ref[at] = moment_update(
                w_ref[at], grads[at] * multiplier, m_ref[at], s_ref[at]
            )
    turned = (head * multiplier)[:classes, :rows]
    cwo_ref[...], cmo_ref[...], cso_ref[...] = moment_update(cw_ref[...], turned, cm_ref[...], cs_ref[...])


def update(core, keep, got, terms, trained, classes):
    classes = [x.T for x in classes]
    v = VMEM_SPEC
    shape = jax.ShapeDtypeStruct(trained[0].shape, F32)
    class_shape = jax.ShapeDtypeStruct(classes[0].shape, F32)
    *out, first, second, third = pl.pallas_call(
        update_kernel,
        out_shape=[jax.ShapeDtypeStruct((2,), F32), jax.ShapeDtypeStruct((1,), F32)] + [shape] * 3 + [class_shape] * 3,
        in_specs=[SMEM_SPEC] + [v] * 9,
        out_specs=[SMEM_SPEC] * 2 + [v] * 6,
        scratch_shapes=[pltpu.VMEM(trained[0].shape, F32)],
        compiler_params=PARAMS,
    )(core, keep, got, terms, *trained, *classes)
    return tuple(out) + (first.T, second.T, third.T)


def after(value, *others):
    return lax.optimization_barrier((value,) + others)[0]


def reduce_all(layers, terms):
    width = layers[0].shape[1]
    core = lax.axis_index("vocab") % 2
    keep = jnp.where(core == 0, layers[0], layers[1])
    send = jnp.where(core == 0, layers[1], layers[0])
    got = swap(jnp.concatenate([send, terms], 1), "vocab", 1)
    keep, terms = keep + got[:, :width], terms + got[:, width:]
    for axis, start in (("vocab", 2), ("dp", 1)):
        size = lax.axis_size(axis)
        while start < size:
            masks = [start] if 2 * start >= size else [start, 2 * start, 3 * start]
            high = lax.reduce_precision(terms, 8, 7)
            middle = lax.reduce_precision(terms - high, 8, 7)
            mine = jnp.concatenate([lax.reduce_precision(keep, 8, 7), high, middle, terms - high - middle], 1)
            sent = mine.astype(BF)
            other = [swap(sent, axis, mask).astype(F32) for mask in masks]
            both = mine + other[0]
            if len(other) == 3:
                both = both + (other[1] + other[2])
            keep = both[:, :width]
            terms = both[:, width : width + 128] + (both[:, width + 128 : width + 256] + both[:, width + 256 :])
            start *= 2 * len(masks) - (2 if len(masks) == 3 else 0)
    return core, keep, swap(keep, "vocab", 1), terms


def body(
    input_token_ids,
    lengths,
    masked_positions,
    masked_token_targets,
    labels,
    token_embedding_table,
    position_table,
    norm_gain_table,
    query_key_value_weight,
    output_weight,
    up_weight,
    down_weight,
    adapter_inputs,
    adapter_down_input,
    head_dense_maps,
    adapter_outputs,
    class_projection,
    adapter_moment_first,
    adapter_moment_second,
    class_moment_first,
    class_moment_second,
):
    table_rows, width = token_embedding_table.shape
    seq_len = input_token_ids.shape[2]
    slots = masked_positions.shape[2]
    vocab_size = lax.axis_size("vocab")
    vocab_index = lax.axis_index("vocab")
    vocab_start = vocab_index * table_rows
    count = input_token_ids.shape[0] * input_token_ids.shape[1]
    picks = -(-(slots + 1) // 16) * 16
    rest = picks - slots

    own_lengths = lengths.reshape(count)
    own_labels = labels.reshape(count)
    own_positions = masked_positions.reshape(count, slots)
    packed = jnp.concatenate(
        [
            input_token_ids.reshape(count, seq_len),
            jnp.pad(masked_token_targets.reshape(count, slots), ((0, 0), (0, rest)), constant_values=-1),
            lengths.reshape(count, 1),
        ],
        1,
    )
    items = lax.all_gather(packed, "vocab", axis=0)
    order = list(range(0, vocab_size, 2)) + list(range(1, vocab_size, 2))
    items = lax.optimization_barrier(
        jnp.stack([lax.dynamic_index_in_dim(items, vocab_index ^ mask, 0, keepdims=False) for mask in order])
    )

    def own_rows(ids):
        local = ids - vocab_start
        inside = (local >= 0) & (local < table_rows)
        inside = inside[..., None]
        rows = jnp.take(token_embedding_table, jnp.clip(local, 0, table_rows - 1), axis=0)
        half = vocab_size // 2
        zero = jnp.zeros((), BF)
        return jnp.where(inside[:half], rows[:half], zero), jnp.where(inside[half:], rows[half:], zero)

    def core_sum(rows):
        sent = swap(rows[1], "vocab", 1)
        return [rows[0][mask] + sent[mask] for mask in range(vocab_size // 2)]

    def spread(own):
        return own[0], functools.reduce(
            jnp.add, [swap(own[mask], "vocab", 2 * mask) for mask in range(1, vocab_size // 2)]
        )

    a_all, a_down, b_all = adapter_tables(adapter_inputs, adapter_down_input, adapter_outputs)
    weights = (query_key_value_weight, output_weight, up_weight, down_weight, a_all, a_down, b_all)
    pick_index = jnp.concatenate(
        [own_positions, jnp.zeros((count, 1), jnp.int32), jnp.full((count, rest - 1), -1, jnp.int32)], 1
    ).reshape(-1, 1)
    own0 = core_sum(own_rows(items[:, 0, :seq_len]))
    second = jnp.concatenate([items[:, 1, :seq_len], items[:, 0, seq_len:-1], items[:, 1, seq_len:-1]], 1)

    def exchange(own, ids):
        return spread(own), own_rows(ids)

    (near0, far0), own1 = lax.cond(
        own_lengths[0] > 0,
        exchange,
        lambda own, ids: ((own[0], own[1]), (jnp.zeros((vocab_size // 2,) + ids.shape[1:] + (width,), BF),) * 2),
        own0,
        second,
    )
    near1, far1 = spread(core_sum(own1))
    picked0, saved_first = first_layer(
        own_lengths, pick_index, after(near0, near1), far0, position_table, norm_gain_table, weights
    )
    far1 = after(far1, picked0)
    saved_second, final, head, top = two_layers(
        own_lengths, pick_index, near1, far1, position_table, (picked0, saved_first[0]), norm_gain_table, weights,
        head_dense_maps,
    )

    z = head[0]
    near_z = [z] + [swap(z, "vocab", 2 * mask) for mask in range(1, vocab_size // 2)]
    far_z = [swap(x, "vocab", 1) for x in near_z]
    live_counts = jnp.minimum(items[:, :, -1] * 15 // 100, slots)
    near_sum, far_sum = table_pass(near_z + far_z, live_counts.reshape(-1), token_embedding_table)
    merged = merge(near_sum, swap(far_sum, "vocab", 1), vocab_size // 2)
    parts = [merged[0]] + [swap(merged[mask], "vocab", 2 * mask) for mask in range(1, vocab_size // 2)]
    label_rows = jnp.where(jnp.arange(picks)[None, :] == slots, own_labels[:, None], -1).reshape(-1, 1)
    live = jnp.arange(picks)[None, :] < own_lengths[:, None] * 15 // 100
    live = (live & (jnp.arange(picks)[None, :] < slots)).reshape(-1)

    layer0, layer1, terms = backward(
        parts, own_lengths, pick_index, near1, far1, live.astype(F32)[:, None], label_rows, class_projection.T, head,
        final, top, (saved_first, saved_second), norm_gain_table, weights, head_dense_maps,
    )
    core, keep, got, terms = reduce_all((layer0, layer1), terms)
    return tuple(
        update(
            core.reshape(1).astype(jnp.int32), keep, got, terms,
            (adapter_outputs, adapter_moment_first, adapter_moment_second),
            (class_projection, class_moment_first, class_moment_second),
        )
    )


def solution(mesh):
    split = P(None, ("dp", "vocab"), None)
    placed = (split, P(None, ("dp", "vocab")), split, split, P(None, ("dp", "vocab")), P("vocab", None)) + (P(),) * 15
    return jax.shard_map(body, mesh=mesh, in_specs=placed, out_specs=(P(),) * 8, check_vma=False)
```

```python
import functools

import jax
import jax.numpy as jnp
from jax import lax
from jax.experimental import pallas as pl
from jax.experimental.pallas import tpu as pltpu
from jax.sharding import PartitionSpec as P

HDIM = 64
STEP = 10
NORM_EPS = 1e-05
ADAPTER_SCALE = 2.0
NEG_FILL = -1e30
CLIP_AT = 0.001
RATE = 0.03
BETA_ONE = 0.9
BETA_TWO = 0.999
ADAM_EPS = 1e-08
DECAY = 0.01
BF = jnp.bfloat16
F32 = jnp.float32


def dot(left, right):
    return jnp.dot(left, right, preferred_element_type=F32)


def dot_nt(left, right):
    return lax.dot_general(left, right, (((1,), (1,)), ((), ())), preferred_element_type=F32)


def dot_tn(left, right):
    return lax.dot_general(left, right, (((0,), (0,)), ((), ())), preferred_element_type=F32)


def norm_parts(values):
    center = values - jnp.mean(values, -1, keepdims=True)
    spread = jnp.mean(center * center, -1, keepdims=True)
    rstd = lax.rsqrt(spread + NORM_EPS)
    return center * rstd, rstd


def norm_back(grad_hat, hat, rstd):
    first = jnp.mean(grad_hat, -1, keepdims=True)
    second = jnp.mean(grad_hat * hat, -1, keepdims=True)
    return rstd * (grad_hat - first - hat * second)


def gelu_both(values):
    root = 0.7978845608028654
    square = values * values
    bend = jnp.tanh(root * values * (1.0 + 0.044715 * square))
    half = 0.5 * (1.0 + bend)
    slope = half + 0.5 * values * (1.0 - bend * bend) * root * (1.0 + 0.134145 * square)
    return values * half, slope


def high_low(values):
    high = lax.reduce_precision(values, 8, 7)
    return high.astype(BF), (values - high).astype(BF)


def swap(value, axis, mask):
    size = lax.axis_size(axis)
    return lax.ppermute(value, axis, [(i, i ^ mask) for i in range(size)])


def adapter_tables(adapter_inputs, adapter_down_input, adapter_outputs):
    layers, width, columns = adapter_inputs.shape
    rank = adapter_down_input.shape[2]
    rows = adapter_inputs.transpose(0, 2, 1).reshape(layers, columns // rank, 1, rank, width)
    rows = jnp.broadcast_to(rows, (layers, columns // rank, 2, rank, width)).reshape(layers, 2 * columns, width)
    a_all = jnp.pad(rows, ((0, 0), (0, 128 - 2 * columns), (0, 0)))
    twice = jnp.concatenate([adapter_down_input, adapter_down_input], 2)
    a_down = jnp.pad(twice, ((0, 0), (0, 0), (2 * columns, 128 - 2 * columns - 2 * rank)))
    scaled = ADAPTER_SCALE * adapter_outputs
    high = lax.reduce_precision(scaled, 8, 7)
    return a_all, a_down, jnp.concatenate([high, scaled - high], 1).astype(BF)


def moment_update(weight, grad, first, second):
    first_new = BETA_ONE * first + (1.0 - BETA_ONE) * grad
    second_new = BETA_TWO * second + (1.0 - BETA_TWO) * grad * grad
    fix_one = 1.0 - BETA_ONE**STEP
    fix_two = 1.0 - BETA_TWO**STEP
    step_size = first_new / fix_one / (jnp.sqrt(second_new / fix_two) + ADAM_EPS)
    return (weight - RATE * (step_size + DECAY * weight), first_new, second_new)


VMEM_SPEC = pl.BlockSpec(memory_space=pltpu.VMEM)
SMEM_SPEC = pl.BlockSpec(memory_space=pltpu.SMEM)
ANY_SPEC = pl.BlockSpec(memory_space=pl.ANY)
PARAMS = pltpu.CompilerParams(vmem_limit_bytes=63 * 2**20)
CHUNK = 16
EXTRA = 128
ADAPTERS = 9


def chunked(rows, body, step=CHUNK):
    for start in range(0, rows, step):
        body(slice(start, start + step))


def lane_half():
    return lax.broadcasted_iota(jnp.int32, (1, 128), 1) < HDIM


def split_three(values):
    high = values.astype(BF)
    rest = values - high.astype(F32)
    middle = rest.astype(BF)
    return high, middle, (rest - middle.astype(F32)).astype(BF)


def lanes_of(parts):
    lane = lax.broadcasted_iota(jnp.int32, (1, 128), 1) % HDIM
    out = jnp.zeros((), BF)
    for i, part in reversed(list(enumerate(parts))):
        out = jnp.where(lane == i, part, out)
    return out


def key_extra(size, length):
    one = jnp.ones((), BF)
    mask = jnp.where(lax.broadcasted_iota(jnp.int32, (size, 1), 0) < length, 0.0, NEG_FILL)
    return lanes_of([one, one, one, jnp.broadcast_to(mask, (size, 128)).astype(BF)])


def attend_kernel(size, queries, items, score_ref, prob_ref):
    left = lane_half()
    lane = lax.broadcasted_iota(jnp.int32, (1, 128), 1)
    spots = [slice(i * queries, (i + 1) * queries) for i in range(len(items))]
    biases = []
    for length, *_, log_ref in items:
        biases.append(jnp.where(lax.broadcasted_iota(jnp.int32, (1, size), 1) < length, 0.0, NEG_FILL))
        log_ref[...] = jnp.zeros(log_ref.shape, BF)

    group = score_ref.shape[0] // 2
    zero, one = jnp.zeros((), BF), jnp.ones((), BF)

    def some(n, carry):
        for sub in range(group):
            scores(n * group + sub, 2 * sub)
        for sub in range(group):
            rest(n * group + sub, 2 * sub)
        return carry

    def scores(p, slot):
        cols = pl.ds(pl.multiple_of(p * 128, 128), 128)
        for spot, (_, q_at, k_at, _, _, _) in zip(spots, items):
            q = q_at(cols) * 0.125
            k_t = k_at(cols).T
            for half in range(2):
                own = left if half == 0 else ~left
                score_ref[slot + half, spot, :] = dot(jnp.where(own, q, zero), k_t)

    def rest(p, slot):
        cols = pl.ds(pl.multiple_of(p * 128, 128), 128)
        for spot, bias, (_, _, _, v_at, out_ref, log_ref) in zip(spots, biases, items):
            v = v_at(cols)
            outs, tops = [], []
            for half in range(2):
                own = left if half == 0 else ~left
                top = []
                for start in range(spot.start, spot.stop, CHUNK):
                    rows = slice(start, start + CHUNK)
                    score = score_ref[slot + half, rows, :] + bias
                    highest = jnp.max(score, -1, keepdims=True)
                    prob_ref[slot + half, rows, :] = jnp.exp(score - highest).astype(BF)
                    top.append(highest)
                outs.append(dot(prob_ref[slot + half, spot, :], jnp.where(own, v, one)))
                tops.append(jnp.concatenate(top, 0))
            total = pltpu.roll(jnp.where(left, outs[1], outs[0]), HDIM, 1)
            out_ref[:, cols] = (jnp.where(left, outs[0], outs[1]) / total).astype(BF)
            log = jnp.where(left, tops[0], tops[1]) + jnp.log(total)
            packed = log_ref[...]
            for half, value in enumerate((log, pltpu.roll(log, HDIM, 1))):
                for i, piece in enumerate(split_three(value)):
                    packed = jnp.where(lane == 6 * p + 3 * half + i, piece, packed)
            log_ref[...] = packed

    lax.fori_loop(0, items[0][4].shape[1] // 128 // group, some, 0)


def attend_back_kernel(size, queries, items, score_ref, grad_ref, prob_ref, ds_ref):
    left = lane_half()
    one = jnp.ones((), BF)
    v_extra = lanes_of([one, one, one])
    lane = lax.broadcasted_iota(jnp.int32, (1, 128), 1)
    row = lax.broadcasted_iota(jnp.int32, (128, 128), 0)
    col = lax.broadcasted_iota(jnp.int32, (128, 128), 1)
    across = jnp.where((row < HDIM) != left, 1.0, 0.0).astype(BF)
    group = 1
    k_extras = [key_extra(size, item[0]) for item in items]

    def some(n, carry):
        for sub in range(group):
            scores(n * group + sub, places(sub))
        for sub in range(group):
            rest(n * group + sub, places(sub))
        return carry

    def places(sub):
        starts = [(sub * len(items) + i) * 128 for i in range(len(items))]
        return [slice(start, start + queries) for start in starts]

    def scores(p, spots):
        cols = pl.ds(pl.multiple_of(p * 128, 128), 128)
        place = jnp.where(
            (col < 3) & (row == 6 * p + 3 + col) | (col >= HDIM) & (col < HDIM + 3) & (row == 6 * p + col - HDIM),
            -1.0,
            0.0,
        ).astype(BF)
        for spot, k_extra, (_, q_at, k_at, v_at, o_at, g_at, log_ref, *_) in zip(spots, k_extras, items):
            q = q_at(cols) * 0.125
            k, v, g = k_at(cols), v_at(cols), g_at(cols)
            q_extra = jnp.where(lane % HDIM == 3, one, dot(log_ref[...], place).astype(BF))
            product = g.astype(F32) * o_at(cols).astype(F32)
            high = product.astype(BF)
            low = (product - high.astype(F32)).astype(BF)
            g_extra = lanes_of([-x for x in split_three(dot(high, across) + dot(low, across))])
            for half in range(2):
                own = left if half == 0 else ~left
                score_ref[half, :, spot] = dot_nt(jnp.where(own, k, k_extra), jnp.where(own, q, q_extra))
                grad_ref[half, :, spot] = dot_nt(jnp.where(own, v, v_extra), jnp.where(own, g, g_extra))

    def rest(p, spots):
        cols = pl.ds(pl.multiple_of(p * 128, 128), 128)
        for spot, (_, q_at, k_at, _, _, g_at, _, dq_ref, dk_ref, dv_ref) in zip(spots, items):
            q = q_at(cols) * 0.125
            k, g = k_at(cols), g_at(cols)
            d_q, d_k, d_v = [], [], []
            for half in range(2):
                for start in range(0, size, CHUNK):
                    rows = slice(start, start + CHUNK)
                    prob = jnp.exp(score_ref[half, rows, spot])
                    prob_ref[half, rows, spot] = prob.astype(BF)
                    ds_ref[half, rows, spot] = (prob * grad_ref[half, rows, spot]).astype(BF)
                d_scores = ds_ref[half, :, spot]
                d_v.append(dot(prob_ref[half, :, spot], g))
                d_k.append(dot(d_scores, q))
                d_q.append(dot_tn(d_scores, k))
            dq_ref[:, cols] = (jnp.where(left, d_q[0], d_q[1]) * 0.125).astype(BF)
            dk_ref[:, cols] = jnp.where(left, d_k[0], d_k[1]).astype(BF)
            dv_ref[:, cols] = jnp.where(left, d_v[0], d_v[1]).astype(BF)

    lax.fori_loop(0, items[0][7].shape[1] // 128 // group, some, 0)


def weight_loads(hbm, width, sems, wqkv, wo, wu, wd, bd, layer=0):
    wqkv_hbm, wo_hbm, wu_hbm, wd_hbm, ad_hbm, b_hbm = hbm
    pieces = {}
    if wqkv is not None:
        pieces["qkv"] = 0, [(wqkv_hbm.at[layer], wqkv.at[:width, :])] + [
            (b_hbm.at[layer, :, pl.ds(i * width, width)], wqkv.at[pl.ds(width + 16 * i, 16), pl.ds(i * width, width)])
            for i in range(3)
        ]
    pieces["o"] = 4, [
        (wo_hbm.at[layer], wo.at[:width, :]),
        (b_hbm.at[layer, :, pl.ds(3 * width, width)], wo.at[pl.ds(width + 48, 16), :]),
    ]
    pieces["down"] = 6, [
        (wd_hbm.at[layer], wd.at[:, :width]),
        (ad_hbm.at[layer], wd.at[:, width:]),
        (b_hbm.at[layer, :, pl.ds(4 * width, width)], bd.at[pl.ds(80, 16), :]),
    ]
    pieces["up"] = 9, [
        (wu_hbm.at[layer], wu.at[:width, :]),
        (b_hbm.at[layer, :, pl.ds(5 * width, wu.shape[1])], wu.at[pl.ds(width + 64, 16), :]),
    ]
    return {
        name: [
            pltpu.make_async_copy(source, target, sems.at[first + n]) for n, (source, target) in enumerate(copies)
        ]
        for name, (first, copies) in pieces.items()
    }


def clear_rows(width, wqkv, wo, wu, bd):
    for ref in (wqkv, wo, wu):
        ref[width:, :] = jnp.zeros((EXTRA, ref.shape[1]), BF)
    bd[...] = jnp.zeros(bd.shape, BF)


def start_all(loads):
    for load in loads:
        load.start()


def wait_all(loads):
    for load in loads:
        load.wait()


def merge_inner(inner, inners):
    lane = lax.broadcasted_iota(jnp.int32, (1, 128), 1) // 16
    return jnp.where(
        lane < 3, inner, jnp.where(lane == 3, inners[0], jnp.where(lane == 4, inners[1], inners[2]))
    )


def upper_kernel(size, width, wide, gain_ref, gain, hidden, attn, x_ref, sum_ref, part, active, slope, wo, wu, wd,
                 a_ref, bd_ref, waits, hat1_ref, rstd1_ref, rstd2_ref, slope_done):
    inner_o = dot_nt(attn[:, :width], a_ref[...]).astype(BF)
    attn[:, width:] = inner_o
    waits("o")
    sum_ref[...] = dot(attn[...], wo[...])

    def middle(r):
        hat, rstd = norm_parts(hidden[r, :] + sum_ref[r, :])
        value = hat * gain_ref[gain : gain + 1, :]
        hidden[r, :] = value
        x_ref[r, :width] = value.astype(BF)
        hat1_ref[r, :] = hat.astype(BF)
        rstd1_ref[r, :] = jnp.broadcast_to(rstd, (CHUNK, 128))

    chunked(size, middle)
    inner_u = dot_nt(x_ref[:, :width], a_ref[...]).astype(BF)
    x_ref[:, width:] = inner_u
    waits("up")
    waits("down")
    steps = wide // width

    def upper(j):
        part[j % 2] = dot(x_ref[...], wu[:, j * width : (j + 1) * width])

    total = None
    upper(0)
    for j in range(steps):
        if j + 1 < steps:
            upper(j + 1)
        cols = slice(j * width, (j + 1) * width)

        def bend(r):
            value, rise = gelu_both(part[j % 2, r, :])
            active[j % 2, r, :] = value.astype(BF)
            slope[r, cols] = rise.astype(BF)

        chunked(size, bend)
        down = dot(active[j % 2], wd[cols, :])
        if j == 0:
            sum_ref[...] = down[:, :width]
            total = down[:, width:]
        else:
            sum_ref[...] += down[:, :width]
            total = total + down[:, width:]
    slope_done()
    inner_d = total.astype(BF)
    sum_ref[...] += dot(inner_d, bd_ref[...])

    def last(r):
        hat, rstd = norm_parts(hidden[r, :] + sum_ref[r, :])
        hidden[r, :] = hat * gain_ref[gain + 1 : gain + 2, :]
        rstd2_ref[r, :] = jnp.broadcast_to(rstd, (CHUNK, 128))

    chunked(size, last)
    return inner_o, inner_u, inner_d


def first_run(
    length, near_ref, far_ref, pos_ref, gain_ref, loads, freed, a_ref, bd_ref, qkv_done, attn_done, slope_done,
    log_ref, inner_ref, hat1_ref, rstd1_ref, rstd2_ref,
    wqkv, wo, wu, wd, hidden, x_ref, qkv, attn, sum_ref, part, active, slope, score, prob,
):
    size, width = pos_ref.shape
    wide = wu.shape[1]

    def embed(r):
        rows = near_ref[r, :].astype(F32) + far_ref[r, :].astype(F32)
        hat, _ = norm_parts(rows + pos_ref[r, :].astype(F32))
        value = hat * gain_ref[0:1, :]
        hidden[r, :] = value
        x_ref[r, :width] = value.astype(BF)

    chunked(size, embed)
    inner = dot_nt(x_ref[:, :width], a_ref[...]).astype(BF)
    x_ref[:, width:] = inner
    wait_all(loads["qkv"])
    for i in range(3):
        cols = slice(i * width, (i + 1) * width)
        qkv[:, cols] = dot(x_ref[...], wqkv[:, cols]).astype(BF)
    freed("qkv")
    qkv_done()
    item = (
        length,
        lambda c: qkv[:, c],
        lambda c: qkv[:, pl.ds(c.start + width, 128)],
        lambda c: qkv[:, pl.ds(c.start + 2 * width, 128)],
        attn.at[:, pl.ds(0, width)],
        log_ref,
    )
    attend_kernel(size, size, [item], score, prob)
    attn_done()
    inners = upper_kernel(
        size, width, wide, gain_ref, 1, hidden, attn, x_ref, sum_ref, part, active, slope, wo, wu, wd, a_ref, bd_ref,
        lambda name: wait_all(loads[name]), hat1_ref, rstd1_ref, rstd2_ref, slope_done,
    )
    for name in ("o", "up", "down"):
        freed(name)
    inner_ref[...] = merge_inner(inner, inners)


def pick_rows(pick_ref, r, hidden, high_ref, size):
    lows = []
    for start in range(0, size, 128):
        s = slice(start, start + 128)
        value = hidden[s, :]
        high = value.astype(BF)
        high_ref[s, :] = high
        lows.append((value - high.astype(F32)).astype(BF))
    hot = (pick_ref[r, :] == lax.broadcasted_iota(jnp.int32, (1, size), 1)).astype(BF)
    return dot(hot, high_ref[...]) + dot(hot, jnp.concatenate(lows, 0))


def first_layer_kernel(
    length_ref, pick_ref, near_ref, far_ref, pos_ref, gain_ref, wqkv_hbm, wo_hbm, wu_hbm, wd_hbm, ad_hbm, b_hbm, a_ref,
    picked_ref, high_ref, qkv_hbm, log_ref, attn_hbm, inner_ref, hat1_ref, rstd1_ref, slope_hbm, rstd2_ref,
    wqkv, wo, wu, wd, bd_ref, hidden, x_ref, qkv, attn, sum_ref, part, active, slope, score, prob, sems,
):
    size, width = near_ref.shape
    hbm = (wqkv_hbm, wo_hbm, wu_hbm, wd_hbm, ad_hbm, b_hbm)
    loads = weight_loads(hbm, width, sems, wqkv, wo, wu, wd, bd_ref)
    a_ref = a_ref.at[0]
    clear_rows(width, wqkv, wo, wu, bd_ref)
    for name in ("qkv", "o", "up", "down"):
        start_all(loads[name])
    stores = [
        pltpu.make_async_copy(qkv, qkv_hbm, sems.at[11]),
        pltpu.make_async_copy(attn.at[:, pl.ds(0, width)], attn_hbm, sems.at[12]),
        pltpu.make_async_copy(slope, slope_hbm, sems.at[13]),
    ]
    first_run(
        length_ref[0], near_ref, far_ref, pos_ref, gain_ref, loads, lambda name: None, a_ref, bd_ref, stores[0].start,
        stores[1].start, stores[2].start, log_ref, inner_ref, hat1_ref, rstd1_ref, rstd2_ref,
        wqkv, wo, wu, wd, hidden, x_ref, qkv, attn, sum_ref, part, active, slope, score, prob,
    )
    picked_ref[...] = pick_rows(pick_ref, slice(0, picked_ref.shape[0]), hidden, high_ref, size)
    wait_all(stores)


def saved_shapes(size, width, wide):
    return [
        ((size, width), BF), ((size, 3 * width), BF), ((size, 128), BF), ((size, width), BF),
        ((size, 128), BF), ((size, width), BF), ((size, 128), F32), ((size, wide), BF), ((size, 128), F32),
    ]


def saved_specs():
    v, a = VMEM_SPEC, ANY_SPEC
    return [v, a, v, a, v, v, v, a, v]


def first_scratch(size, width, wide):
    return [
        pltpu.VMEM((width + EXTRA, 3 * width), BF), pltpu.VMEM((width + EXTRA, width), BF),
        pltpu.VMEM((width + EXTRA, wide), BF), pltpu.VMEM((wide, width + EXTRA), BF), pltpu.VMEM((EXTRA, width), BF),
        pltpu.VMEM((size, width), F32), pltpu.VMEM((size, width + EXTRA), BF),
        pltpu.VMEM((size, 3 * width), BF),
        pltpu.VMEM((size, width + EXTRA), BF), pltpu.VMEM((size, width), F32),
        pltpu.VMEM((2, size, width), F32), pltpu.VMEM((2, size, width), BF), pltpu.VMEM((size, wide), BF),
        pltpu.VMEM((2, size, size), F32), pltpu.VMEM((2, size, size), BF),
    ]


def first_layer(lengths, picks, near, far, positions, gains, weights):
    wqkv, wo, wu, wd, a_all, a_down, b_all = weights
    size, width = positions.shape
    wide = wu.shape[2]
    count = lengths.shape[0]
    shapes = [((picks.shape[0] // count, width), F32)] + saved_shapes(size, width, wide)
    v, a = VMEM_SPEC, ANY_SPEC
    picked, *saved = pl.pallas_call(
        first_layer_kernel,
        out_shape=[jax.ShapeDtypeStruct(*s) for s in shapes],
        in_specs=[SMEM_SPEC] + [v] * 5 + [a] * 6 + [v],
        out_specs=[v] + saved_specs(),
        scratch_shapes=first_scratch(size, width, wide) + [pltpu.SemaphoreType.DMA((14,))],
        compiler_params=PARAMS,
    )(lengths, picks, near, far, positions, gains, wqkv, wo, wu, wd, a_down, b_all, a_all)
    return picked, tuple(saved)


def upper_back_kernel(size, width, wide, inner_t, grad_at, gain_ref, gain, high_ref, rstd2_ref, slope, hat1_ref, rstd1_ref,
                      wo, wu, wd, a_ref, bd_ref, out_ref, waits, grad2, x_ref, sum_ref, part, active, grad1_at, more=False):
    def second(r):
        scale = gain_ref[gain + 1 : gain + 2, :]
        value = norm_back(grad_at(r) * scale, high_ref[r, :].astype(F32) * (1.0 / scale), rstd2_ref[r, 0:1])
        grad2[r, :] = value
        x_ref[r, :width] = value.astype(BF)

    def put(cols, value):
        out_ref[:, cols] = out_ref[:, cols] + value if more else value

    chunked(size, second)
    low = x_ref[:, :width]
    waits("down")
    x_ref[:, width:] = dot_nt(low, bd_ref[...]).astype(BF)
    put(slice(4 * width, 5 * width), ADAPTER_SCALE * dot(inner_t[80:96], low)[:8])
    waits("up")
    steps = wide // width

    def inward(j):
        part[j % 2] = dot_nt(x_ref[...], wd[j * width : (j + 1) * width, :])

    total = None
    inward(0)
    for j in range(steps):
        if j + 1 < steps:
            inward(j + 1)
        cols = slice(j * width, (j + 1) * width)

        def bend(r):
            active[j % 2, r, :] = (part[j % 2, r, :] * slope[r, cols].astype(F32)).astype(BF)

        chunked(size, bend)
        piece = dot_nt(active[j % 2], wu[:, cols])
        put(slice((5 + j) * width, (6 + j) * width), ADAPTER_SCALE * dot(inner_t[64:80], active[j % 2])[:8])
        if j == 0:
            sum_ref[...] = piece[:, :width]
            total = piece[:, width:]
        else:
            sum_ref[...] += piece[:, :width]
            total = total + piece[:, width:]
    sum_ref[...] += dot(total.astype(BF), a_ref[...])

    def first(r):
        value = norm_back(
            (grad2[r, :] + sum_ref[r, :]) * gain_ref[gain : gain + 1, :], hat1_ref[r, :].astype(F32), rstd1_ref[r, 0:1]
        )
        x_ref[r, :width] = value.astype(BF)
        if grad1_at is not None:
            grad1_at[r, :] = value

    chunked(size, first)
    low = x_ref[:, :width]
    waits("o")
    both = dot_nt(low, wo[...])
    put(slice(3 * width, 4 * width), ADAPTER_SCALE * dot(inner_t[48:64], low)[:8])
    return (both[:, :width] + dot(both[:, width:].astype(BF), a_ref[...])).astype(BF)


def two_layers_kernel(
    length_ref, pick_ref, near_ref, far_ref, pos_ref, picked0_ref, high0_ref, gain_ref,
    wqkv_hbm, wo_hbm, wu_hbm, wd_hbm, ad_hbm, b_hbm, map_hbm, a_ref,
    high1_ref, qkv_hbm, log_ref, attn_hbm, inner_ref, hat1_ref, rstd1_ref, slope_hbm, rstd2_ref,
    final_ref, z_ref, head_hat_ref, head_rstd_ref, head_slope_ref,
    q_ref, kv_hbm, top_log_ref, attn_out_ref, top_inner_ref, inner_kv_ref, top_hat1_ref, top_rstd1_ref, top_slope,
    top_rstd2_ref,
    wqkv, wo, wu, wd, bd_ref, hidden, x_ref, qkv, attn, sum_ref, part, active, slope, score, prob, map_ref, x_kv, kv,
    sems,
):
    count = kv.shape[0]
    size, width = pos_ref.shape
    rows = final_ref.shape[0]
    a0_ref, a1_ref = a_ref.at[0], a_ref.at[1]
    picks = rows // count
    wide = wu.shape[1]
    hbm = (wqkv_hbm, wo_hbm, wu_hbm, wd_hbm, ad_hbm, b_hbm)
    loads = weight_loads(hbm, width, sems, wqkv, wo, wu, wd, bd_ref)
    later = weight_loads(hbm, width, sems, wqkv, wo, wu, wd, bd_ref, 1)
    clear_rows(width, wqkv, wo, wu, bd_ref)
    load_map = pltpu.make_async_copy(map_hbm.at[0], map_ref, sems.at[15])
    for name in ("qkv", "o", "up", "down"):
        start_all(loads[name])
    load_map.start()
    stores = [
        pltpu.make_async_copy(qkv, qkv_hbm, sems.at[11]),
        pltpu.make_async_copy(attn.at[:, pl.ds(0, width)], attn_hbm, sems.at[12]),
        pltpu.make_async_copy(slope, slope_hbm, sems.at[13]),
        pltpu.make_async_copy(kv, kv_hbm, sems.at[14]),
    ]
    first_run(
        length_ref[1], near_ref, far_ref, pos_ref, gain_ref, loads, lambda name: start_all(later[name]), a0_ref, bd_ref,
        stores[0].start, stores[1].start, stores[2].start, log_ref, inner_ref, hat1_ref, rstd1_ref, rstd2_ref,
        wqkv, wo, wu, wd, hidden, x_ref, qkv, attn, sum_ref, part, active, slope, score, prob,
    )
    picked = [picked0_ref[...], pick_rows(pick_ref, slice(picks, rows), hidden, high1_ref, size)]
    stores[1].wait()
    top_hidden, top_x, top_attn = hidden.at[pl.ds(0, rows)], x_ref.at[pl.ds(0, rows)], attn.at[pl.ds(0, rows)]
    top_sum = sum_ref.at[pl.ds(0, rows)]
    for i, high_ref in enumerate((high0_ref, high1_ref)):
        r = slice(i * picks, (i + 1) * picks)
        hidden[r, :] = picked[i]
        x_ref[r, :width] = picked[i].astype(BF)
        x_kv[i, :, :width] = high_ref[...]
        inner_kv = dot_nt(high_ref[...], a1_ref[...]).astype(BF)
        inner_kv_ref[i] = inner_kv
        x_kv[i, :, width:] = inner_kv
    inner = dot_nt(top_x[:, :width], a1_ref[...]).astype(BF)
    x_ref[:rows, width:] = inner
    wait_all(later["qkv"])
    q_ref[...] = dot(top_x[...], wqkv[:, :width]).astype(BF)
    for i in range(count):
        for j in range(2):
            kv[i, :, j * width : (j + 1) * width] = dot(
                x_kv[i], wqkv[:, (j + 1) * width : (j + 2) * width]
            ).astype(BF)
    stores[3].start()
    items = [
        (
            length_ref[i],
            lambda c, i=i: q_ref[i * picks : (i + 1) * picks, c],
            lambda c, i=i: kv[i, :, c],
            lambda c, i=i: kv[i, :, pl.ds(c.start + width, 128)],
            attn.at[pl.ds(i * picks, picks), pl.ds(0, width)],
            top_log_ref.at[pl.ds(i * picks, picks)],
        )
        for i in range(count)
    ]
    attend_kernel(size, picks, items, score, prob)
    attn_out_ref[...] = attn[:rows, :width]
    inners = upper_kernel(
        rows, width, wide, gain_ref, 3, top_hidden, top_attn, top_x, top_sum, part.at[:, pl.ds(0, rows)],
        active.at[:, pl.ds(0, rows)], top_slope, wo, wu, wd, a1_ref, bd_ref, lambda name: wait_all(later[name]),
        top_hat1_ref, top_rstd1_ref, top_rstd2_ref, lambda: None,
    )
    top_inner_ref[...] = merge_inner(inner, inners)
    final_ref[...] = hidden[:rows, :].astype(BF)
    load_map.wait()
    sum_ref[:rows, :] = dot(final_ref[...], map_ref[...])

    def head(r):
        value, rise = gelu_both(sum_ref[r, :])
        hat, rstd = norm_parts(value)
        head_slope_ref[r, :] = rise
        head_hat_ref[r, :] = hat
        head_rstd_ref[r, :] = jnp.broadcast_to(rstd, (CHUNK, 128))
        z_ref[r, :] = (hat * gain_ref[5:6, :]).astype(BF)

    chunked(rows, head)
    stores[0].wait()
    stores[2].wait()
    stores[3].wait()


def two_layers(lengths, picks, near, far, positions, first, gains, weights, maps):
    wqkv, wo, wu, wd, a_all, a_down, b_all = weights
    picked0, high0 = first
    size, width = positions.shape
    wide = wu.shape[2]
    count = 2
    total = picks.shape[0]
    shapes = saved_shapes(size, width, wide) + [
        ((total, width), BF), ((total, width), BF), ((total, width), F32), ((total, 128), F32), ((total, width), F32),
        ((total, width), BF), ((count, size, 2 * width), BF), ((total, 128), BF), ((total, width), BF),
        ((total, 128), BF), ((count, size, 128), BF), ((total, width), BF), ((total, 128), F32), ((total, wide), BF),
        ((total, 128), F32),
    ]
    v, a = VMEM_SPEC, ANY_SPEC
    out = pl.pallas_call(
        two_layers_kernel,
        out_shape=[jax.ShapeDtypeStruct(*s) for s in shapes],
        in_specs=[SMEM_SPEC] + [v] * 7 + [a] * 7 + [v],
        out_specs=saved_specs() + [v] * 6 + [a] + [v] * 8,
        scratch_shapes=first_scratch(size, width, wide) + [
            pltpu.VMEM((width, width), BF), pltpu.VMEM((count, size, width + EXTRA), BF),
            pltpu.VMEM((count, size, 2 * width), BF), pltpu.SemaphoreType.DMA((16,)),
        ],
        compiler_params=PARAMS,
    )(lengths, picks, near, far, positions, picked0, high0, gains, wqkv, wo, wu, wd, a_down, b_all, maps, a_all)
    return tuple(out[:9]), out[9], tuple(out[10:14]), tuple(out[14:])


def backward_kernel(part_count, *refs):
    backward_run(refs[:part_count], *refs[part_count:])


def backward_run(
    part_refs, length_ref, pick_ref, near_ref, far_ref, live_ref, label_ref, projection_ref, gain_ref,
    z_ref, head_hat_ref, head_rstd_ref, head_slope_ref, final_ref,
    q_ref, kv_hbm, log_ref, attn_ref, inner_ref, inner_kv_ref, hat1_ref, rstd1_ref, slope, rstd2_ref,
    high0_hbm, qkv0_hbm, log0_hbm, attn0_hbm, inner0_hbm, hat0_hbm, rstd0_hbm, slope0_hbm, rrstd0_hbm,
    high1_hbm, qkv1_hbm, log1_hbm, attn1_hbm, inner1_hbm, hat1_hbm, rstd1_hbm, slope1_hbm, rrstd1_hbm,
    wqkv_hbm, wo_hbm, wu_hbm, wd_hbm, ad_hbm, b_hbm, map_hbm, a_ref,
    layer0_ref, layer1_ref, term_ref,
    wqkv, wo, wu, wd, bd_ref, kv, grads, grad1, grad2, x_ref, sum_ref, part, active, d_attn, dq, dkv,
    score, dscore, prob, ds, s_high, s_log, s_attn, s_inner, s_hat1, s_rstd1, s_slope, s_rstd2, sems,
):
    count, size, _ = kv.shape
    rows, width = z_ref.shape
    picks = rows // count
    wide = wu.shape[1]
    hbm = (wqkv_hbm, wo_hbm, wu_hbm, wd_hbm, ad_hbm, b_hbm)
    loads = weight_loads(hbm, width, sems, wqkv, wo, wu, wd, bd_ref, 1)
    lower = weight_loads(hbm, width, sems, None, wo, wu, wd, bd_ref, 0)
    clear_rows(width, wqkv, wo, wu, bd_ref)
    map_refs = [wqkv.at[pl.ds(0, width), pl.ds(i * width, width)] for i in range(2)]
    loads["map"] = [pltpu.make_async_copy(map_hbm.at[i], map_refs[i], sems.at[22 + i]) for i in range(2)]
    loads["kv"] = [pltpu.make_async_copy(kv_hbm, kv, sems.at[11])]
    total_width = ADAPTERS * width
    adapter0_ref, adapter1_ref = (x.at[:, pl.ds(0, total_width)] for x in (layer0_ref, layer1_ref))
    class_out_ref = layer0_ref.at[:, pl.ds(total_width, width + EXTRA)]
    layer1_ref[:, total_width:] = jnp.zeros((8, width + EXTRA), F32)
    a0_ref, a1_ref = a_ref.at[0], a_ref.at[1]
    first_target = near_ref.shape[0] - rows
    kept = (s_high, None, s_log, s_attn, s_inner, s_hat1, s_rstd1, s_slope, s_rstd2)
    items = []
    for source_refs in (
        (high0_hbm, qkv0_hbm, log0_hbm, attn0_hbm, inner0_hbm, hat0_hbm, rstd0_hbm, slope0_hbm, rrstd0_hbm),
        (high1_hbm, qkv1_hbm, log1_hbm, attn1_hbm, inner1_hbm, hat1_hbm, rstd1_hbm, slope1_hbm, rrstd1_hbm),
    ):
        copies = [
            pltpu.make_async_copy(source, target, sems.at[12 + n])
            for n, (source, target) in enumerate(zip(source_refs, kept))
            if target is not None
        ]
        qkv_hbm = source_refs[1]
        copies.append(pltpu.make_async_copy(qkv_hbm.at[:, pl.ds(0, 2 * width)], kv.at[0], sems.at[13]))
        copies.append(
            pltpu.make_async_copy(
                qkv_hbm.at[:, pl.ds(2 * width, width)], kv.at[1, :, pl.ds(0, width)], sems.at[21]
            )
        )
        items.append(copies)
    early, late = (0, 3, 4, 5, 6, 7), (1, 2, 8, 9)
    for name in ("map", "down", "up", "o", "kv"):
        start_all(loads[name])
    for n in early:
        items[0][n].start()
    part_rows = pl.ds(0, rows)

    def head(r):
        live = live_ref[r, :]
        t = slice(first_target + r.start, first_target + r.stop)
        target = near_ref[t, :].astype(F32) + far_ref[t, :].astype(F32)
        mean, log_total = mean_of(part_refs, r, width)
        logit = jnp.sum(z_ref[r, :].astype(F32) * target, -1, keepdims=True)
        losses.append(jnp.sum(jnp.where(live > 0.0, log_total - logit, 0.0), 0, keepdims=True))
        lives.append(jnp.sum(live, 0, keepdims=True))
        grad_z = jnp.where(live > 0.0, mean - target, 0.0)
        value = norm_back(grad_z * gain_ref[5:6, :], head_hat_ref[r, :], head_rstd_ref[r, 0:1])
        x_ref[r, :width] = (value * head_slope_ref[r, :]).astype(BF)

    wait_all(loads["map"])
    class_part, class_loss = class_head(label_ref, final_ref, map_refs[1], projection_ref, class_out_ref)
    losses, lives = [class_loss], [jnp.full((1, 1), count, F32)]
    chunked(rows, head)
    lane = lax.broadcasted_iota(jnp.int32, (8, 128), 1)
    term_ref[...] = jnp.where(lane == 0, functools.reduce(jnp.add, losses), functools.reduce(jnp.add, lives))
    grads[0, :rows, :] = dot_nt(x_ref[:rows, :width], map_refs[0][...]) + class_part
    start_all(loads["qkv"])
    inner_t = inner_ref[...].T
    d_attn[:rows, :] = upper_back_kernel(
        rows, width, wide, inner_t, lambda r: grads[0, r, :], gain_ref, 3, final_ref, rstd2_ref, slope, hat1_ref,
        rstd1_ref, wo, wu, wd, a1_ref, bd_ref, adapter1_ref, lambda name: wait_all(loads[name]),
        grad2.at[part_rows], x_ref.at[part_rows], sum_ref.at[part_rows], part.at[:, part_rows],
        active.at[:, part_rows], grad1,
    )
    for name in ("down", "up", "o"):
        start_all(lower[name])
    wait_all(loads["kv"])
    both_items = [
        (
            length_ref[i],
            lambda c, i=i: q_ref[i * picks : (i + 1) * picks, c],
            lambda c, i=i: kv[i, :, c],
            lambda c, i=i: kv[i, :, pl.ds(c.start + width, 128)],
            lambda c, i=i: attn_ref[i * picks : (i + 1) * picks, c],
            lambda c, i=i: d_attn[i * picks : (i + 1) * picks, c],
            log_ref.at[pl.ds(i * picks, picks)],
            dq.at[pl.ds(i * picks, picks)],
            dkv.at[i, :, pl.ds(0, width)],
            dkv.at[i, :, pl.ds(width, width)],
        )
        for i in range(count)
    ]
    attend_back_kernel(size, picks, both_items, score, dscore, prob, ds)
    for n in late:
        items[0][n].start()
    wait_all(loads["qkv"])
    both = dot_nt(dq[:rows, :], wqkv[:, :width])
    grad1[...] += both[:, :width] + dot(both[:, width:].astype(BF), a1_ref[...])
    adapter1_ref[:, :width] = ADAPTER_SCALE * dot(inner_t[0:16], dq[:rows, :])[:8]
    total = None
    for i in range(count):
        r = slice(i * picks, (i + 1) * picks)
        hot = (pick_ref[r, :] == lax.broadcasted_iota(jnp.int32, (1, size), 1)).astype(BF)
        value = grad1[r, :]
        high = value.astype(BF)
        low = (value - high.astype(F32)).astype(BF)
        both = dot_nt(dkv[i], wqkv[:, width:])
        grads[i] = (
            both[:, :width]
            + dot(both[:, width:].astype(BF), a1_ref[...])
            + dot_tn(jnp.concatenate([hot, hot], 0), jnp.concatenate([high, low], 0))
        )
        piece = dot(inner_kv_ref[i].T[16:48], dkv[i])
        total = piece if total is None else total + piece
    adapter1_ref[:, width : 2 * width] = ADAPTER_SCALE * total[0:8, :width]
    adapter1_ref[:, 2 * width : 3 * width] = ADAPTER_SCALE * total[16:24, width:]

    for i in range(count):
        for n in early:
            items[i][n].wait()
        inner_t = s_inner[...].T
        d_attn[...] = upper_back_kernel(
            size, width, wide, inner_t, lambda r: grads[i, r, :], gain_ref, 1, s_high, s_rstd2, s_slope, s_hat1,
            s_rstd1, wo, wu, wd, a0_ref, bd_ref, adapter0_ref,
            lambda name: wait_all(lower[name]) if i == 0 else None, grad2, x_ref, sum_ref, part, active, None, i > 0,
        )
        if i + 1 < count:
            for n in early:
                items[i + 1][n].start()
        for n in late:
            items[i][n].wait()
        item = (
            length_ref[i],
            lambda c: kv[0, :, c],
            lambda c: kv[0, :, pl.ds(c.start + width, 128)],
            lambda c: kv[1, :, c],
            lambda c: s_attn[:, c],
            lambda c: d_attn[:, c],
            s_log,
            dq,
            dkv.at[0, :, pl.ds(0, width)],
            dkv.at[0, :, pl.ds(width, width)],
        )
        attend_back_kernel(size, size, [item], score, dscore, prob, ds)
        if i + 1 < count:
            for n in late:
                items[i + 1][n].start()
        for j, value in enumerate((dq[...], dkv[0, :, :width], dkv[0, :, width:])):
            cols = slice(j * width, (j + 1) * width)
            piece = ADAPTER_SCALE * dot(inner_t[16 * j : 16 * j + 16], value)[:8]
            adapter0_ref[:, cols] = piece if i == 0 else adapter0_ref[:, cols] + piece


def backward(parts, lengths, picks, near, far, live, labels, projection, head, final, top, saved, gains, weights, maps):
    wqkv, wo, wu, wd, a_all, a_down, b_all = weights
    kv = top[1]
    rows, width = final.shape
    count, size, _ = kv.shape
    wide = wu.shape[2]
    v, a = VMEM_SPEC, ANY_SPEC
    low = pltpu.VMEM((size, width), BF)
    full = pltpu.VMEM((size, width), F32)
    layer = jax.ShapeDtypeStruct((8, b_all.shape[2] + width + EXTRA), F32)
    return pl.pallas_call(
        functools.partial(backward_kernel, len(parts)),
        out_shape=[layer, layer, jax.ShapeDtypeStruct((8, 128), F32)],
        in_specs=[v] * len(parts) + [SMEM_SPEC] + [v] * 13 + [a] + [v] * 8 + [a] * 18 + [a] * 7 + [v],
        out_specs=[v] * 3,
        scratch_shapes=[
            pltpu.VMEM((width + EXTRA, 3 * width), BF), pltpu.VMEM((width + EXTRA, width), BF),
            pltpu.VMEM((width + EXTRA, wide), BF), pltpu.VMEM((wide, width + EXTRA), BF), pltpu.VMEM((EXTRA, width), BF),
            pltpu.VMEM(kv.shape, BF),
            pltpu.VMEM((count, size, width), F32), pltpu.VMEM((rows, width), F32), full,
            pltpu.VMEM((size, width + EXTRA), BF), full, pltpu.VMEM((2, size, width), F32),
            pltpu.VMEM((2, size, width), BF), low, low, pltpu.VMEM(kv.shape, BF),
            pltpu.VMEM((2, size, size), F32), pltpu.VMEM((2, size, size), F32),
            pltpu.VMEM((2, size, size), BF), pltpu.VMEM((2, size, size), BF),
        ] + [pltpu.VMEM(*s) for n, s in enumerate(saved_shapes(size, width, wide)) if n != 1] + [
            pltpu.SemaphoreType.DMA((24,))
        ],
        compiler_params=PARAMS,
    )(*parts, lengths, picks, near, far, live, labels, projection, gains, *head, final, *top, *saved[0], *saved[1],
      wqkv, wo, wu, wd, a_down, b_all, maps, a_all)


def class_head(label_ref, final_ref, map_ref, projection_ref, out_ref):
    width = final_ref.shape[1]
    classes = projection_ref.shape[0]
    label = label_ref[...]
    live = label >= 0
    pooled = jnp.tanh(dot(final_ref[...], map_ref[...]))
    logits = [
        jnp.sum(pooled * projection_ref[c : c + 1, :width], -1, keepdims=True)
        + projection_ref[c : c + 1, width : width + 1]
        for c in range(classes)
    ]
    top = functools.reduce(jnp.maximum, logits)
    exponents = [jnp.exp(x - top) for x in logits]
    total = functools.reduce(jnp.add, exponents)
    loss = top + jnp.log(total)
    pulled = 0.0
    out_ref[...] = jnp.zeros(out_ref.shape, F32)
    for c in range(classes):
        hit = (label == c).astype(F32)
        loss = loss - logits[c] * hit
        grad = jnp.where(live, exponents[c] / total - hit, 0.0)
        pulled = pulled + grad * projection_ref[c : c + 1, :width]
        out_ref[c : c + 1, :width] = jnp.sum(pooled * grad, 0, keepdims=True)
        out_ref[c : c + 1, width:] = jnp.broadcast_to(jnp.sum(grad, 0, keepdims=True), (1, 128))
    back = dot_nt((pulled * (1.0 - pooled * pooled)).astype(BF), map_ref[...])
    return back, jnp.sum(jnp.where(live, loss, 0.0), 0, keepdims=True)


BLOCK = 1024


def table_kernel(count, *refs):
    table_run(refs[:count], *refs[count:])


def table_run(
    part_refs, live_ref, table_hbm, near_out, far_out, place, z_ref, table, acc, score, prob, base, top, total, flag, sems
):
    rows, width = z_ref.shape
    half = rows // 2
    length = table.shape[0]
    blocks = length // BLOCK // 2 * 2
    tail = length - blocks * BLOCK
    sizes = [BLOCK] * blocks + [tail] * (tail > 0)
    for i, size in enumerate(sizes):
        at = pl.ds(i * BLOCK, size)
        pltpu.make_async_copy(table_hbm.at[at, :], table.at[at, :], sems.at[i]).start()

    def wait(i, size):
        at = pl.ds(0, size)
        pltpu.make_async_copy(table_hbm.at[at, :], table.at[at, :], sems.at[i]).wait()

    own = rows // len(part_refs)
    span = own // 2
    lane = lax.broadcasted_iota(jnp.int32, (1, rows), 1)
    number = jnp.full((1, rows), -1, jnp.int32)
    used = 0
    for i in range(2 * len(part_refs)):
        live = live_ref[i]
        slot = lane - i * span
        number = jnp.where((slot >= 0) & (slot < live), slot + used, number)
        used = used + live
    for first in range(0, rows, 64):
        at = lax.broadcasted_iota(jnp.int32, (64, rows), 0) + first
        place[first : first + 64, :] = (at == number).astype(BF)
    for i, part_ref in enumerate(part_refs):
        prob[0, i * own : (i + 1) * own, :width] = part_ref[...]
    z_ref[...] = dot(place[...], prob[0, :, :width]).astype(BF)

    def scores(rows, start, size, slot):
        score[slot, :rows, :size] = dot_nt(z_ref[:rows, :], table[pl.ds(start, size), :])

    def fold(rows, start, size, slot):
        for first in range(0, rows, CHUNK):
            r = slice(first, first + CHUNK)
            low = base[r, :1]
            best, added = top[r, :], total[r, :]
            for column in range(0, size, 128):
                cols = slice(column, min(column + 128, size))
                value = score[slot, r, cols]
                exponent = jnp.exp(value - low)
                prob[slot, r, cols] = exponent.astype(BF)
                if column + 128 <= size:
                    best = jnp.maximum(best, value)
                    added = added + exponent
                else:
                    best = jnp.maximum(best, jnp.max(value, -1, keepdims=True))
                    here = lax.broadcasted_iota(jnp.int32, added.shape, 1)
                    added = added + jnp.where(here == 0, jnp.sum(exponent, -1, keepdims=True), 0.0)
            top[r, :] = best
            total[r, :] = added
        acc[:rows, :] += dot(prob[slot, :rows, :size], table[pl.ds(start, size), :])

    def first_block(rows):
        scores(rows, 0, BLOCK, 0)
        for first in range(0, rows, CHUNK):
            r = slice(first, first + CHUNK)
            highest = jnp.max(score[0, r, :BLOCK], -1, keepdims=True)
            base[r, :] = jnp.broadcast_to(highest, (CHUNK, 128))

    def even(rows, start):
        scores(rows, start + BLOCK, BLOCK, 1)
        fold(rows, start, BLOCK, 0)

    def odd(rows, start):
        scores(rows, jnp.minimum(start + 2 * BLOCK, (blocks - 1) * BLOCK), BLOCK, 0)
        fold(rows, start + BLOCK, BLOCK, 1)

    def rest(rows):
        scores(rows, blocks * BLOCK, tail, 0)
        fold(rows, blocks * BLOCK, tail, 0)

    few = rows * 3 // 4

    def either(body, *at):
        @pl.when(used <= few)
        def _():
            body(few, *at)

        @pl.when(used > few)
        def _():
            body(rows, *at)

    def clear():
        top[...] = jnp.full(top.shape, NEG_FILL, F32)
        total[...] = jnp.zeros(total.shape, F32)
        acc[...] = jnp.zeros(acc.shape, F32)

    def two(i, carry):
        start = pl.multiple_of(i * 2 * BLOCK, BLOCK)
        wait(2 * i + 1, BLOCK)
        either(even, start)

        @pl.when(i + 1 < blocks // 2)
        def _():
            wait(2 * i + 2, BLOCK)

        either(odd, start)
        return carry

    clear()
    base[...] = jnp.zeros(base.shape, F32)
    wait(0, BLOCK)
    either(first_block)
    lax.fori_loop(0, blocks // 2, two, 0)
    if tail:
        wait(blocks, tail)
        either(rest)

    best = jnp.max(top[...], -1, keepdims=True)
    flag[0] = jnp.max(best - base[:, :1])

    @pl.when(flag[0] > 40.0)
    def _():
        base[...] = jnp.broadcast_to(best, base.shape)
        clear()
        scores(rows, 0, BLOCK, 0)

        def again(i, carry):
            start = pl.multiple_of(i * 2 * BLOCK, BLOCK)
            even(rows, start)
            odd(rows, start)
            return carry

        lax.fori_loop(0, blocks // 2, again, 0)
        if tail:
            rest(rows)

    acc[...] = acc[...] / jnp.maximum(jnp.sum(total[...], -1, keepdims=True), 1e-30)
    z_ref[...] = acc[...].astype(BF)
    logs = jnp.log(jnp.maximum(jnp.sum(total[...], -1, keepdims=True), 1e-30))
    extra = lanes_of(split_three(jnp.broadcast_to(base[:, :1] + logs, (rows, 128))))
    for out_ref, r in ((near_out, slice(0, half)), (far_out, slice(half, rows))):
        out_ref[:, :width] = dot_tn(place[:, r], z_ref[...]).astype(BF)
        out_ref[:, width:] = dot_tn(place[:, r], extra).astype(BF)


def table_pass(parts, live, table):
    own, width = parts[0].shape
    rows = own * len(parts)
    length = table.shape[0]
    widest = max(BLOCK, length - length // BLOCK // 2 * 2 * BLOCK)
    widest += -widest % 128
    return pl.pallas_call(
        functools.partial(table_kernel, len(parts)),
        out_shape=[jax.ShapeDtypeStruct((rows // 2, width + EXTRA), BF)] * 2,
        in_specs=[VMEM_SPEC] * len(parts) + [SMEM_SPEC, ANY_SPEC],
        out_specs=[VMEM_SPEC] * 2,
        scratch_shapes=[
            pltpu.VMEM((rows, rows), BF), pltpu.VMEM((rows, width), BF), pltpu.VMEM((length, width), BF),
            pltpu.VMEM((rows, width), F32),
            pltpu.VMEM((2, rows, widest), F32), pltpu.VMEM((2, rows, widest), BF),
            pltpu.VMEM((rows, 128), F32), pltpu.VMEM((rows, 128), F32), pltpu.VMEM((rows, 128), F32),
            pltpu.SMEM((1,), F32), pltpu.SemaphoreType.DMA((length // BLOCK + 1,)),
        ],
        compiler_params=PARAMS,
    )(*parts, live, table)


def mean_of(part_refs, r, width):
    logs = [
        jnp.sum(part_ref[r, width : width + HDIM].astype(F32), -1, keepdims=True) for part_ref in part_refs
    ]
    top = functools.reduce(jnp.maximum, logs)
    shares = [jnp.exp(log - top) for log in logs]
    total = functools.reduce(jnp.add, shares)
    mean = functools.reduce(
        jnp.add, [part_ref[r, :width].astype(F32) * share for part_ref, share in zip(part_refs, shares)]
    )
    return mean / total, top + jnp.log(total)


def merge_kernel(left_ref, right_ref, *out_refs):
    rows, columns = out_refs[0].shape
    width = columns - EXTRA
    for i, out_ref in enumerate(out_refs):
        for start in range(0, rows, CHUNK):
            r = slice(start, start + CHUNK)
            mean, log = mean_of((left_ref, right_ref), slice(i * rows + start, i * rows + start + CHUNK), width)
            out_ref[r, :width] = mean.astype(BF)
            out_ref[r, width:] = lanes_of(split_three(jnp.broadcast_to(log, (CHUNK, EXTRA))))


def merge(left, right, count):
    rows, columns = left.shape
    return pl.pallas_call(
        merge_kernel,
        out_shape=[jax.ShapeDtypeStruct((rows // count, columns), BF)] * count,
        in_specs=[VMEM_SPEC] * 2,
        out_specs=[VMEM_SPEC] * count,
        compiler_params=PARAMS,
    )(left, right)


def update_kernel(core_ref, keep_ref, got_ref, term_ref, w_ref, m_ref, s_ref, cw_ref, cm_ref, cs_ref,
                  sum_ref, norm_ref, wo_ref, mo_ref, so_ref, cwo_ref, cmo_ref, cso_ref, grads):
    total = w_ref.shape[2]
    classes, rows = cw_ref.shape
    count = term_ref[0:1, 1:2]
    first = core_ref[0] == 0
    step = rows - 1
    square = 0.0
    for start in range(0, total, step):
        cols = slice(start, start + step)
        keep, got = keep_ref[:, cols] / count, got_ref[:, cols] / count
        square = square + (keep * keep + got * got)
        grads[0, :, cols] = jnp.where(first, keep, got)
        grads[1, :, cols] = jnp.where(first, got, keep)
    head = jnp.where(first, keep_ref[:, total:], got_ref[:, total:]) / count
    inside = (lax.broadcasted_iota(jnp.int32, head.shape, 0) < classes) & (
        lax.broadcasted_iota(jnp.int32, head.shape, 1) < rows
    )
    head = jnp.where(inside, head, 0.0)
    norm = jnp.sqrt(
        jnp.sum(jnp.sum(square, 1, keepdims=True), 0, keepdims=True)
        + jnp.sum(jnp.sum(head * head, 1, keepdims=True), 0, keepdims=True)
    )
    multiplier = CLIP_AT / jnp.maximum(norm, CLIP_AT)
    sum_ref[0] = term_ref[0, 0]
    sum_ref[1] = term_ref[0, 1]
    norm_ref[0] = norm[0, 0]
    for layer in range(2):
        for start in range(0, total, step):
            at = (layer, slice(None), slice(start, start + step))
            wo_ref[at], mo_ref[at], so_ref[at] = moment_update(
                w_ref[at], grads[at] * multiplier, m_ref[at], s_ref[at]
            )
    turned = (head * multiplier)[:classes, :rows]
    cwo_ref[...], cmo_ref[...], cso_ref[...] = moment_update(cw_ref[...], turned, cm_ref[...], cs_ref[...])


def update(core, keep, got, terms, trained, classes):
    classes = [x.T for x in classes]
    v = VMEM_SPEC
    shape = jax.ShapeDtypeStruct(trained[0].shape, F32)
    class_shape = jax.ShapeDtypeStruct(classes[0].shape, F32)
    *out, first, second, third = pl.pallas_call(
        update_kernel,
        out_shape=[jax.ShapeDtypeStruct((2,), F32), jax.ShapeDtypeStruct((1,), F32)] + [shape] * 3 + [class_shape] * 3,
        in_specs=[SMEM_SPEC] + [v] * 9,
        out_specs=[SMEM_SPEC] * 2 + [v] * 6,
        scratch_shapes=[pltpu.VMEM(trained[0].shape, F32)],
        compiler_params=PARAMS,
    )(core, keep, got, terms, *trained, *classes)
    return tuple(out) + (first.T, second.T, third.T)


def reduce_all(layers, terms):
    width = layers[0].shape[1]
    core = lax.axis_index("vocab") % 2
    keep = jnp.where(core == 0, layers[0], layers[1])
    send = jnp.where(core == 0, layers[1], layers[0])
    got = swap(jnp.concatenate([send, terms], 1), "vocab", 1)
    keep, terms = keep + got[:, :width], terms + got[:, width:]
    axes = ("dp", "vocab")
    size = lax.axis_size("vocab") * lax.axis_size("dp")
    bit = 2
    while bit < size:
        masks = [bit] if 2 * bit >= size else [bit, 2 * bit, 3 * bit]
        high = lax.reduce_precision(terms, 8, 7)
        middle = lax.reduce_precision(terms - high, 8, 7)
        mine = jnp.concatenate([lax.reduce_precision(keep, 8, 7), high, middle, terms - high - middle], 1)
        sent = mine.astype(BF)
        other = [
            lax.ppermute(sent, axes, [(i, i ^ mask) for i in range(size)]).astype(F32) for mask in masks
        ]
        both = mine + other[0]
        if len(other) == 3:
            both = both + (other[1] + other[2])
        keep = both[:, :width]
        terms = both[:, width : width + 128] + (both[:, width + 128 : width + 256] + both[:, width + 256 :])
        bit *= 2 if len(masks) == 1 else 4
    return core, keep, swap(keep, "vocab", 1), terms


def body(
    input_token_ids,
    lengths,
    masked_positions,
    masked_token_targets,
    labels,
    token_embedding_table,
    position_table,
    norm_gain_table,
    query_key_value_weight,
    output_weight,
    up_weight,
    down_weight,
    adapter_inputs,
    adapter_down_input,
    head_dense_maps,
    adapter_outputs,
    class_projection,
    adapter_moment_first,
    adapter_moment_second,
    class_moment_first,
    class_moment_second,
):
    table_rows, width = token_embedding_table.shape
    seq_len = input_token_ids.shape[2]
    slots = masked_positions.shape[2]
    vocab_size = lax.axis_size("vocab")
    vocab_index = lax.axis_index("vocab")
    vocab_start = vocab_index * table_rows
    count = input_token_ids.shape[0] * input_token_ids.shape[1]
    picks = -(-(slots + 1) // 16) * 16
    rest = picks - slots

    own_lengths = lengths.reshape(count)
    own_labels = labels.reshape(count)
    own_positions = masked_positions.reshape(count, slots)
    packed = jnp.concatenate(
        [
            input_token_ids.reshape(count, seq_len),
            jnp.pad(masked_token_targets.reshape(count, slots), ((0, 0), (0, rest)), constant_values=-1),
            lengths.reshape(count, 1),
        ],
        1,
    )
    items = lax.all_gather(packed, "vocab", axis=0)
    order = list(range(0, vocab_size, 2)) + list(range(1, vocab_size, 2))
    items = lax.optimization_barrier(
        jnp.stack([lax.dynamic_index_in_dim(items, vocab_index ^ mask, 0, keepdims=False) for mask in order])
    )

    def own_rows(ids):
        local = ids - vocab_start
        inside = (local >= 0) & (local < table_rows)
        inside = inside[..., None]
        rows = token_embedding_table.at[jnp.clip(local, 0, table_rows - 1)].get(mode="promise_in_bounds")
        half = vocab_size // 2
        zero = jnp.zeros((), BF)
        return jnp.where(inside[:half], rows[:half], zero), jnp.where(inside[half:], rows[half:], zero)

    def core_sum(rows):
        sent = swap(rows[1], "vocab", 1)
        return [rows[0][mask] + sent[mask] for mask in range(vocab_size // 2)]

    def spread(own):
        return own[0], functools.reduce(
            jnp.add, [swap(own[mask], "vocab", 2 * mask) for mask in range(1, vocab_size // 2)]
        )

    a_all, a_down, b_all = adapter_tables(adapter_inputs, adapter_down_input, adapter_outputs)
    weights = (query_key_value_weight, output_weight, up_weight, down_weight, a_all, a_down, b_all)
    pick_index = jnp.concatenate(
        [own_positions, jnp.zeros((count, 1), jnp.int32), jnp.full((count, rest - 1), -1, jnp.int32)], 1
    ).reshape(-1, 1)
    own0 = core_sum(own_rows(items[:, 0, :seq_len]))
    second = jnp.concatenate([items[:, 1, :seq_len], items[:, 0, seq_len:-1], items[:, 1, seq_len:-1]], 1)

    def exchange(own, ids):
        return spread(own), own_rows(ids)

    (near0, far0), own1 = lax.cond(
        own_lengths[0] > 0,
        exchange,
        lambda own, ids: ((own[0], own[1]), (jnp.zeros((vocab_size // 2,) + ids.shape[1:] + (width,), BF),) * 2),
        own0,
        second,
    )
    near1, far1 = spread(core_sum(own1))
    picked0, saved_first = first_layer(
        own_lengths, pick_index, near0, far0, position_table, norm_gain_table, weights
    )
    saved_second, final, head, top = two_layers(
        own_lengths, pick_index, near1, far1, position_table, (picked0, saved_first[0]), norm_gain_table, weights,
        head_dense_maps,
    )

    z = head[0]
    near_z = [z] + [swap(z, "vocab", 2 * mask) for mask in range(1, vocab_size // 2)]
    far_z = [swap(x, "vocab", 1) for x in near_z]
    live_counts = jnp.minimum(items[:, :, -1] * 15 // 100, slots)
    near_sum, far_sum = table_pass(near_z + far_z, live_counts.reshape(-1), token_embedding_table)
    merged = merge(near_sum, swap(far_sum, "vocab", 1), vocab_size // 2)
    parts = [merged[0]] + [swap(merged[mask], "vocab", 2 * mask) for mask in range(1, vocab_size // 2)]
    label_rows = jnp.where(jnp.arange(picks)[None, :] == slots, own_labels[:, None], -1).reshape(-1, 1)
    live = jnp.arange(picks)[None, :] < own_lengths[:, None] * 15 // 100
    live = (live & (jnp.arange(picks)[None, :] < slots)).reshape(-1)

    layer0, layer1, terms = backward(
        parts, own_lengths, pick_index, near1, far1, live.astype(F32)[:, None], label_rows, class_projection.T, head,
        final, top, (saved_first, saved_second), norm_gain_table, weights, head_dense_maps,
    )
    core, keep, got, terms = reduce_all((layer0, layer1), terms)
    return tuple(
        update(
            core.reshape(1).astype(jnp.int32), keep, got, terms,
            (adapter_outputs, adapter_moment_first, adapter_moment_second),
            (class_projection, class_moment_first, class_moment_second),
        )
    )


def solution(mesh):
    split = P(None, ("dp", "vocab"), None)
    placed = (split, P(None, ("dp", "vocab")), split, split, P(None, ("dp", "vocab")), P("vocab", None)) + (P(),) * 15
    return jax.shard_map(body, mesh=mesh, in_specs=placed, out_specs=(P(),) * 8, check_vma=False)
```
